512 devices in a mesh: tile: 128 (over z, x, core), grp: 4 (over y).
Axes of the slice: x: 4, y: 4, z: 16, core: 2. Of those that a mesh axis runs over, the one named last changes fastest.
Arguments:
- features: bfloat16 [4, 512, 64, 512], P('grp', 'tile'), may hold values from -6 to 6
- brick_count: int32 [4, 128], P('grp', 'tile'), may hold values from 1 to 4, as said below
- send_list: int32 [4, 128, 4, 4], P('grp', 'tile'), may hold values from 0 to 24, as said below
- halo_src: int32 [4, 512, 26], P('grp', 'tile'), may hold values from 0 to 40, as said below
- kernel: bfloat16 [64, 1728], replicated, may hold values from -0.15625 to 0.15625
- down_kernel: bfloat16 [128, 512], replicated, may hold values from -0.25 to 0.25
- out_grad: bfloat16 [4, 512, 64, 128], P('grp', 'tile'), may hold values from -6 to 6
Outputs:
- coarse: bfloat16 [4, 512, 64, 128], P('grp', 'tile')
- grad_features: bfloat16 [4, 512, 64, 512], P('grp', 'tile')
- grad_kernel: float32 [64, 1728], replicated
- grad_down: float32 [128, 512], replicated
The draws below stay inside these ranges and needn't reach their ends.
Inputs may be any that keep to these rules, and one draw needn't show every extreme that they name: `brick_count`: some device of every region holds all 4 slots occupied. `send_list`: used places hold 6 s + f for an occupied slot s and face f and come first; 24 marks an unused place; places towards offsets that leave the tile axis are unused; some device of every region fills all 4 places towards every offset. `halo_src`: entries below 24 name local faces, 24 a zero block, larger ones used received places.
All inputs are finite; a program needn't handle non-finite values.
Results may differ from the reference program's by a relative error of at most 0.005.
Values may be sent and summed in bfloat16 or wider, within the bound.
No kernel may reach another device: no remote copies, remote signals or barrier semaphores. Data moves between devices by JAX's collectives and lax.ppermute only.
A program may use at most 64 MiB of HBM per device.

```python
import jax
import jax.numpy as jnp
from jax import lax

C = 64
C2 = 128
VOX = 512
SLOTS = 4
REACH = 2
NOFF = 4
CAP = 4
REGIONS = 4
BRICKS = 512
N_TILE = 128


def geometry(key):
    keys = jax.random.split(key, 11)
    tiles = jnp.arange(N_TILE)
    counts = jax.random.randint(keys[0], (REGIONS, N_TILE), max(1, SLOTS // 4), SLOTS + 1)
    fullest = jax.random.randint(keys[1], (REGIONS, 1), 0, N_TILE)
    counts = jnp.where(tiles[None, :] == fullest, SLOTS, counts)
    offsets = jnp.array([o for step in range(1, REACH + 1) for o in (step, -step)], jnp.int32)
    target = tiles[:, None] + offsets[None, :]
    in_range = (target >= 0) & (target < N_TILE)
    filled = jax.random.randint(keys[2], (REGIONS, N_TILE, NOFF), 1, CAP + 1)
    busiest = jax.random.randint(keys[3], (REGIONS, 1, 1), REACH, N_TILE - REACH)
    filled = jnp.where(tiles[None, :, None] == busiest, CAP, filled)
    filled = jnp.where(in_range[None], filled, 0)
    slot_pick = jax.random.randint(keys[4], (REGIONS, N_TILE, NOFF, CAP), 0, counts[:, :, None, None])
    face_pick = jax.random.randint(keys[5], (REGIONS, N_TILE, NOFF, CAP), 0, 6)
    places = jnp.arange(CAP)
    sends = jnp.where(places[None, None, None, :] < filled[..., None], slot_pick * 6 + face_pick, 6 * SLOTS)
    source_tile = tiles[:, None] - offsets[None, :]
    source_ok = (source_tile >= 0) & (source_tile < N_TILE)
    clipped = jnp.clip(source_tile, 0, N_TILE - 1)
    arrived = filled[:, clipped, jnp.arange(NOFF)[None, :]] * source_ok[None].astype(jnp.int32)
    shape = (REGIONS, N_TILE, SLOTS, 26)
    kinds = jax.random.randint(keys[6], shape, 0, 10)
    local_slot = jax.random.randint(keys[7], shape, 0, counts[:, :, None, None])
    local_face = jax.random.randint(keys[8], shape, 0, 6)
    remote_j = jax.random.randint(keys[9], shape, 0, NOFF)
    spread = jnp.broadcast_to(arrived[:, :, None, :], (REGIONS, N_TILE, SLOTS, NOFF))
    avail = jnp.take_along_axis(spread, remote_j, axis=3)
    remote_c = jax.random.randint(keys[10], shape, 0, jnp.maximum(avail, 1))
    remote = 6 * SLOTS + 1 + remote_j * CAP + remote_c
    local = local_slot * 6 + local_face
    sources = jnp.where(kinds < 3, 6 * SLOTS, jnp.where(kinds < 7, local, jnp.where(avail > 0, remote, 6 * SLOTS)))
    return (counts.astype(jnp.int32), sends.astype(jnp.int32), sources.reshape(REGIONS, N_TILE * SLOTS, 26).astype(jnp.int32))


def draw_brick_count(key, part):
    return geometry(key)[0]


def draw_send_list(key, part):
    return geometry(key)[1]


def draw_halo_src(key, part):
    return geometry(key)[2]


def block_levels(own_key, shape, cuts, smallest, top_value):
    gain = 1.0
    for dim, shards_of in cuts:
        draws = jax.random.uniform(jax.random.fold_in(jax.random.fold_in(own_key, 6), dim), (shards_of,), jnp.float32, smallest / len(cuts), top_value / len(cuts))
        gain = gain * jnp.repeat(jnp.exp(draws), shape[dim] // shards_of).reshape((-1,) + (1,) * (len(shape) - 1 - dim))
    return gain


def bell_draw(key, extent, deviation, limit, cuts=(), kind=jnp.bfloat16):
    values = jax.random.normal(key, extent, jnp.float32) * deviation
    if len(cuts) > 0:
        values = block_levels(key, extent, cuts, -0.22, 0.18) * values
    return jnp.clip(values, min=-limit, max=limit).astype(kind)


def setup_inputs(seed: int = 0) -> dict:
    key_list = jax.random.split(jax.random.key(seed), 8)
    features = bell_draw(key_list[0], (REGIONS, BRICKS, C, VOX), 1.0, 6.0, ((0, 4), (1, 128)))
    brick_count = draw_brick_count(jax.random.fold_in(key_list[7], 71), 0)
    send_list = draw_send_list(jax.random.fold_in(key_list[7], 71), 0)
    halo_src = draw_halo_src(jax.random.fold_in(key_list[7], 71), 0)
    kernel = bell_draw(key_list[4], (C, 27 * C), (27 * C) ** -0.5, 0.15625)
    down_kernel = bell_draw(key_list[5], (C2, 8 * C), (8 * C) ** -0.5, 0.25)
    out_grad = bell_draw(key_list[6], (REGIONS, BRICKS, 64, C2), 1.0, 6.0, ((0, 4), (1, 128)))
    return {"features": features, "brick_count": brick_count, "send_list": send_list, "halo_src": halo_src, "kernel": kernel, "down_kernel": down_kernel, "out_grad": out_grad}


DIRECTIONS = [(a, b, c) for a in (-1, 0, 1) for b in (-1, 0, 1) for c in (-1, 0, 1) if (a, b, c) != (0, 0, 0)]
STENCIL = [(a, b, c) for a in (-1, 0, 1) for b in (-1, 0, 1) for c in (-1, 0, 1)]

def target_slices(direction):
    return tuple((slice(0, 1) if s == -1 else slice(9, 10) if s == 1 else slice(1, 9) for s in direction))

def face_select(direction):
    leading = [i for i in range(3) if direction[i] != 0][0]
    others = [i for i in range(3) if i != leading]
    chosen = tuple((slice(0, 1) if direction[i] == 1 else slice(7, 8) if direction[i] == -1 else slice(0, 8) for i in others))
    return (leading, chosen)

def pad_brick(brick_cube, entries):
    channels = brick_cube.shape[0]
    padded = jnp.pad(brick_cube.reshape(channels, 8, 8, 8), ((0, 0), (1, 1), (1, 1), (1, 1)))
    for position, direction in enumerate(DIRECTIONS):
        leading, chosen = face_select(direction)
        face_piece = entries[position].reshape(channels, 8, 8)[(slice(None),) + chosen]
        face_piece = jnp.expand_dims(face_piece, 1 + leading)
        padded = padded.at[(slice(None),) + target_slices(direction)].set(face_piece)
    return padded

def unfold_brick(padded):
    channels = padded.shape[0]
    return jnp.concatenate([padded[:, 1 + a:9 + a, 1 + b:9 + b, 1 + c:9 + c].reshape(channels, 512) for a, b, c in STENCIL], axis=0)

def fold_columns(columns, channels):
    result = jnp.zeros((channels, 10, 10, 10), jnp.float32)
    for position, (a, b, c) in enumerate(STENCIL):
        part_cols = columns[position * channels:(position + 1) * channels].reshape(channels, 8, 8, 8)
        result = result.at[:, 1 + a:9 + a, 1 + b:9 + b, 1 + c:9 + c].add(part_cols)
    return result

def rim_grad(grad_pad, direction):
    channels = grad_pad.shape[0]
    leading, chosen = face_select(direction)
    region = jnp.squeeze(grad_pad[(slice(None),) + target_slices(direction)], axis=1 + leading)
    grad_block = jnp.zeros((channels, 8, 8), jnp.float32).at[(slice(None),) + chosen].set(region)
    return grad_block.reshape(channels, 64)

def down_columns(active):
    channels = active.shape[0]
    return active.reshape(channels, 4, 2, 4, 2, 4, 2).transpose(2, 4, 6, 0, 1, 3, 5).reshape(8 * channels, 64)

def up_columns(columns, channels):
    return columns.reshape(2, 2, 2, channels, 4, 4, 4).transpose(3, 4, 0, 5, 1, 6, 2).reshape(channels, 512)

def face_table(brick_cubes):
    brick_total, channels = (brick_cubes.shape[0], brick_cubes.shape[1])
    shaped = brick_cubes.reshape(brick_total, channels, 8, 8, 8)
    layers = [jnp.take(shaped, 7 * e, axis=2 + a) for a in range(3) for e in range(2)]
    stacked = jnp.stack(layers, axis=1).reshape(brick_total * 6, channels, 64)
    return jnp.concatenate([stacked, jnp.zeros((1, channels, 64), brick_cubes.dtype)], axis=0)

def add_faces(interior, grad_faces):
    brick_total, channels = (interior.shape[0], interior.shape[1])
    shaped = interior.reshape(brick_total, channels, 8, 8, 8)
    layered = grad_faces.reshape(brick_total, 6, channels, 8, 8)
    for a in range(3):
        for e in range(2):
            spot = [slice(None)] * 5
            spot[2 + a] = 7 * e
            shaped = shaped.at[tuple(spot)].add(layered[:, 2 * a + e])
    return shaped.reshape(brick_total, channels, 512)

def device_step(brick_cubes, halo_table, sources, occupied, kernel, down_kernel, out_grad):
    channels = brick_cubes.shape[1]
    dims_first = (((0,), (1,)), ((), ()))

    def per_brick(totals, brick_items):
        brick_cube, source_row, filled, grad_out = brick_items
        padded = pad_brick(brick_cube, halo_table[source_row])
        columns = unfold_brick(padded)
        preact = jnp.dot(kernel, columns, preferred_element_type=jnp.float32)
        sigmoid_part = jax.nn.sigmoid(preact)
        active = (preact * sigmoid_part * filled).astype(jnp.bfloat16)
        lowered = down_columns(active)
        coarse = lax.dot_general(lowered, down_kernel, dims_first, preferred_element_type=jnp.float32).astype(jnp.bfloat16)
        grad_down = lax.dot_general(grad_out, lowered, (((0,), (1,)), ((), ())), preferred_element_type=jnp.float32)
        grad_low = lax.dot_general(down_kernel, grad_out, (((0,), (1,)), ((), ())), preferred_element_type=jnp.float32)
        grad_active = up_columns(grad_low, channels)
        grad_preact = (grad_active * sigmoid_part * (1.0 + preact * (1.0 - sigmoid_part)) * filled).astype(jnp.bfloat16)
        grad_kernel = lax.dot_general(grad_preact, columns, (((1,), (1,)), ((), ())), preferred_element_type=jnp.float32)
        grad_cols = lax.dot_general(kernel, grad_preact, (((0,), (0,)), ((), ())), preferred_element_type=jnp.float32)
        grad_pad = fold_columns(grad_cols, channels)
        interior = grad_pad[:, 1:9, 1:9, 1:9].reshape(channels, 512)
        rims = jnp.stack([rim_grad(grad_pad, direction) for direction in DIRECTIONS])
        return ((totals[0] + grad_kernel, totals[1] + grad_down), (coarse, interior, rims))
    start = (jnp.zeros(kernel.shape, jnp.float32), jnp.zeros(down_kernel.shape, jnp.float32))
    (grad_kernel, grad_down), (coarse, interior, rims) = lax.scan(per_brick, start, (brick_cubes, sources, occupied, out_grad))
    grad_table = jax.ops.segment_sum(rims.reshape(-1, channels, 64), sources.reshape(-1), num_segments=halo_table.shape[0])
    return (coarse, grad_kernel, grad_down, grad_table, interior)

def reference(features, brick_count, send_list, halo_src, kernel, down_kernel, out_grad):
    offsets = [o for step in range(1, REACH + 1) for o in (step, -step)]
    tiles = jnp.arange(N_TILE).astype(jnp.int32)
    region_ids = jnp.arange(REGIONS).astype(jnp.int32)[:, None, None]
    brick_cubes = features.reshape(REGIONS, N_TILE, SLOTS, C, 512)
    occupied = (jnp.arange(SLOTS)[None, None, :] < brick_count[:, :, None]).astype(jnp.float32)
    masked = brick_cubes * occupied[..., None, None].astype(features.dtype)
    faces = jax.vmap(jax.vmap(face_table))(masked)
    received = []
    for j, offset in enumerate(offsets):
        sender = tiles - offset
        in_range = (sender >= 0) & (sender < N_TILE)
        clipped = jnp.clip(sender, 0, N_TILE - 1).astype(jnp.int32)
        entries = send_list[:, clipped, j, :]
        arrived = faces[region_ids, clipped[None, :, None], entries]
        received.append(arrived * in_range[None, :, None, None, None].astype(arrived.dtype))
    halo_table = jnp.concatenate([faces] + received, axis=2)
    sources = halo_src.reshape(REGIONS * N_TILE, SLOTS, 26)
    grads = out_grad.reshape(REGIONS * N_TILE, SLOTS, 64, C2)
    table_rows = halo_table.shape[2]

    def run_device(device_items):
        return device_step(device_items[0], device_items[1], device_items[2], device_items[3], kernel, down_kernel, device_items[4])
    coarse, grad_kernel, grad_down, grad_table, interior = lax.map(run_device, (masked.reshape(REGIONS * N_TILE, SLOTS, C, 512), halo_table.reshape(REGIONS * N_TILE, table_rows, C, 64), sources, occupied.reshape(REGIONS * N_TILE, SLOTS), grads))
    grad_table = grad_table.reshape(REGIONS, N_TILE, table_rows, C, 64)
    remote_start = 6 * SLOTS + 1
    grad_faces = grad_table[:, :, :remote_start]
    for j, offset in enumerate(offsets):
        target = tiles + offset
        in_range = (target >= 0) & (target < N_TILE)
        clipped = jnp.clip(target, 0, N_TILE - 1).astype(jnp.int32)
        returned = grad_table[:, clipped, remote_start + j * CAP:remote_start + (j + 1) * CAP]
        returned = returned * in_range[None, :, None, None, None].astype(returned.dtype)
        grad_faces = grad_faces.at[region_ids, tiles[None, :, None], send_list[:, :, j, :]].add(returned)
    grad_faces = grad_faces.reshape(REGIONS * N_TILE, remote_start, C, 64)[:, :6 * SLOTS]
    grad_cubes = jax.vmap(add_faces)(interior, grad_faces)
    grad_cubes = grad_cubes * occupied.reshape(REGIONS * N_TILE, SLOTS)[:, :, None, None]
    grad_features = grad_cubes.astype(jnp.bfloat16).reshape(REGIONS, BRICKS, C, 512)
    return (coarse.reshape(REGIONS, BRICKS, 64, C2), grad_features, lax.optimization_barrier(jnp.sum(grad_kernel, axis=0)), lax.optimization_barrier(jnp.sum(grad_down, axis=0)))
```

```python
import jax
import jax.numpy as jnp
import ml_dtypes
import numpy as np
from jax import lax
from jax.experimental import pallas as pl
from jax.experimental.pallas import tpu as pltpu
from jax.sharding import Mesh
from jax.sharding import PartitionSpec as P

BF = jnp.bfloat16
F32 = jnp.float32
DIRECTIONS = [
    (a, b, c) for a in (-1, 0, 1) for b in (-1, 0, 1) for c in (-1, 0, 1) if (a, b, c) != (0, 0, 0)
]
SHIFTS = [10 * b + c for b in (-1, 0, 1) for c in (-1, 0, 1)]
SLOTS, C, C2, NOFF, CAP = 4, 64, 128, 4, 4
LOCAL = 6 * SLOTS + 1
TABLE = LOCAL + NOFF * CAP
OFFSETS = (1, -1, 2, -2)
VMEM_LIMIT = 56 * 2**20


def rim_cells(d, full):
    if d == -1:
        return [(7, 0)]
    if d == 1:
        return [(0, 9)]
    return [(i, i + 1) for i in range(full)]


def one_hot_tables():
    faces = np.zeros((512, 6, 128), np.float32)
    for x in range(8):
        for y in range(8):
            for z in range(8):
                v = (x, y, z)
                for a in range(3):
                    p, q = [v[i] for i in range(3) if i != a]
                    for e in range(2):
                        if v[a] == 7 * e:
                            faces[x * 64 + y * 8 + z, 2 * a + e, p * 8 + q] = 1
    inner = np.zeros((2, 64, 2, 128), np.float32)
    for s in range(2):
        for y in range(8):
            for z in range(8):
                inner[s, y * 8 + z, s, (y + 1) * 10 + z + 1] = 1
    cap = np.zeros((9, 128, 128), np.float32)
    side = np.zeros((8, 128, 8, 128), np.float32)
    for m, d in enumerate([d for d in DIRECTIONS if d[0] == 0]):
        if d[1] != 0:
            yy = 0 if d[1] == -1 else 9
            for x in range(8):
                for i, zz in rim_cells(d[2], 8):
                    side[m, x * 8 + i, x, yy * 10 + zz] = 1
        else:
            zz = 0 if d[2] == -1 else 9
            for x in range(8):
                for y in range(8):
                    side[m, x * 8 + y, x, (y + 1) * 10 + zz] = 1
    for m, (dy, dz) in enumerate([(b, c) for b in (-1, 0, 1) for c in (-1, 0, 1)]):
        for i, yy in rim_cells(dy, 8):
            for k, zz in rim_cells(dz, 8):
                cap[m, i * 8 + k, yy * 10 + zz] = 1
    down = np.zeros((2, 2, 4, 4, 4, 4, 128), np.float32)
    for ty in range(2):
        for tz in range(2):
            for X in range(4):
                for Y in range(4):
                    for Z in range(4):
                        lane = (2 * Y + ty + 1) * 10 + 2 * Z + tz + 1
                        down[ty, tz, X, Y, Z, X, lane] = 1
    b = ml_dtypes.bfloat16
    return (
        faces.reshape(512, 768).astype(b),
        inner.reshape(128, 256).astype(b),
        cap.reshape(1152, 128).astype(b),
        side.reshape(1024, 1024).astype(b),
        down.reshape(256, 512).astype(b),
    )


def nn(a, b):
    return jnp.dot(a, b, preferred_element_type=F32)


def nt(a, b):
    return lax.dot_general(a, b, (((1,), (1,)), ((), ())), preferred_element_type=F32)


def masked_rows(features, count):
    return jnp.concatenate(
        [features[0, s] * jnp.where(s < count, 1.0, 0.0).astype(BF) for s in range(SLOTS)], axis=0
    )


def faces_kernel(count, sends, features, face_hot, table, outgoing):
    masked = masked_rows(features, count[0, 0])
    for f in range(6):
        layer = nn(masked, face_hot[:, f * 128 : (f + 1) * 128]).astype(BF)
        for s in range(SLOTS):
            table[6 * s + f] = layer[s * C : (s + 1) * C]
    table[6 * SLOTS] = jnp.zeros((C, 128), BF)
    for j in range(NOFF):
        for c in range(CAP):
            outgoing[j, c] = table[sends[0, 0, j, c]]


def upper_kernel(out_grad, down_hot, down_rows, grad_active):
    for s in range(SLOTS):
        turned = jnp.transpose(out_grad[0, s].astype(F32)).astype(BF)
        spread = jnp.concatenate(
            [nn(turned, down_hot[t * 64 : (t + 1) * 64]).astype(BF) for t in range(4)], axis=0
        )
        grad_active[s] = nn(down_rows[...], spread)


def main_kernel(
    count,
    sources,
    features,
    table,
    received,
    conv,
    down_cols,
    out_grad,
    grad_active,
    inner_hot,
    cap_hot,
    side_hot,
    down_hot,
    coarse,
    grad_preact,
    sums,
    halo,
    entries,
    padded,
    stack,
    shifted,
    lowered,
    total,
):
    halo[0:LOCAL] = table[...]
    for j in range(NOFF):
        halo[LOCAL + j * CAP : LOCAL + (j + 1) * CAP] = received[j]
    for s in range(SLOTS):
        for k in range(26):
            entries[s * C : (s + 1) * C, k * 128 : (k + 1) * 128] = halo[sources[0, s, k]]
    masked = masked_rows(features, count[0, 0])
    padded[:, 0:128] = nn(entries[:, 0:1152], cap_hot[...]).astype(BF)
    padded[:, 1152:1280] = nn(entries[:, 2176:3328], cap_hot[...]).astype(BF)
    for i in range(4):
        block = nn(entries[:, 1152:2176], side_hot[:, i * 256 : (i + 1) * 256])
        block = block + nn(masked[:, i * 128 : (i + 1) * 128], inner_hot[...])
        padded[:, 128 + i * 256 : 384 + i * 256] = block.astype(BF)

    lane = lax.broadcasted_iota(jnp.int32, (C, 1024), 1) & 127
    row, column = lane // 10, lane % 10
    valid = (row >= 1) & (row <= 8) & (column >= 1) & (column <= 8)
    shifted[...] = jnp.zeros_like(shifted)
    total[...] = jnp.zeros_like(total)

    def brick(s, carry):
        filled = jnp.where(s < count[0, 0], 1.0, 0.0).astype(F32)
        here = pl.ds(pl.multiple_of(s * C, C), C)
        for x in range(10):
            plane = padded[here, x * 128 : (x + 1) * 128]
            for k, shift in enumerate(SHIFTS):
                moved = plane if shift == 0 else pltpu.roll(plane, (-shift) % 128, 1)
                stack[k * C : (k + 1) * C, x * 128 : (x + 1) * 128] = moved
        triple = nn(conv[...], stack[...])
        preact = triple[0:C, 0:1024] + triple[C : 2 * C, 128:1152] + triple[2 * C :, 256:1280]
        sigmoid = jax.nn.sigmoid(preact)
        active = jnp.where(valid, preact * sigmoid * filled, 0.0).astype(BF)
        halves = jnp.concatenate(
            [
                jnp.concatenate(
                    [active[:, (2 * X + tx) * 128 : (2 * X + tx + 1) * 128] for X in range(4)],
                    axis=1,
                )
                for tx in range(2)
            ],
            axis=0,
        )
        picked = nt(down_hot[...], halves).astype(BF)
        for t in range(4):
            lowered[here, t * 128 : (t + 1) * 128] = picked[t * 64 : (t + 1) * 64]
        upper = jnp.concatenate(
            [
                grad_active[s, (x % 2) * C : (x % 2 + 1) * C, (x // 2) * 128 : (x // 2 + 1) * 128]
                for x in range(8)
            ],
            axis=1,
        )
        grads = upper * sigmoid * (1.0 + preact * (1.0 - sigmoid)) * filled
        grads = jnp.where(valid, grads, 0.0).astype(BF)
        grad_preact[s] = grads
        for o in range(3):
            shifted[o * C : (o + 1) * C, o * 128 : o * 128 + 1024] = grads
        total[...] += nt(shifted[...], stack[...])
        return carry

    lax.fori_loop(0, SLOTS, brick, 0)
    rows = lowered[...]
    coarse[...] = nt(rows, down_cols[...]).astype(BF).reshape(coarse.shape)
    turned = jnp.transpose(out_grad[...].reshape(SLOTS * 64, C2).astype(F32)).astype(BF)
    grad_down = nn(turned, rows)
    for j in range(5):
        width = min(128, 576 - j * 128)
        sums[j * 192 : (j + 1) * 192, 0:width] = total[:, j * 128 : j * 128 + width].astype(BF)
    sums[4 * 192 : 5 * 192, 64:128] = jnp.zeros((192, 64), BF)
    for j in range(4):
        sums[960 + j * C2 : 960 + (j + 1) * C2] = grad_down[:, j * 128 : (j + 1) * 128].astype(BF)
    sums[1472:1536] = jnp.zeros((64, 128), BF)


def fold_kernel(
    sources,
    grad_preact,
    conv_back,
    inner_hot,
    cap_hot,
    side_hot,
    interior,
    grad_local,
    grad_remote,
    stack,
    high,
    low,
    rims,
    grad_table,
):
    high[...] = jnp.zeros_like(high)

    def brick(s, carry):
        here = pl.ds(pl.multiple_of(s * C, C), C)
        for x in range(8):
            plane = grad_preact[s, :, x * 128 : (x + 1) * 128]
            for k, shift in enumerate(SHIFTS):
                moved = plane if shift == 0 else pltpu.roll(plane, shift % 128, 1)
                stack[k * C : (k + 1) * C, x * 128 : (x + 1) * 128] = moved
        triple = nn(conv_back[...], stack[...])
        for x in range(10):
            value = None
            for o in range(3):
                if 0 <= x - o < 8:
                    part = triple[o * C : (o + 1) * C, (x - o) * 128 : (x - o + 1) * 128]
                    value = part if value is None else value + part
            top = value.astype(BF)
            high[here, x * 128 : (x + 1) * 128] = top
            low[here, x * 128 : (x + 1) * 128] = (value - top.astype(F32)).astype(BF)
        return carry

    lax.fori_loop(0, SLOTS, brick, 0)
    rims[:, 0:1152] = nt(high[:, 0:128], cap_hot[...])
    rims[:, 1152:2176] = nt(high[:, 128:1152], side_hot[...])
    rims[:, 2176:3328] = nt(high[:, 1152:1280], cap_hot[...])
    grad_table[...] = jnp.zeros_like(grad_table)
    for s in range(SLOTS):
        for k in range(26):
            place = sources[0, s, k]
            grad_table[place] += rims[s * C : (s + 1) * C, k * 128 : (k + 1) * 128]
    for i in range(4):
        lanes = slice(128 + i * 256, 384 + i * 256)
        interior[:, i * 128 : (i + 1) * 128] = nt(high[:, lanes], inner_hot[...]) + nt(
            low[:, lanes], inner_hot[...]
        )
    grad_local[...] = grad_table[0:LOCAL]
    for j in range(NOFF):
        grad_remote[j] = grad_table[LOCAL + j * CAP : LOCAL + (j + 1) * CAP].astype(BF)


def finish_kernel(
    count, sends, interior, grad_local, returned, face_hot, grad_features, table, layers
):
    table[...] = grad_local[...]
    for j in range(NOFF):
        for c in range(CAP):
            table[sends[0, 0, j, c]] += returned[j, c].astype(F32)
    for s in range(SLOTS):
        for f in range(6):
            layers[s * C : (s + 1) * C, f * 128 : (f + 1) * 128] = table[6 * s + f].astype(BF)
    whole = interior[...] + nt(layers[...], face_hot[...])
    for s in range(SLOTS):
        filled = jnp.where(s < count[0, 0], 1.0, 0.0).astype(F32)
        grad_features[0, s] = (whole[s * C : (s + 1) * C] * filled).astype(BF)


def call(kernel, memories, outs, scratch, flops, *args):
    where = {"s": pltpu.SMEM, "v": pltpu.VMEM}
    return pl.pallas_call(
        kernel,
        in_specs=[pl.BlockSpec(memory_space=where[m]) for m in memories],
        out_specs=[pl.BlockSpec(memory_space=pltpu.VMEM) for _ in outs],
        out_shape=[jax.ShapeDtypeStruct(s, d) for s, d in outs],
        scratch_shapes=[pltpu.VMEM(s, d) for s, d in scratch],
        compiler_params=pltpu.CompilerParams(vmem_limit_bytes=VMEM_LIMIT),
        cost_estimate=pl.CostEstimate(flops=flops, bytes_accessed=2**20, transcendentals=0),
        name=kernel.__name__,
    )(*args)


def gather_sum(block, axes, parts):
    copies = jnp.broadcast_to(block[None], (parts,) + block.shape)
    got = lax.all_to_all(copies, axes, 0, 0)
    return got.astype(F32).sum(0)


def sum_over_all(block, sizes):
    near = ("x", "c", "grp")
    parts = sizes["x"] * sizes["c"] * sizes["grp"]
    rows = block.shape[0] // parts
    got = lax.all_to_all(block.reshape(parts, rows, 128), near, 0, 0)
    part = got.astype(F32).sum(0)
    for axis in ("zl", "zh"):
        if sizes[axis] > 1:
            part = gather_sum(part.astype(BF), (axis,), sizes[axis])
    copies = jnp.broadcast_to(part.astype(BF)[None], (parts, rows, 128))
    return lax.all_to_all(copies, near, 0, 0).reshape(block.shape)


def from_behind(block, axes, devices, distance):
    route = [(i - distance, i) for i in range(devices) if 0 <= i - distance < devices]
    return lax.ppermute(block, axes, route)


def on_device(sizes, features, brick_count, send_list, halo_src, kernel, down_kernel, out_grad):
    face_hot, inner_hot, cap_hot, side_hot, down_hot = one_hot_tables()
    tile = ("zh", "zl", "x", "c")
    devices = sizes["zh"] * sizes["zl"] * sizes["x"] * sizes["c"]
    conv5 = kernel.reshape(C, 3, 9, C)
    conv = conv5.transpose(1, 0, 2, 3).reshape(192, 576)
    conv_back = conv5.transpose(1, 3, 2, 0).reshape(192, 576)
    down5 = down_kernel.reshape(C2, 2, 4, C)
    down_cols = down5.transpose(0, 2, 1, 3).reshape(C2, 512)
    down_rows = down5.transpose(1, 3, 2, 0).reshape(2 * C, 4 * C2)

    table, outgoing = call(
        faces_kernel,
        "ssvv",
        [((LOCAL, C, 128), BF), ((NOFF, CAP, C, 128), BF)],
        [],
        2 * 256 * 512 * 768,
        brick_count,
        send_list,
        features,
        face_hot,
    )
    received = jnp.stack(
        [from_behind(outgoing[j], tile, devices, o) for j, o in enumerate(OFFSETS)]
    )
    (grad_active,) = call(
        upper_kernel,
        "vvv",
        [((SLOTS, 2 * C, 512), F32)],
        [],
        10**9,
        out_grad,
        down_hot,
        down_rows,
    )
    coarse, grad_preact, sums = call(
        main_kernel,
        "ssvvvvvvvvvvv",
        [((1, SLOTS, 64, C2), BF), ((SLOTS, C, 1024), BF), ((1536, 128), BF)],
        [
            ((TABLE, C, 128), BF),
            ((256, 26 * 128), BF),
            ((256, 1280), BF),
            ((576, 1280), BF),
            ((192, 1280), BF),
            ((256, 512), BF),
            ((192, 576), F32),
        ],
        5 * 10**9,
        brick_count,
        halo_src,
        features,
        table,
        received,
        conv,
        down_cols,
        out_grad,
        grad_active,
        inner_hot,
        cap_hot,
        side_hot,
        down_hot,
    )
    sums = sum_over_all(sums, sizes)
    grad_kernel = sums[:960].reshape(5, 3, C, 128).transpose(2, 1, 0, 3).reshape(C, 3, 640)
    grad_kernel = grad_kernel[:, :, :576].reshape(C, 1728).astype(F32)
    grad_down = sums[960:1472].reshape(4, C2, 2, C).transpose(1, 2, 0, 3)
    grad_down = grad_down.reshape(C2, 512).astype(F32)

    interior, grad_local, grad_remote = call(
        fold_kernel,
        "svvvvv",
        [((256, 512), F32), ((LOCAL, C, 128), F32), ((NOFF, CAP, C, 128), BF)],
        [
            ((576, 1024), BF),
            ((256, 1280), BF),
            ((256, 1280), BF),
            ((256, 26 * 128), F32),
            ((TABLE, C, 128), F32),
        ],
        3 * 10**9,
        halo_src,
        grad_preact,
        conv_back,
        inner_hot,
        cap_hot,
        side_hot,
    )
    returned = jnp.stack(
        [from_behind(grad_remote[j], tile, devices, -o) for j, o in enumerate(OFFSETS)]
    )
    (grad_features,) = call(
        finish_kernel,
        "ssvvvv",
        [((1, SLOTS, C, 512), BF)],
        [((LOCAL, C, 128), F32), ((256, 768), BF)],
        2 * 256 * 512 * 768,
        brick_count,
        send_list,
        interior,
        grad_local,
        returned,
        face_hot,
    )
    return coarse, grad_features, grad_kernel, grad_down


def solution(mesh):
    tile, grp = mesh.shape["tile"], mesh.shape["grp"]
    near = tile // 8
    low = 4 if near % 4 == 0 else near
    sizes = {"zh": near // low, "zl": low, "x": 4, "c": 2, "grp": grp}
    fine = Mesh(mesh.devices.reshape(tuple(sizes.values())), tuple(sizes))
    line = ("zh", "zl", "x", "c")
    in_specs = (
        P("grp", line, None, None),
        P("grp", line),
        P("grp", line, None, None),
        P("grp", line, None),
        P(),
        P(),
        P("grp", line, None, None),
    )
    out_specs = (P("grp", line, None, None), P("grp", line, None, None), P(), P())

    def step(*args):
        return on_device(sizes, *args)

    return jax.shard_map(step, mesh=fine, in_specs=in_specs, out_specs=out_specs, check_vma=False)
```

```python
import jax
import jax.numpy as jnp
import ml_dtypes
import numpy as np
from jax import lax
from jax.experimental import pallas as pl
from jax.experimental.pallas import tpu as pltpu
from jax.sharding import Mesh
from jax.sharding import PartitionSpec as P

BF = jnp.bfloat16
F32 = jnp.float32
DIRECTIONS = [
    (a, b, c) for a in (-1, 0, 1) for b in (-1, 0, 1) for c in (-1, 0, 1) if (a, b, c) != (0, 0, 0)
]
SHIFTS = [10 * b + c for b in (-1, 0, 1) for c in (-1, 0, 1)]
SLOTS, C, C2, NOFF, CAP = 4, 64, 128, 4, 4
LOCAL = 6 * SLOTS + 1
TABLE = LOCAL + NOFF * CAP
OFFSETS = (1, -1, 2, -2)
NEAR = ("x", "c", "grp")


def rim_cells(d, full):
    if d == -1:
        return [(7, 0)]
    if d == 1:
        return [(0, 9)]
    return [(i, i + 1) for i in range(full)]


def one_hot_tables():
    faces = np.zeros((512, 6, 128), np.float32)
    for x in range(8):
        for y in range(8):
            for z in range(8):
                v = (x, y, z)
                for a in range(3):
                    p, q = [v[i] for i in range(3) if i != a]
                    for e in range(2):
                        if v[a] == 7 * e:
                            faces[x * 64 + y * 8 + z, 2 * a + e, p * 8 + q] = 1
    inner = np.zeros((2, 64, 2, 128), np.float32)
    for s in range(2):
        for y in range(8):
            for z in range(8):
                inner[s, y * 8 + z, s, (y + 1) * 10 + z + 1] = 1
    cap = np.zeros((9, 128, 128), np.float32)
    side = np.zeros((8, 128, 8, 128), np.float32)
    for m, d in enumerate([d for d in DIRECTIONS if d[0] == 0]):
        if d[1] != 0:
            yy = 0 if d[1] == -1 else 9
            for x in range(8):
                for i, zz in rim_cells(d[2], 8):
                    side[m, x * 8 + i, x, yy * 10 + zz] = 1
        else:
            zz = 0 if d[2] == -1 else 9
            for x in range(8):
                for y in range(8):
                    side[m, x * 8 + y, x, (y + 1) * 10 + zz] = 1
    for m, (dy, dz) in enumerate([(b, c) for b in (-1, 0, 1) for c in (-1, 0, 1)]):
        for i, yy in rim_cells(dy, 8):
            for k, zz in rim_cells(dz, 8):
                cap[m, i * 8 + k, yy * 10 + zz] = 1
    down = np.zeros((2, 2, 4, 4, 4, 4, 128), np.float32)
    for ty in range(2):
        for tz in range(2):
            for X in range(4):
                for Y in range(4):
                    for Z in range(4):
                        lane = (2 * Y + ty + 1) * 10 + 2 * Z + tz + 1
                        down[ty, tz, X, Y, Z, X, lane] = 1
    b = ml_dtypes.bfloat16
    return (
        faces.reshape(512, 768).astype(b),
        inner.reshape(128, 256).astype(b),
        cap.reshape(1152, 128).astype(b),
        side.reshape(1024, 1024).astype(b),
        down.reshape(256, 512).astype(b),
    )


def nn(a, b):
    return jnp.dot(a, b, preferred_element_type=F32)


def nt(a, b):
    return lax.dot_general(a, b, (((1,), (1,)), ((), ())), preferred_element_type=F32)


def masked_rows(features, count):
    return jnp.concatenate(
        [features[0, s] * jnp.where(s < count, 1.0, 0.0).astype(BF) for s in range(SLOTS)], axis=0
    )


def faces_kernel(count, sends, features, face_hot, table, *outgoing):
    masked = masked_rows(features, count[0, 0])
    for f in range(6):
        layer = nn(masked, face_hot[:, f * 128 : (f + 1) * 128]).astype(BF)
        for s in range(SLOTS):
            table[6 * s + f] = layer[s * C : (s + 1) * C]
    table[6 * SLOTS] = jnp.zeros((C, 128), BF)
    for j in range(NOFF):
        for c in range(CAP):
            outgoing[j][c] = table[sends[0, 0, j, c]]


def upper_kernel(out_grad, down_hot, down_kernel, grad_active):
    tall = jnp.transpose(down_kernel[...].astype(F32)).astype(BF)
    down_rows = jnp.concatenate(
        [
            jnp.concatenate([tall[(4 * tx + t) * C : (4 * tx + t + 1) * C] for t in range(4)], axis=1)
            for tx in range(2)
        ],
        axis=0,
    )
    for s in range(SLOTS):
        turned = jnp.transpose(out_grad[0, s].astype(F32)).astype(BF)
        spread = jnp.concatenate(
            [nn(turned, down_hot[t * 64 : (t + 1) * 64]).astype(BF) for t in range(4)], axis=0
        )
        grad_active[s] = nn(down_rows, spread)


def main_kernel(
    count,
    sources,
    features,
    table,
    ahead,
    behind,
    ahead2,
    behind2,
    kernel,
    down_kernel,
    out_grad,
    grad_active,
    inner_hot,
    cap_hot,
    side_hot,
    down_hot,
    coarse,
    grad_preact,
    sums,
    halo,
    conv,
    entries,
    padded,
    stack,
    shifted,
    lowered,
    total,
):
    halo[0:LOCAL] = table[...]
    for j in range(NOFF):
        halo[LOCAL + j * CAP : LOCAL + (j + 1) * CAP] = (ahead, behind, ahead2, behind2)[j][...]
    for s in range(SLOTS):
        for k in range(26):
            entries[s * C : (s + 1) * C, k * 128 : (k + 1) * 128] = halo[sources[0, s, k]]
    for o in range(3):
        conv[o * C : (o + 1) * C] = kernel[:, o * 576 : (o + 1) * 576]
    masked = masked_rows(features, count[0, 0])
    padded[:, 0:128] = nn(entries[:, 0:1152], cap_hot[...]).astype(BF)
    padded[:, 1152:1280] = nn(entries[:, 2176:3328], cap_hot[...]).astype(BF)
    for i in range(4):
        block = nn(entries[:, 1152:2176], side_hot[:, i * 256 : (i + 1) * 256])
        block = block + nn(masked[:, i * 128 : (i + 1) * 128], inner_hot[...])
        padded[:, 128 + i * 256 : 384 + i * 256] = block.astype(BF)

    lane = lax.broadcasted_iota(jnp.int32, (C, 1024), 1) & 127
    row, column = lane // 10, lane % 10
    valid = (row >= 1) & (row <= 8) & (column >= 1) & (column <= 8)
    shifted[...] = jnp.zeros_like(shifted)
    total[...] = jnp.zeros_like(total)

    def brick(s, carry):
        filled = jnp.where(s < count[0, 0], 1.0, 0.0).astype(F32)
        here = pl.ds(pl.multiple_of(s * C, C), C)
        for x in range(10):
            plane = padded[here, x * 128 : (x + 1) * 128]
            for k, shift in enumerate(SHIFTS):
                moved = plane if shift == 0 else pltpu.roll(plane, (-shift) % 128, 1)
                stack[k * C : (k + 1) * C, x * 128 : (x + 1) * 128] = moved
        triple = nn(conv[...], stack[...])
        preact = triple[0:C, 0:1024] + triple[C : 2 * C, 128:1152] + triple[2 * C :, 256:1280]
        sigmoid = jax.nn.sigmoid(preact)
        active = jnp.where(valid, preact * sigmoid * filled, 0.0).astype(BF)
        halves = jnp.concatenate(
            [
                jnp.concatenate(
                    [active[:, (2 * X + tx) * 128 : (2 * X + tx + 1) * 128] for X in range(4)],
                    axis=1,
                )
                for tx in range(2)
            ],
            axis=0,
        )
        picked = nt(down_hot[...], halves).astype(BF)
        for t in range(4):
            lowered[here, t * 128 : (t + 1) * 128] = picked[t * 64 : (t + 1) * 64]
        upper = jnp.concatenate(
            [
                grad_active[s, (x % 2) * C : (x % 2 + 1) * C, (x // 2) * 128 : (x // 2 + 1) * 128]
                for x in range(8)
            ],
            axis=1,
        )
        grads = upper * sigmoid * (1.0 + preact * (1.0 - sigmoid)) * filled
        grads = jnp.where(valid, grads, 0.0).astype(BF)
        grad_preact[s] = grads
        for o in range(3):
            shifted[o * C : (o + 1) * C, o * 128 : o * 128 + 1024] = grads
        total[...] += nt(shifted[...], stack[...])
        return carry

    lax.fori_loop(0, SLOTS, brick, 0)
    rows = lowered[...]
    down_cols = jnp.concatenate(
        [down_kernel[:, (4 * tx + t) * C : (4 * tx + t + 1) * C] for t in range(4) for tx in range(2)],
        axis=1,
    )
    coarse[...] = nt(rows, down_cols).astype(BF).reshape(coarse.shape)
    turned = jnp.transpose(out_grad[...].reshape(SLOTS * 64, C2).astype(F32)).astype(BF)
    grad_down = nn(turned, rows)
    for j in range(5):
        width = min(128, 576 - j * 128)
        sums[j * 192 : (j + 1) * 192, 0:width] = total[:, j * 128 : j * 128 + width].astype(BF)
    sums[4 * 192 : 5 * 192, 64:128] = jnp.zeros((192, 64), BF)
    for j in range(4):
        sums[960 + j * C2 : 960 + (j + 1) * C2] = grad_down[:, j * 128 : (j + 1) * 128].astype(BF)
    sums[1472:1536] = jnp.zeros((64, 128), BF)


def fold_kernel(
    sources,
    grad_preact,
    conv_back,
    inner_hot,
    cap_hot,
    side_hot,
    interior,
    grad_local,
    to_ahead,
    to_behind,
    to_ahead2,
    to_behind2,
    stack,
    high,
    low,
    rims,
    grad_table,
):
    high[...] = jnp.zeros_like(high)

    def brick(s, carry):
        here = pl.ds(pl.multiple_of(s * C, C), C)
        for x in range(8):
            plane = grad_preact[s, :, x * 128 : (x + 1) * 128]
            for k, shift in enumerate(SHIFTS):
                moved = plane if shift == 0 else pltpu.roll(plane, shift % 128, 1)
                stack[k * C : (k + 1) * C, x * 128 : (x + 1) * 128] = moved
        triple = nn(conv_back[...], stack[...])
        for x in range(10):
            value = None
            for o in range(3):
                if 0 <= x - o < 8:
                    part = triple[o * C : (o + 1) * C, (x - o) * 128 : (x - o + 1) * 128]
                    value = part if value is None else value + part
            top = value.astype(BF)
            high[here, x * 128 : (x + 1) * 128] = top
            low[here, x * 128 : (x + 1) * 128] = (value - top.astype(F32)).astype(BF)
        return carry

    lax.fori_loop(0, SLOTS, brick, 0)
    rims[:, 0:1152] = nt(high[:, 0:128], cap_hot[...])
    rims[:, 1152:2176] = nt(high[:, 128:1152], side_hot[...])
    rims[:, 2176:3328] = nt(high[:, 1152:1280], cap_hot[...])
    grad_table[...] = jnp.zeros_like(grad_table)
    for s in range(SLOTS):
        for k in range(26):
            place = sources[0, s, k]
            grad_table[place] += rims[s * C : (s + 1) * C, k * 128 : (k + 1) * 128]
    for i in range(4):
        lanes = slice(128 + i * 256, 384 + i * 256)
        interior[:, i * 128 : (i + 1) * 128] = nt(high[:, lanes], inner_hot[...]) + nt(
            low[:, lanes], inner_hot[...]
        )
    grad_local[...] = grad_table[0:LOCAL]
    for j in range(NOFF):
        block = grad_table[LOCAL + j * CAP : LOCAL + (j + 1) * CAP].astype(BF)
        (to_ahead, to_behind, to_ahead2, to_behind2)[j][...] = block


def unpack_kernel(sums, grad_kernel, grad_down):
    parts = []
    for o in range(3):
        tiles = [sums[j * 192 + o * C : j * 192 + (o + 1) * C].astype(F32) for j in range(5)]
        parts.append(jnp.concatenate(tiles, axis=1)[:, :576])
    grad_kernel[...] = jnp.concatenate(parts, axis=1)
    tiles = [sums[960 + t * C2 : 960 + (t + 1) * C2].astype(F32) for t in range(4)]
    grad_down[...] = jnp.concatenate(
        [tiles[t][:, tx * C : (tx + 1) * C] for tx in range(2) for t in range(4)], axis=1
    )


def finish_kernel(
    count,
    sends,
    interior,
    grad_local,
    ahead,
    behind,
    ahead2,
    behind2,
    face_hot,
    grad_features,
    table,
    layers,
):
    table[...] = grad_local[...]
    for j in range(NOFF):
        for c in range(CAP):
            block = (ahead, behind, ahead2, behind2)[j][c]
            table[sends[0, 0, j, c]] += block.astype(F32)
    for s in range(SLOTS):
        for f in range(6):
            layers[s * C : (s + 1) * C, f * 128 : (f + 1) * 128] = table[6 * s + f].astype(BF)
    whole = interior[...] + nt(layers[...], face_hot[...])
    for s in range(SLOTS):
        filled = jnp.where(s < count[0, 0], 1.0, 0.0).astype(F32)
        grad_features[0, s] = (whole[s * C : (s + 1) * C] * filled).astype(BF)


def call(kernel, limit, memories, outs, scratch, flops, *args):
    where = {"s": pltpu.SMEM, "v": pltpu.VMEM}
    return pl.pallas_call(
        kernel,
        in_specs=[pl.BlockSpec(memory_space=where[m]) for m in memories],
        out_specs=[pl.BlockSpec(memory_space=pltpu.VMEM) for _ in outs],
        out_shape=[jax.ShapeDtypeStruct(s, d) for s, d in outs],
        scratch_shapes=[pltpu.VMEM(s, d) for s, d in scratch],
        compiler_params=pltpu.CompilerParams(vmem_limit_bytes=limit * 2**20),
        cost_estimate=pl.CostEstimate(flops=flops, bytes_accessed=2**20, transcendentals=0),
        name=kernel.__name__,
    )(*args)


def gather_sum(block, axes, parts):
    copies = jnp.broadcast_to(block[None], (parts,) + block.shape)
    got = lax.all_to_all(copies, axes, 0, 0)
    return got.astype(F32).sum(0)


def near_sum(block, sizes):
    parts = sizes["x"] * sizes["c"] * sizes["grp"]
    rows = block.shape[0] // parts
    got = lax.all_to_all(block.reshape(parts, rows, 128), NEAR, 0, 0)
    return got.astype(F32).sum(0).astype(BF)


def near_gather(block, sizes):
    parts = sizes["x"] * sizes["c"] * sizes["grp"]
    copies = jnp.broadcast_to(block[None], (parts,) + block.shape)
    return lax.all_to_all(copies, NEAR, 0, 0).reshape(parts * block.shape[0], 128)


def from_behind(block, axes, devices, distance):
    route = [(i - distance, i) for i in range(devices) if 0 <= i - distance < devices]
    return lax.ppermute(block, axes, route)


def on_device(sizes, features, brick_count, send_list, halo_src, kernel, down_kernel, out_grad):
    face_hot, inner_hot, cap_hot, side_hot, down_hot = one_hot_tables()
    tile = ("z", "x", "c")
    devices = sizes["z"] * sizes["x"] * sizes["c"]
    swap = [((CAP, C, 128), BF)] * NOFF
    conv_back = kernel.reshape(C, 3, 9, C).transpose(1, 3, 2, 0).reshape(192, 576)

    table, *outgoing = call(
        faces_kernel,
        8,
        "ssvv",
        [((LOCAL, C, 128), BF)] + swap,
        [],
        2 * 256 * 512 * 768,
        brick_count,
        send_list,
        features,
        face_hot,
    )
    received = [from_behind(b, tile, devices, o) for b, o in zip(outgoing, OFFSETS)]
    (grad_active,) = call(
        upper_kernel,
        12,
        "vvv",
        [((SLOTS, 2 * C, 512), F32)],
        [],
        10**9,
        out_grad,
        down_hot,
        down_kernel,
    )
    coarse, grad_preact, sums = call(
        main_kernel,
        28,
        "ss" + "v" * 14,
        [((1, SLOTS, 64, C2), BF), ((SLOTS, C, 1024), BF), ((1536, 128), BF)],
        [
            ((TABLE, C, 128), BF),
            ((192, 576), BF),
            ((256, 26 * 128), BF),
            ((256, 1280), BF),
            ((576, 1280), BF),
            ((192, 1280), BF),
            ((256, 512), BF),
            ((192, 576), F32),
        ],
        5 * 10**9,
        brick_count,
        halo_src,
        features,
        table,
        *received,
        kernel,
        down_kernel,
        out_grad,
        grad_active,
        inner_hot,
        cap_hot,
        side_hot,
        down_hot,
    )
    part = near_sum(sums, sizes)
    interior, grad_local, *remote = call(
        fold_kernel,
        24,
        "svvvvv",
        [((256, 512), F32), ((LOCAL, C, 128), F32)] + swap,
        [
            ((576, 1024), BF),
            ((256, 1280), BF),
            ((256, 1280), BF),
            ((256, 26 * 128), F32),
            ((TABLE, C, 128), F32),
        ],
        3 * 10**9,
        halo_src,
        grad_preact,
        conv_back,
        inner_hot,
        cap_hot,
        side_hot,
    )
    part, *remote = lax.optimization_barrier((part, *remote))
    part = gather_sum(part, ("z",), sizes["z"])
    returned = [from_behind(b, tile, devices, -o) for b, o in zip(remote, OFFSETS)]
    part, *returned = lax.optimization_barrier((part, *returned))
    sums = near_gather(part.astype(BF), sizes)
    (grad_features,) = call(
        finish_kernel,
        12,
        "ss" + "v" * 7,
        [((1, SLOTS, C, 512), BF)],
        [((LOCAL, C, 128), F32), ((256, 768), BF)],
        2 * 256 * 512 * 768,
        brick_count,
        send_list,
        interior,
        grad_local,
        *returned,
        face_hot,
    )
    grad_kernel, grad_down = call(
        unpack_kernel, 8, "v", [((C, 1728), F32), ((C2, 512), F32)], [], 10**6, sums
    )
    return coarse, grad_features, grad_kernel, grad_down


def solution(mesh):
    tile, grp = mesh.shape["tile"], mesh.shape["grp"]
    sizes = {"z": tile // 8, "x": 4, "c": 2, "grp": grp}
    fine = Mesh(mesh.devices.reshape(tuple(sizes.values())), tuple(sizes))
    line = ("z", "x", "c")
    in_specs = (
        P("grp", line, None, None),
        P("grp", line),
        P("grp", line, None, None),
        P("grp", line, None),
        P(),
        P(),
        P("grp", line, None, None),
    )
    out_specs = (P("grp", line, None, None), P("grp", line, None, None), P(), P())

    def step(*args):
        return on_device(sizes, *args)

    return jax.shard_map(step, mesh=fine, in_specs=in_specs, out_specs=out_specs, check_vma=False)
```

```python
import jax
import jax.numpy as jnp
import ml_dtypes
import numpy as np
from jax import lax
from jax.experimental import pallas as pl
from jax.experimental.pallas import tpu as pltpu
from jax.sharding import Mesh
from jax.sharding import PartitionSpec as P

BF = jnp.bfloat16
F32 = jnp.float32
DIRECTIONS = [
    (a, b, c) for a in (-1, 0, 1) for b in (-1, 0, 1) for c in (-1, 0, 1) if (a, b, c) != (0, 0, 0)
]
SHIFTS = [10 * b + c for b in (-1, 0, 1) for c in (-1, 0, 1)]
SLOTS, C, C2, NOFF, CAP = 4, 64, 128, 4, 4
LOCAL = 6 * SLOTS + 1
TABLE = LOCAL + NOFF * CAP
OFFSETS = (1, -1, 2, -2)
NEAR = ("zl", "x", "c", "grp")


def rim_cells(d, full):
    if d == -1:
        return [(7, 0)]
    if d == 1:
        return [(0, 9)]
    return [(i, i + 1) for i in range(full)]


def one_hot_tables():
    faces = np.zeros((512, 6, 128), np.float32)
    for x in range(8):
        for y in range(8):
            for z in range(8):
                v = (x, y, z)
                for a in range(3):
                    p, q = [v[i] for i in range(3) if i != a]
                    for e in range(2):
                        if v[a] == 7 * e:
                            faces[x * 64 + y * 8 + z, 2 * a + e, p * 8 + q] = 1
    inner = np.zeros((2, 64, 2, 128), np.float32)
    for s in range(2):
        for y in range(8):
            for z in range(8):
                inner[s, y * 8 + z, s, (y + 1) * 10 + z + 1] = 1
    cap = np.zeros((9, 128, 128), np.float32)
    side = np.zeros((8, 128, 8, 128), np.float32)
    for m, d in enumerate([d for d in DIRECTIONS if d[0] == 0]):
        if d[1] != 0:
            yy = 0 if d[1] == -1 else 9
            for x in range(8):
                for i, zz in rim_cells(d[2], 8):
                    side[m, x * 8 + i, x, yy * 10 + zz] = 1
        else:
            zz = 0 if d[2] == -1 else 9
            for x in range(8):
                for y in range(8):
                    side[m, x * 8 + y, x, (y + 1) * 10 + zz] = 1
    for m, (dy, dz) in enumerate([(b, c) for b in (-1, 0, 1) for c in (-1, 0, 1)]):
        for i, yy in rim_cells(dy, 8):
            for k, zz in rim_cells(dz, 8):
                cap[m, i * 8 + k, yy * 10 + zz] = 1
    down = np.zeros((2, 2, 4, 4, 4, 4, 128), np.float32)
    for ty in range(2):
        for tz in range(2):
            for X in range(4):
                for Y in range(4):
                    for Z in range(4):
                        lane = (2 * Y + ty + 1) * 10 + 2 * Z + tz + 1
                        down[ty, tz, X, Y, Z, X, lane] = 1
    b = ml_dtypes.bfloat16
    return (
        faces.reshape(512, 768).astype(b),
        inner.reshape(128, 256).astype(b),
        cap.reshape(1152, 128).astype(b),
        side.reshape(1024, 1024).astype(b),
        down.reshape(256, 512).astype(b),
    )


def nn(a, b):
    return jnp.dot(a, b, preferred_element_type=F32)


def nt(a, b):
    return lax.dot_general(a, b, (((1,), (1,)), ((), ())), preferred_element_type=F32)


def masked_rows(features, count):
    return jnp.concatenate(
        [features[0, s] * jnp.where(s < count, 1.0, 0.0).astype(BF) for s in range(SLOTS)], axis=0
    )


def fetch(sources, targets, done):
    copies = [
        pltpu.make_async_copy(a, b, done.at[i]) for i, (a, b) in enumerate(zip(sources, targets))
    ]
    for copy in copies:
        copy.start()
    return copies


def faces_kernel(
    count, sends_far, features_far, face_far, table, *rest
):
    outgoing, (sends, features, face_hot, done) = rest[:NOFF], rest[NOFF:]
    copies = fetch((features_far, face_far, sends_far), (features, face_hot, sends), done)
    for copy in copies:
        copy.wait()
    masked = masked_rows(features, count[0, 0])
    for f in range(6):
        layer = nn(masked, face_hot[:, f * 128 : (f + 1) * 128]).astype(BF)
        for s in range(SLOTS):
            table[6 * s + f] = layer[s * C : (s + 1) * C]
    table[6 * SLOTS] = jnp.zeros((C, 128), BF)
    for j in range(NOFF):
        for c in range(CAP):
            outgoing[j][c] = table[sends[0, 0, j, c]]


def upper_kernel(
    out_grad,
    down_hot,
    down_kernel,
    kernel,
    grad_active,
    conv_back,
    out_grad_kept,
    down_hot_kept,
    down_kernel_kept,
    kernel_kept,
    done,
):
    copies = fetch(
        (out_grad, down_hot, down_kernel, kernel),
        (out_grad_kept, down_hot_kept, down_kernel_kept, kernel_kept),
        done,
    )
    tall = jnp.transpose(kernel[...].astype(F32)).astype(BF)
    for o in range(3):
        conv_back[o * C : (o + 1) * C] = jnp.concatenate(
            [tall[(9 * o + k) * C : (9 * o + k + 1) * C] for k in range(9)], axis=1
        )
    tall = jnp.transpose(down_kernel[...].astype(F32)).astype(BF)
    down_rows = jnp.concatenate(
        [
            jnp.concatenate([tall[(4 * tx + t) * C : (4 * tx + t + 1) * C] for t in range(4)], axis=1)
            for tx in range(2)
        ],
        axis=0,
    )
    for s in range(SLOTS):
        turned = jnp.transpose(out_grad[0, s].astype(F32)).astype(BF)
        spread = jnp.concatenate(
            [nn(turned, down_hot[t * 64 : (t + 1) * 64]).astype(BF) for t in range(4)], axis=0
        )
        grad_active[s] = nn(down_rows, spread)
    for copy in copies:
        copy.wait()


def main_kernel(
    count,
    sources,
    features,
    table,
    ahead,
    behind,
    ahead2,
    behind2,
    kernel,
    down_kernel,
    out_grad,
    grad_active,
    inner_hot,
    cap_hot,
    side_hot,
    down_hot,
    coarse,
    grad_preact,
    sums,
    halo,
    conv,
    entries,
    padded,
    stack,
    shifted,
    lowered,
    total,
):
    halo[0:LOCAL] = table[...]
    for j in range(NOFF):
        halo[LOCAL + j * CAP : LOCAL + (j + 1) * CAP] = (ahead, behind, ahead2, behind2)[j][...]
    for s in range(SLOTS):
        for k in range(26):
            entries[s * C : (s + 1) * C, k * 128 : (k + 1) * 128] = halo[sources[0, s, k]]
    for o in range(3):
        conv[o * C : (o + 1) * C] = kernel[:, o * 576 : (o + 1) * 576]
    masked = masked_rows(features, count[0, 0])
    padded[:, 0:128] = nn(entries[:, 0:1152], cap_hot[...]).astype(BF)
    padded[:, 1152:1280] = nn(entries[:, 2176:3328], cap_hot[...]).astype(BF)
    for i in range(4):
        block = nn(entries[:, 1152:2176], side_hot[:, i * 256 : (i + 1) * 256])
        block = block + nn(masked[:, i * 128 : (i + 1) * 128], inner_hot[...])
        padded[:, 128 + i * 256 : 384 + i * 256] = block.astype(BF)

    lane = lax.broadcasted_iota(jnp.int32, (C, 1024), 1) & 127
    row, column = lane // 10, lane % 10
    valid = (row >= 1) & (row <= 8) & (column >= 1) & (column <= 8)
    shifted[...] = jnp.zeros_like(shifted)
    total[...] = jnp.zeros_like(total)

    def brick(s, carry):
        filled = jnp.where(s < count[0, 0], 1.0, 0.0).astype(F32)
        here = pl.ds(pl.multiple_of(s * C, C), C)
        for x in range(10):
            plane = padded[here, x * 128 : (x + 1) * 128]
            for k, shift in enumerate(SHIFTS):
                moved = plane if shift == 0 else pltpu.roll(plane, (-shift) % 128, 1)
                stack[k * C : (k + 1) * C, x * 128 : (x + 1) * 128] = moved
        triple = nn(conv[...], stack[...])
        preact = triple[0:C, 0:1024] + triple[C : 2 * C, 128:1152] + triple[2 * C :, 256:1280]
        sigmoid = jax.nn.sigmoid(preact)
        active = jnp.where(valid, preact * sigmoid * filled, 0.0).astype(BF)
        halves = jnp.concatenate(
            [
                jnp.concatenate(
                    [active[:, (2 * X + tx) * 128 : (2 * X + tx + 1) * 128] for X in range(4)],
                    axis=1,
                )
                for tx in range(2)
            ],
            axis=0,
        )
        picked = nt(down_hot[...], halves).astype(BF)
        for t in range(4):
            lowered[here, t * 128 : (t + 1) * 128] = picked[t * 64 : (t + 1) * 64]
        upper = jnp.concatenate(
            [
                grad_active[s, (x % 2) * C : (x % 2 + 1) * C, (x // 2) * 128 : (x // 2 + 1) * 128]
                for x in range(8)
            ],
            axis=1,
        )
        grads = upper * sigmoid * (1.0 + preact * (1.0 - sigmoid)) * filled
        grads = jnp.where(valid, grads, 0.0).astype(BF)
        grad_preact[s] = grads
        for o in range(3):
            shifted[o * C : (o + 1) * C, o * 128 : o * 128 + 1024] = grads
        total[...] += nt(shifted[...], stack[...])
        return carry

    lax.fori_loop(0, SLOTS, brick, 0)
    rows = lowered[...]
    down_cols = jnp.concatenate(
        [down_kernel[:, (4 * tx + t) * C : (4 * tx + t + 1) * C] for t in range(4) for tx in range(2)],
        axis=1,
    )
    coarse[...] = nt(rows, down_cols).astype(BF).reshape(coarse.shape)
    turned = jnp.transpose(out_grad[...].reshape(SLOTS * 64, C2).astype(F32)).astype(BF)
    grad_down = nn(turned, rows)
    for j in range(5):
        width = min(128, 576 - j * 128)
        sums[j * 192 : (j + 1) * 192, 0:width] = total[:, j * 128 : j * 128 + width].astype(BF)
    sums[4 * 192 : 5 * 192, 64:128] = jnp.zeros((192, 64), BF)
    for j in range(4):
        sums[960 + j * C2 : 960 + (j + 1) * C2] = grad_down[:, j * 128 : (j + 1) * 128].astype(BF)
    sums[1472:1536] = jnp.zeros((64, 128), BF)


def fold_kernel(
    sources,
    grad_preact,
    conv_back,
    inner_hot,
    cap_hot,
    side_hot,
    interior,
    grad_local,
    to_ahead,
    to_behind,
    to_ahead2,
    to_behind2,
    stack,
    high,
    low,
    rims,
    grad_table,
):
    high[...] = jnp.zeros_like(high)

    def brick(s, carry):
        here = pl.ds(pl.multiple_of(s * C, C), C)
        for x in range(8):
            plane = grad_preact[s, :, x * 128 : (x + 1) * 128]
            for k, shift in enumerate(SHIFTS):
                moved = plane if shift == 0 else pltpu.roll(plane, shift % 128, 1)
                stack[k * C : (k + 1) * C, x * 128 : (x + 1) * 128] = moved
        triple = nn(conv_back[...], stack[...])
        for x in range(10):
            value = None
            for o in range(3):
                if 0 <= x - o < 8:
                    part = triple[o * C : (o + 1) * C, (x - o) * 128 : (x - o + 1) * 128]
                    value = part if value is None else value + part
            top = value.astype(BF)
            high[here, x * 128 : (x + 1) * 128] = top
            low[here, x * 128 : (x + 1) * 128] = (value - top.astype(F32)).astype(BF)
        return carry

    lax.fori_loop(0, SLOTS, brick, 0)
    rims[:, 0:1152] = nt(high[:, 0:128], cap_hot[...])
    rims[:, 1152:2176] = nt(high[:, 128:1152], side_hot[...])
    rims[:, 2176:3328] = nt(high[:, 1152:1280], cap_hot[...])
    grad_table[...] = jnp.zeros_like(grad_table)
    for s in range(SLOTS):
        for k in range(26):
            place = sources[0, s, k]
            grad_table[place] += rims[s * C : (s + 1) * C, k * 128 : (k + 1) * 128]
    for i in range(4):
        lanes = slice(128 + i * 256, 384 + i * 256)
        interior[:, i * 128 : (i + 1) * 128] = nt(high[:, lanes], inner_hot[...]) + nt(
            low[:, lanes], inner_hot[...]
        )
    grad_local[...] = grad_table[0:LOCAL]
    for j in range(NOFF):
        block = grad_table[LOCAL + j * CAP : LOCAL + (j + 1) * CAP].astype(BF)
        (to_ahead, to_behind, to_ahead2, to_behind2)[j][...] = block


def unpack_kernel(sums, grad_kernel, grad_down):
    parts = []
    for o in range(3):
        tiles = [sums[j * 192 + o * C : j * 192 + (o + 1) * C].astype(F32) for j in range(5)]
        parts.append(jnp.concatenate(tiles, axis=1)[:, :576])
    grad_kernel[...] = jnp.concatenate(parts, axis=1)
    tiles = [sums[960 + t * C2 : 960 + (t + 1) * C2].astype(F32) for t in range(4)]
    grad_down[...] = jnp.concatenate(
        [tiles[t][:, tx * C : (tx + 1) * C] for tx in range(2) for t in range(4)], axis=1
    )


def finish_kernel(
    count,
    sends,
    interior,
    grad_local,
    ahead,
    behind,
    ahead2,
    behind2,
    face_hot,
    grad_features,
    table,
    layers,
):
    table[...] = grad_local[...]
    for j in range(NOFF):
        for c in range(CAP):
            block = (ahead, behind, ahead2, behind2)[j][c]
            table[sends[0, 0, j, c]] += block.astype(F32)
    for s in range(SLOTS):
        for f in range(6):
            layers[s * C : (s + 1) * C, f * 128 : (f + 1) * 128] = table[6 * s + f].astype(BF)
    whole = interior[...] + nt(layers[...], face_hot[...])
    for s in range(SLOTS):
        filled = jnp.where(s < count[0, 0], 1.0, 0.0).astype(F32)
        grad_features[0, s] = (whole[s * C : (s + 1) * C] * filled).astype(BF)


def call(kernel, limit, memories, outs, scratch, flops, *args):
    where = {"s": pltpu.SMEM, "v": pltpu.VMEM, "h": pltpu.HBM}
    return pl.pallas_call(
        kernel,
        in_specs=[pl.BlockSpec(memory_space=where[m]) for m in memories],
        out_specs=[pl.BlockSpec(memory_space=pltpu.VMEM) for _ in outs],
        out_shape=[jax.ShapeDtypeStruct(s, d) for s, d in outs],
        scratch_shapes=[pltpu.VMEM(*s) if isinstance(s, tuple) else s for s in scratch],
        compiler_params=pltpu.CompilerParams(vmem_limit_bytes=limit * 2**20),
        cost_estimate=pl.CostEstimate(flops=flops, bytes_accessed=2**20, transcendentals=0),
        name=kernel.__name__,
    )(*args)


def gather_sum(block, axes, parts):
    copies = jnp.broadcast_to(block[None], (parts,) + block.shape)
    got = lax.all_to_all(copies, axes, 0, 0)
    return got.astype(F32).sum(0)


def near_sum(block, sizes):
    parts = sizes["zl"] * sizes["x"] * sizes["c"] * sizes["grp"]
    rows = block.shape[0] // parts
    got = lax.all_to_all(block.reshape(parts, rows, 128), NEAR, 0, 0)
    return got.astype(F32).sum(0).astype(BF)


def near_gather(block, sizes):
    parts = sizes["zl"] * sizes["x"] * sizes["c"] * sizes["grp"]
    copies = jnp.broadcast_to(block[None], (parts,) + block.shape)
    return lax.all_to_all(copies, NEAR, 0, 0).reshape(parts * block.shape[0], 128)


def from_behind(block, axes, devices, distance):
    route = [(i - distance, i) for i in range(devices) if 0 <= i - distance < devices]
    return lax.ppermute(block, axes, route)


def on_device(sizes, features, brick_count, send_list, halo_src, kernel, down_kernel, out_grad):
    face_hot, inner_hot, cap_hot, side_hot, down_hot = one_hot_tables()
    tile = ("zh", "zl", "x", "c")
    devices = sizes["zh"] * sizes["zl"] * sizes["x"] * sizes["c"]
    swap = [((CAP, C, 128), BF)] * NOFF

    table, *outgoing = call(
        faces_kernel,
        56,
        "shhh",
        [((LOCAL, C, 128), BF)] + swap,
        [
            pltpu.SMEM((1, 1, NOFF, CAP), jnp.int32),
            ((1, SLOTS, C, 512), BF),
            ((512, 768), BF),
            pltpu.SemaphoreType.DMA((3,)),
        ],
        2 * 256 * 512 * 768,
        brick_count,
        send_list,
        features,
        face_hot,
    )
    received = [from_behind(b, tile, devices, o) for b, o in zip(outgoing, OFFSETS)]
    grad_active, conv_back, out_grad, down_hot, down_kernel, kernel = call(
        upper_kernel,
        12,
        "vvvv",
        [
            ((SLOTS, 2 * C, 512), F32),
            ((192, 576), BF),
            ((1, SLOTS, 64, C2), BF),
            ((256, 512), BF),
            ((C2, 512), BF),
            ((C, 1728), BF),
        ],
        [pltpu.SemaphoreType.DMA((4,))],
        10**9,
        out_grad,
        down_hot,
        down_kernel,
        kernel,
    )
    coarse, grad_preact, sums = call(
        main_kernel,
        28,
        "ss" + "v" * 14,
        [
            ((1, SLOTS, 64, C2), BF),
            ((SLOTS, C, 1024), BF),
            ((1536, 128), BF),
        ],
        [
            ((TABLE, C, 128), BF),
            ((192, 576), BF),
            ((256, 26 * 128), BF),
            ((256, 1280), BF),
            ((576, 1280), BF),
            ((192, 1280), BF),
            ((256, 512), BF),
            ((192, 576), F32),
        ],
        5 * 10**9,
        brick_count,
        halo_src,
        features,
        table,
        *received,
        kernel,
        down_kernel,
        out_grad,
        grad_active,
        inner_hot,
        cap_hot,
        side_hot,
        down_hot,
    )
    part = near_sum(sums, sizes)
    interior, grad_local, *remote = call(
        fold_kernel,
        24,
        "svvvvv",
        [((256, 512), F32), ((LOCAL, C, 128), F32)] + swap,
        [
            ((576, 1024), BF),
            ((256, 1280), BF),
            ((256, 1280), BF),
            ((256, 26 * 128), F32),
            ((TABLE, C, 128), F32),
        ],
        3 * 10**9,
        halo_src,
        grad_preact,
        conv_back,
        inner_hot,
        cap_hot,
        side_hot,
    )
    part, *remote = lax.optimization_barrier((part, *remote))
    part = gather_sum(part, ("zh",), sizes["zh"])
    returned = [from_behind(b, tile, devices, -o) for b, o in zip(remote, OFFSETS)]
    part, *returned = lax.optimization_barrier((part, *returned))
    sums = near_gather(part.astype(BF), sizes)
    (grad_features,) = call(
        finish_kernel,
        12,
        "ss" + "v" * 7,
        [((1, SLOTS, C, 512), BF)],
        [((LOCAL, C, 128), F32), ((256, 768), BF)],
        2 * 256 * 512 * 768,
        brick_count,
        send_list,
        interior,
        grad_local,
        *returned,
        face_hot,
    )
    grad_kernel, grad_down = call(
        unpack_kernel, 8, "v", [((C, 1728), F32), ((C2, 512), F32)], [], 10**6, sums
    )
    return coarse, grad_features, grad_kernel, grad_down


def solution(mesh):
    tile, grp = mesh.shape["tile"], mesh.shape["grp"]
    planes = tile // 8
    pair = 2 - planes % 2
    sizes = {"zh": planes // pair, "zl": pair, "x": 4, "c": 2, "grp": grp}
    fine = Mesh(mesh.devices.reshape(tuple(sizes.values())), tuple(sizes))
    line = ("zh", "zl", "x", "c")
    in_specs = (
        P("grp", line, None, None),
        P("grp", line),
        P("grp", line, None, None),
        P("grp", line, None),
        P(),
        P(),
        P("grp", line, None, None),
    )
    out_specs = (P("grp", line, None, None), P("grp", line, None, None), P(), P())

    def step(*args):
        return on_device(sizes, *args)

    return jax.shard_map(step, mesh=fine, in_specs=in_specs, out_specs=out_specs, check_vma=False)
```

```python
import jax
import jax.numpy as jnp
import ml_dtypes
import numpy as np
from jax import lax
from jax.experimental import pallas as pl
from jax.experimental.pallas import tpu as pltpu
from jax.sharding import Mesh
from jax.sharding import PartitionSpec as P

BF = jnp.bfloat16
F32 = jnp.float32
DIRECTIONS = [
    (a, b, c) for a in (-1, 0, 1) for b in (-1, 0, 1) for c in (-1, 0, 1) if (a, b, c) != (0, 0, 0)
]
SHIFTS = [10 * b + c for b in (-1, 0, 1) for c in (-1, 0, 1)]
SLOTS, C, C2, NOFF, CAP = 4, 64, 128, 4, 4
LOCAL = 6 * SLOTS + 1
TABLE = LOCAL + NOFF * CAP
PLACES = list(range(9)) + [None] + list(range(9, 26)) + [None]
OFFSETS = (1, -1, 2, -2)
NEAR = ("x", "c", "grp")


def rim_cells(d, full):
    if d == -1:
        return [(7, 0)]
    if d == 1:
        return [(0, 9)]
    return [(i, i + 1) for i in range(full)]


def one_hot_tables():
    faces = np.zeros((512, 6, 128), np.float32)
    for x in range(8):
        for y in range(8):
            for z in range(8):
                v = (x, y, z)
                for a in range(3):
                    p, q = [v[i] for i in range(3) if i != a]
                    for e in range(2):
                        if v[a] == 7 * e:
                            faces[x * 64 + y * 8 + z, 2 * a + e, p * 8 + q] = 1
    inner = np.zeros((2, 64, 2, 128), np.float32)
    for s in range(2):
        for y in range(8):
            for z in range(8):
                inner[s, y * 8 + z, s, (y + 1) * 10 + z + 1] = 1
    cap = np.zeros((10, 64, 128), np.float32)
    side = np.zeros((8, 64, 8, 128), np.float32)
    for m, d in enumerate([d for d in DIRECTIONS if d[0] == 0]):
        if d[1] != 0:
            yy = 0 if d[1] == -1 else 9
            for x in range(8):
                for i, zz in rim_cells(d[2], 8):
                    side[m, x * 8 + i, x, yy * 10 + zz] = 1
        else:
            zz = 0 if d[2] == -1 else 9
            for x in range(8):
                for y in range(8):
                    side[m, x * 8 + y, x, (y + 1) * 10 + zz] = 1
    for m, (dy, dz) in enumerate([(b, c) for b in (-1, 0, 1) for c in (-1, 0, 1)]):
        for i, yy in rim_cells(dy, 8):
            for k, zz in rim_cells(dz, 8):
                cap[m, i * 8 + k, yy * 10 + zz] = 1
    window = np.zeros((2, 128, 9, 2, 64), np.float32)
    for k, shift in enumerate(SHIFTS):
        for y in range(8):
            for z in range(8):
                for p in range(2):
                    window[p, (y + 1) * 10 + z + 1 + shift, k, p, y * 8 + z] = 1
    spread = np.zeros((4, 4, 4, 2, 2, 4, 64), np.float32)
    pick = np.zeros((2, 2, 2, 4, 4, 2, 64), np.float32)
    for ty in range(2):
        for tz in range(2):
            for Y in range(4):
                for Z in range(4):
                    lane = (2 * Y + ty) * 8 + 2 * Z + tz
                    for X in range(4):
                        spread[X, Y, Z, ty, tz, X, lane] = 1
                    for tx in range(2):
                        pick[tx, ty, tz, Y, Z, tx, lane] = 1
    b = ml_dtypes.bfloat16
    return (
        faces.reshape(512, 768).astype(b),
        inner.reshape(128, 256).astype(b),
        cap.reshape(640, 128).astype(b),
        side.reshape(512, 1024).astype(b),
        window.reshape(256, 1152).astype(b),
        spread.reshape(64, 1024).astype(b),
        pick.reshape(128, 128).astype(b),
    )


def nn(a, b):
    return jnp.dot(a, b, preferred_element_type=F32)


def nt(a, b):
    return lax.dot_general(a, b, (((1,), (1,)), ((), ())), preferred_element_type=F32)


def masked_rows(features, count):
    return jnp.concatenate(
        [features[0, s] * jnp.where(s < count, 1.0, 0.0).astype(BF) for s in range(SLOTS)], axis=0
    )


def fetch(sources, targets, done):
    copies = [
        pltpu.make_async_copy(a, b, done.at[i]) for i, (a, b) in enumerate(zip(sources, targets))
    ]
    for copy in copies:
        copy.start()
    return copies


def faces_kernel(
    count, sends_far, features_far, face_far, table, *rest
):
    outgoing, (sends, features, face_hot, done) = rest[:NOFF], rest[NOFF:]
    copies = fetch((features_far, face_far, sends_far), (features, face_hot, sends), done)
    for copy in copies:
        copy.wait()
    masked = masked_rows(features, count[0, 0])
    for f in range(6):
        layer = nn(masked, face_hot[:, f * 128 : (f + 1) * 128]).astype(BF)
        for s in range(SLOTS):
            table[6 * s + f] = layer[s * C : (s + 1) * C]
    table[6 * SLOTS] = jnp.zeros((C, 128), BF)
    for j in range(NOFF):
        for c in range(CAP):
            outgoing[j][c] = table[sends[0, 0, j, c]]


def main_kernel(
    count,
    sources,
    features,
    table,
    ahead,
    behind,
    ahead2,
    behind2,
    kernel,
    down_kernel,
    out_grad,
    inner_hot,
    cap_hot,
    side_hot,
    window_hot,
    spread_hot,
    pick_hot,
    coarse,
    grad_preact,
    sums,
    conv_back,
    halo,
    halo_high,
    conv,
    entries,
    padded,
    stack,
    shifted,
    lowered,
    total,
):
    halo[0:LOCAL] = table[...]
    for j in range(NOFF):
        halo[LOCAL + j * CAP : LOCAL + (j + 1) * CAP] = (ahead, behind, ahead2, behind2)[j][...]
    halo_high[...] = pltpu.roll(halo[...].reshape(TABLE * C, 128), 64, 1).reshape(TABLE, C, 128)
    for s in range(SLOTS):
        for t in range(14):
            even, odd = PLACES[2 * t], PLACES[2 * t + 1]
            block = halo[sources[0, s, even]]
            if odd is not None:
                block = block + halo_high[sources[0, s, odd]]
            entries[s * C : (s + 1) * C, t * 128 : (t + 1) * 128] = block
    masked = masked_rows(features, count[0, 0])
    padded[:, 0:128] = nn(entries[:, 0:640], cap_hot[...]).astype(BF)
    padded[:, 1152:1280] = nn(entries[:, 1152:1792], cap_hot[...]).astype(BF)
    for i in range(4):
        block = nn(entries[:, 640:1152], side_hot[:, i * 256 : (i + 1) * 256])
        block = block + nn(masked[:, i * 128 : (i + 1) * 128], inner_hot[...])
        padded[:, 128 + i * 256 : 384 + i * 256] = block.astype(BF)
    for i in range(5):
        planes = nn(padded[:, i * 256 : (i + 1) * 256], window_hot[...]).astype(BF)
        for s in range(SLOTS):
            lanes = slice((s % 2) * 640 + i * 128, (s % 2) * 640 + (i + 1) * 128)
            for k in range(9):
                block = planes[s * C : (s + 1) * C, k * 128 : (k + 1) * 128]
                stack[s // 2, k * C : (k + 1) * C, lanes] = block

    for o in range(3):
        conv[o * C : (o + 1) * C] = kernel[:, o * 576 : (o + 1) * 576]
    tall = jnp.transpose(kernel[...].astype(F32)).astype(BF)
    for o in range(3):
        conv_back[o * C : (o + 1) * C] = jnp.concatenate(
            [tall[(9 * o + k) * C : (9 * o + k + 1) * C] for k in range(9)], axis=1
        )
    tall = jnp.transpose(down_kernel[...].astype(F32)).astype(BF)
    down_rows = jnp.concatenate(
        [
            jnp.concatenate([tall[(4 * tx + t) * C : (4 * tx + t + 1) * C] for t in range(4)], axis=1)
            for tx in range(2)
        ],
        axis=0,
    )
    left = lax.broadcasted_iota(jnp.int32, (16, 128), 1) < 64
    edge = jnp.zeros((C, 64), BF)
    wide = jnp.zeros((C, 128), BF)
    total[...] = jnp.zeros_like(total)

    def pair(p, carry):
        triple = nn(conv[...], stack[p])
        for j in range(2):
            s = 2 * p + j
            filled = jnp.where(s < count[0, 0], 1.0, 0.0).astype(F32)
            base = j * 640
            preact = (
                triple[0:C, base : base + 512]
                + triple[C : 2 * C, base + 64 : base + 576]
                + triple[2 * C :, base + 128 : base + 640]
            )
            sigmoid = jax.nn.sigmoid(preact)
            active = (preact * sigmoid * filled).astype(BF)
            for h in range(2):
                halves = [active[:, (2 * h + i) * 128 : (2 * h + i + 1) * 128] for i in range(2)]
                rows = jnp.concatenate([halves[0], halves[0], halves[1], halves[1]], axis=0)
                picked = nt(pick_hot[...], rows)
                for i in range(2):
                    X = 2 * h + i
                    for q in range(4):
                        lanes = slice(i * 128, (i + 1) * 128)
                        block = jnp.where(
                            left,
                            picked[32 * q : 32 * q + 16, lanes],
                            picked[32 * q + 16 : 32 * q + 32, lanes],
                        )
                        lowered[s, X * 16 : (X + 1) * 16, q * 128 : (q + 1) * 128] = block.astype(BF)
            turned = jnp.transpose(out_grad[0, s].astype(F32)).astype(BF)
            spread = nn(turned, spread_hot[...]).astype(BF)
            spread = jnp.concatenate([spread[:, t * 256 : (t + 1) * 256] for t in range(4)], axis=0)
            grown = nn(down_rows, spread)
            upper = jnp.concatenate(
                [
                    grown[tx * C : (tx + 1) * C, X * 64 : (X + 1) * 64]
                    for X in range(4)
                    for tx in range(2)
                ],
                axis=1,
            )
            grads = upper * sigmoid * (1.0 + preact * (1.0 - sigmoid)) * filled
            grads = grads.astype(BF)
            grad_preact[s] = grads
            shifted[0:C, base : base + 640] = jnp.concatenate([grads, wide], axis=1)
            shifted[C : 2 * C, base : base + 640] = jnp.concatenate([edge, grads, edge], axis=1)
            shifted[2 * C :, base : base + 640] = jnp.concatenate([wide, grads], axis=1)
        total[...] += nt(shifted[...], stack[p])
        return carry

    lax.fori_loop(0, SLOTS // 2, pair, 0)
    rows = lowered[...].reshape(SLOTS * 64, 512)
    coarse[...] = nt(rows, down_kernel[...]).astype(BF).reshape(coarse.shape)
    turned = jnp.transpose(out_grad[...].reshape(SLOTS * 64, C2).astype(F32)).astype(BF)
    grad_down = nn(turned, rows)
    for j in range(5):
        width = min(128, 576 - j * 128)
        sums[j * 192 : (j + 1) * 192, 0:width] = total[:, j * 128 : j * 128 + width].astype(BF)
    sums[4 * 192 : 5 * 192, 64:128] = jnp.zeros((192, 64), BF)
    for j in range(4):
        sums[960 + j * C2 : 960 + (j + 1) * C2] = grad_down[:, j * 128 : (j + 1) * 128].astype(BF)
    sums[1472:1536] = jnp.zeros((64, 128), BF)


def fold_kernel(
    sources,
    grad_preact,
    conv_back,
    inner_hot,
    cap_hot,
    side_hot,
    interior,
    grad_local,
    to_ahead,
    to_behind,
    to_ahead2,
    to_behind2,
    planes,
    stack,
    high,
    low,
    rims,
    grad_table,
    grad_table_high,
):
    rows = grad_preact[...].reshape(SLOTS * C, 512)
    for i in range(4):
        block = nn(rows[:, i * 128 : (i + 1) * 128], inner_hot[...])
        planes[:, i * 256 : (i + 1) * 256] = block.astype(BF)
    high[...] = jnp.zeros_like(high)

    def brick(s, carry):
        here = pl.ds(pl.multiple_of(s * C, C), C)
        for x in range(8):
            plane = planes[here, x * 128 : (x + 1) * 128]
            for k, shift in enumerate(SHIFTS):
                moved = plane if shift == 0 else pltpu.roll(plane, shift % 128, 1)
                stack[k * C : (k + 1) * C, x * 128 : (x + 1) * 128] = moved
        triple = nn(conv_back[...], stack[...])
        for x in range(10):
            value = None
            for o in range(3):
                if 0 <= x - o < 8:
                    part = triple[o * C : (o + 1) * C, (x - o) * 128 : (x - o + 1) * 128]
                    value = part if value is None else value + part
            top = value.astype(BF)
            high[here, x * 128 : (x + 1) * 128] = top
            low[here, x * 128 : (x + 1) * 128] = (value - top.astype(F32)).astype(BF)
        return carry

    lax.fori_loop(0, SLOTS, brick, 0)
    rims[:, 0:640] = nt(high[:, 0:128], cap_hot[...])
    rims[:, 640:1152] = nt(high[:, 128:1152], side_hot[...])
    rims[:, 1152:1792] = nt(high[:, 1152:1280], cap_hot[...])
    grad_table[...] = jnp.zeros_like(grad_table)
    grad_table_high[...] = jnp.zeros_like(grad_table_high)
    for s in range(SLOTS):
        for t in range(14):
            block = rims[s * C : (s + 1) * C, t * 128 : (t + 1) * 128]
            grad_table[sources[0, s, PLACES[2 * t]]] += block
            if PLACES[2 * t + 1] is not None:
                grad_table_high[sources[0, s, PLACES[2 * t + 1]]] += block
    turned = pltpu.roll(grad_table_high[...].reshape(TABLE * C, 128), 64, 1)
    grad_table[...] += turned.reshape(TABLE, C, 128)
    for i in range(4):
        lanes = slice(128 + i * 256, 384 + i * 256)
        interior[:, i * 128 : (i + 1) * 128] = nt(high[:, lanes], inner_hot[...]) + nt(
            low[:, lanes], inner_hot[...]
        )
    grad_local[...] = grad_table[0:LOCAL]
    for j in range(NOFF):
        block = grad_table[LOCAL + j * CAP : LOCAL + (j + 1) * CAP].astype(BF)
        (to_ahead, to_behind, to_ahead2, to_behind2)[j][...] = block


def unpack_kernel(sums, grad_kernel, grad_down):
    parts = []
    for o in range(3):
        tiles = [sums[j * 192 + o * C : j * 192 + (o + 1) * C].astype(F32) for j in range(5)]
        parts.append(jnp.concatenate(tiles, axis=1)[:, :576])
    grad_kernel[...] = jnp.concatenate(parts, axis=1)
    tiles = [sums[960 + t * C2 : 960 + (t + 1) * C2].astype(F32) for t in range(4)]
    grad_down[...] = jnp.concatenate(tiles, axis=1)


def finish_kernel(
    count,
    sends,
    interior,
    grad_local,
    ahead,
    behind,
    ahead2,
    behind2,
    face_hot,
    grad_features,
    table,
    layers,
):
    table[...] = grad_local[...]
    for j in range(NOFF):
        for c in range(CAP):
            block = (ahead, behind, ahead2, behind2)[j][c]
            table[sends[0, 0, j, c]] += block.astype(F32)
    for s in range(SLOTS):
        for f in range(6):
            layers[s * C : (s + 1) * C, f * 128 : (f + 1) * 128] = table[6 * s + f].astype(BF)
    whole = interior[...] + nt(layers[...], face_hot[...])
    for s in range(SLOTS):
        filled = jnp.where(s < count[0, 0], 1.0, 0.0).astype(F32)
        grad_features[0, s] = (whole[s * C : (s + 1) * C] * filled).astype(BF)


def call(kernel, limit, memories, outs, scratch, flops, *args):
    where = {"s": pltpu.SMEM, "v": pltpu.VMEM, "h": pltpu.HBM}
    return pl.pallas_call(
        kernel,
        in_specs=[pl.BlockSpec(memory_space=where[m]) for m in memories],
        out_specs=[pl.BlockSpec(memory_space=pltpu.VMEM) for _ in outs],
        out_shape=[jax.ShapeDtypeStruct(s, d) for s, d in outs],
        scratch_shapes=[pltpu.VMEM(*s) if isinstance(s, tuple) else s for s in scratch],
        compiler_params=pltpu.CompilerParams(vmem_limit_bytes=limit * 2**20),
        cost_estimate=pl.CostEstimate(flops=flops, bytes_accessed=2**20, transcendentals=0),
        name=kernel.__name__,
    )(*args)


def gather_sum(block, axes, parts):
    copies = jnp.broadcast_to(block[None], (parts,) + block.shape)
    got = lax.all_to_all(copies, axes, 0, 0)
    return got.astype(F32).sum(0)


def near_sum(block, sizes):
    parts = sizes["x"] * sizes["c"] * sizes["grp"]
    rows = block.shape[0] // parts
    got = lax.all_to_all(block.reshape(parts, rows, 128), NEAR, 0, 0)
    return got.astype(F32).sum(0).astype(BF)


def near_gather(block, sizes):
    parts = sizes["x"] * sizes["c"] * sizes["grp"]
    copies = jnp.broadcast_to(block[None], (parts,) + block.shape)
    return lax.all_to_all(copies, NEAR, 0, 0).reshape(parts * block.shape[0], 128)


def from_behind(block, axes, devices, distance):
    route = [(i - distance, i) for i in range(devices) if 0 <= i - distance < devices]
    return lax.ppermute(block, axes, route)


def on_device(sizes, features, brick_count, send_list, halo_src, kernel, down_kernel, out_grad):
    face_hot, inner_hot, cap_hot, side_hot, window_hot, spread_hot, pick_hot = one_hot_tables()
    tile = ("z", "x", "c")
    devices = sizes["z"] * sizes["x"] * sizes["c"]
    swap = [((CAP, C, 128), BF)] * NOFF

    table, *outgoing = call(
        faces_kernel,
        56,
        "shhh",
        [((LOCAL, C, 128), BF)] + swap,
        [
            pltpu.SMEM((1, 1, NOFF, CAP), jnp.int32),
            ((1, SLOTS, C, 512), BF),
            ((512, 768), BF),
            pltpu.SemaphoreType.DMA((3,)),
        ],
        2 * 256 * 512 * 768,
        brick_count,
        send_list,
        features,
        face_hot,
    )
    received = [from_behind(b, tile, devices, o) for b, o in zip(outgoing, OFFSETS)]
    coarse, grad_preact, sums, conv_back = call(
        main_kernel,
        28,
        "ss" + "v" * 15,
        [
            ((1, SLOTS, 64, C2), BF),
            ((SLOTS, C, 512), BF),
            ((1536, 128), BF),
            ((192, 576), BF),
        ],
        [
            ((TABLE, C, 128), BF),
            ((TABLE, C, 128), BF),
            ((192, 576), BF),
            ((256, 14 * 128), BF),
            ((256, 1280), BF),
            ((2, 576, 1280), BF),
            ((192, 1280), BF),
            ((SLOTS, 64, 512), BF),
            ((192, 576), F32),
        ],
        5 * 10**9,
        brick_count,
        halo_src,
        features,
        table,
        *received,
        kernel,
        down_kernel,
        out_grad,
        inner_hot,
        cap_hot,
        side_hot,
        window_hot,
        spread_hot,
        pick_hot,
    )
    part = near_sum(sums, sizes)
    interior, grad_local, *remote = call(
        fold_kernel,
        24,
        "svvvvv",
        [((256, 512), F32), ((LOCAL, C, 128), F32)] + swap,
        [
            ((256, 1024), BF),
            ((576, 1024), BF),
            ((256, 1280), BF),
            ((256, 1280), BF),
            ((256, 14 * 128), F32),
            ((TABLE, C, 128), F32),
            ((TABLE, C, 128), F32),
        ],
        3 * 10**9,
        halo_src,
        grad_preact,
        conv_back,
        inner_hot,
        cap_hot,
        side_hot,
    )
    part, *remote = lax.optimization_barrier((part, *remote))
    part = gather_sum(part, ("z",), sizes["z"])
    returned = [from_behind(b, tile, devices, -o) for b, o in zip(remote, OFFSETS)]
    part, *returned = lax.optimization_barrier((part, *returned))
    sums = near_gather(part.astype(BF), sizes)
    (grad_features,) = call(
        finish_kernel,
        12,
        "ss" + "v" * 7,
        [((1, SLOTS, C, 512), BF)],
        [((LOCAL, C, 128), F32), ((256, 768), BF)],
        2 * 256 * 512 * 768,
        brick_count,
        send_list,
        interior,
        grad_local,
        *returned,
        face_hot,
    )
    grad_kernel, grad_down = call(
        unpack_kernel, 8, "v", [((C, 1728), F32), ((C2, 512), F32)], [], 10**6, sums
    )
    return coarse, grad_features, grad_kernel, grad_down


def solution(mesh):
    tile, grp = mesh.shape["tile"], mesh.shape["grp"]
    sizes = {"z": tile // 8, "x": 4, "c": 2, "grp": grp}
    fine = Mesh(mesh.devices.reshape(tuple(sizes.values())), tuple(sizes))
    line = ("z", "x", "c")
    in_specs = (
        P("grp", line, None, None),
        P("grp", line),
        P("grp", line, None, None),
        P("grp", line, None),
        P(),
        P(),
        P("grp", line, None, None),
    )
    out_specs = (P("grp", line, None, None), P("grp", line, None, None), P(), P())

    def step(*args):
        return on_device(sizes, *args)

    return jax.shard_map(step, mesh=fine, in_specs=in_specs, out_specs=out_specs, check_vma=False)
```

```python
import jax
import jax.numpy as jnp
import ml_dtypes
import numpy as np
from jax import lax
from jax.experimental import pallas as pl
from jax.experimental.pallas import tpu as pltpu
from jax.sharding import Mesh
from jax.sharding import PartitionSpec as P

BF = jnp.bfloat16
F32 = jnp.float32
DIRECTIONS = [
    (a, b, c) for a in (-1, 0, 1) for b in (-1, 0, 1) for c in (-1, 0, 1) if (a, b, c) != (0, 0, 0)
]
SHIFTS = [10 * b + c for b in (-1, 0, 1) for c in (-1, 0, 1)]
SLOTS, C, C2, NOFF, CAP = 4, 64, 128, 4, 4
LOCAL = 6 * SLOTS + 1
TABLE = LOCAL + NOFF * CAP
PLACES = list(range(9)) + [None] + list(range(9, 26)) + [None]
OFFSETS = (1, -1, 2, -2)
NEAR = ("x", "c", "grp")


def rim_cells(d, full):
    if d == -1:
        return [(7, 0)]
    if d == 1:
        return [(0, 9)]
    return [(i, i + 1) for i in range(full)]


def one_hot_tables():
    faces = np.zeros((512, 6, 128), np.float32)
    for x in range(8):
        for y in range(8):
            for z in range(8):
                v = (x, y, z)
                for a in range(3):
                    p, q = [v[i] for i in range(3) if i != a]
                    for e in range(2):
                        if v[a] == 7 * e:
                            faces[x * 64 + y * 8 + z, 2 * a + e, p * 8 + q] = 1
    inner = np.zeros((2, 64, 2, 128), np.float32)
    for s in range(2):
        for y in range(8):
            for z in range(8):
                inner[s, y * 8 + z, s, (y + 1) * 10 + z + 1] = 1
    cap = np.zeros((10, 64, 128), np.float32)
    side = np.zeros((8, 64, 128), np.float32)
    for m, d in enumerate([d for d in DIRECTIONS if d[0] == 0]):
        if d[1] != 0:
            yy = 0 if d[1] == -1 else 9
            for x in range(8):
                for i, zz in rim_cells(d[2], 8):
                    side[m, x * 8 + i, yy * 10 + zz] = 1
        else:
            zz = 0 if d[2] == -1 else 9
            for x in range(8):
                for y in range(8):
                    side[m, x * 8 + y, (y + 1) * 10 + zz] = 1
    for m, (dy, dz) in enumerate([(b, c) for b in (-1, 0, 1) for c in (-1, 0, 1)]):
        for i, yy in rim_cells(dy, 8):
            for k, zz in rim_cells(dz, 8):
                cap[m, i * 8 + k, yy * 10 + zz] = 1
    window = np.zeros((2, 128, 9, 2, 64), np.float32)
    for k, shift in enumerate(SHIFTS):
        for y in range(8):
            for z in range(8):
                for p in range(2):
                    window[p, (y + 1) * 10 + z + 1 + shift, k, p, y * 8 + z] = 1
    spread = np.zeros((4, 4, 4, 2, 2, 4, 64), np.float32)
    pick = np.zeros((2, 2, 2, 4, 4, 2, 64), np.float32)
    for ty in range(2):
        for tz in range(2):
            for Y in range(4):
                for Z in range(4):
                    lane = (2 * Y + ty) * 8 + 2 * Z + tz
                    for X in range(4):
                        spread[X, Y, Z, ty, tz, X, lane] = 1
                    for tx in range(2):
                        pick[tx, ty, tz, Y, Z, tx, lane] = 1
    def stacked(table):
        rows, lanes = table.shape
        return table.reshape(rows, lanes // 128, 128).transpose(1, 0, 2).reshape(-1, 128)

    placing = np.concatenate(
        [
            cap.reshape(640, 128),
            side.reshape(512, 128),
            stacked(inner.reshape(128, 256)),
            pick.reshape(128, 128),
            stacked(spread.reshape(64, 1024)),
            stacked(window.reshape(256, 1152)),
        ]
    )
    b = ml_dtypes.bfloat16
    return faces.reshape(512, 768).astype(b), placing.astype(b)


CAP_ROWS, SIDE_ROWS, INNER_ROWS, PICK_ROWS, SPREAD_ROWS = 0, 640, 1152, 1408, 1536
WINDOW_ROWS, FOLD_ROWS, ALL_ROWS = 2048, 1408, 4352


def tiles_of(table, start, rows, first, count):
    blocks = [table[start + (first + i) * rows : start + (first + i + 1) * rows] for i in range(count)]
    return jnp.concatenate(blocks, axis=1)


def side_tiles(table, first, count):
    side = table[SIDE_ROWS : SIDE_ROWS + 512]
    plane = (lax.broadcasted_iota(jnp.int32, (512, 128), 0) // 8) % 8
    return jnp.concatenate(
        [jnp.where(plane == first + i, side, jnp.zeros_like(side)) for i in range(count)], axis=1
    )


def low_lanes(shape):
    return lax.broadcasted_iota(jnp.int32, shape, 1) < 64


def nn(a, b):
    return jnp.dot(a, b, preferred_element_type=F32)


def nt(a, b):
    return lax.dot_general(a, b, (((1,), (1,)), ((), ())), preferred_element_type=F32)


def masked_rows(features, count):
    return jnp.concatenate(
        [features[0, s] * jnp.where(s < count, 1.0, 0.0).astype(BF) for s in range(SLOTS)], axis=0
    )


def fetch(sources, targets, done):
    copies = [
        pltpu.make_async_copy(a, b, done.at[i]) for i, (a, b) in enumerate(zip(sources, targets))
    ]
    for copy in copies:
        copy.start()
    return copies


def wait(copies):
    for copy in copies:
        copy.wait()


def faces_kernel(
    count, sends_far, features_far, face_far, table, *rest
):
    outgoing, (sends, features, face_hot, done) = rest[:NOFF], rest[NOFF:]
    wait(fetch((features_far, face_far, sends_far), (features, face_hot, sends), done))
    masked = masked_rows(features, count[0, 0])
    for f in range(6):
        layer = nn(masked, face_hot[:, f * 128 : (f + 1) * 128]).astype(BF)
        for s in range(SLOTS):
            table[6 * s + f] = layer[s * C : (s + 1) * C]
    table[6 * SLOTS] = jnp.zeros((C, 128), BF)
    for j in range(NOFF):
        for q in range(CAP // 2):
            high = table[sends[0, 0, j, 2 * q + 1]]
            outgoing[j][q] = table[sends[0, 0, j, 2 * q]] + pltpu.roll(high, 64, 1)


def main_kernel(
    count,
    sources_far,
    table,
    ahead,
    behind,
    ahead2,
    behind2,
    features_far,
    placing_far,
    kernel_far,
    down_far,
    out_far,
    coarse,
    grad_preact,
    sums,
    conv_back,
    sources,
    arrived,
    features,
    placing,
    kernel,
    down_kernel,
    out_grad,
    halo,
    halo_high,
    conv,
    entries,
    padded,
    stack,
    shifted,
    lowered,
    total,
    done,
):
    copies = fetch(
        (ahead, behind, ahead2, behind2, table, sources_far)
        + (features_far, placing_far, kernel_far, down_far, out_far),
        [arrived.at[j] for j in range(NOFF)]
        + [halo.at[0:LOCAL], sources, features, placing, kernel, down_kernel, out_grad],
        done,
    )
    wait(copies[: NOFF + 2])
    low = low_lanes((C, 128))
    none = jnp.zeros((C, 128), BF)
    halo_high[0:LOCAL] = pltpu.roll(
        halo[0:LOCAL].reshape(LOCAL * C, 128), 64, 1
    ).reshape(LOCAL, C, 128)
    for j in range(NOFF):
        for q in range(CAP // 2):
            block, place = arrived[j, q], LOCAL + j * CAP + 2 * q
            turned = pltpu.roll(block, 64, 1)
            halo[place] = jnp.where(low, block, none)
            halo[place + 1] = jnp.where(low, turned, none)
            halo_high[place] = jnp.where(low, none, turned)
            halo_high[place + 1] = jnp.where(low, none, block)
    for s in range(SLOTS):
        for t in range(14):
            even, odd = PLACES[2 * t], PLACES[2 * t + 1]
            block = halo[sources[0, s, even]]
            if odd is not None:
                block = block + halo_high[sources[0, s, odd]]
            entries[s * C : (s + 1) * C, t * 128 : (t + 1) * 128] = block
    wait(copies[NOFF + 2 :])
    cap_hot = placing[CAP_ROWS : CAP_ROWS + 640]
    inner_hot = tiles_of(placing, INNER_ROWS, 128, 0, 2)
    pick_hot = placing[PICK_ROWS : PICK_ROWS + 128]
    masked = masked_rows(features, count[0, 0])
    padded[:, 0:128] = nn(entries[:, 0:640], cap_hot).astype(BF)
    padded[:, 1152:1280] = nn(entries[:, 1152:1792], cap_hot).astype(BF)
    for i in range(4):
        block = nn(entries[:, 640:1152], side_tiles(placing, 2 * i, 2))
        block = block + nn(masked[:, i * 128 : (i + 1) * 128], inner_hot)
        padded[:, 128 + i * 256 : 384 + i * 256] = block.astype(BF)
    window_hot = tiles_of(placing, WINDOW_ROWS, 256, 0, 9)
    for i in range(5):
        planes = nn(padded[:, i * 256 : (i + 1) * 256], window_hot).astype(BF)
        for s in range(SLOTS):
            lanes = slice((s % 2) * 640 + i * 128, (s % 2) * 640 + (i + 1) * 128)
            for k in range(9):
                block = planes[s * C : (s + 1) * C, k * 128 : (k + 1) * 128]
                stack[s // 2, k * C : (k + 1) * C, lanes] = block

    for o in range(3):
        conv[o * C : (o + 1) * C] = kernel[:, o * 576 : (o + 1) * 576]
    tall = jnp.transpose(kernel[...].astype(F32)).astype(BF)
    for o in range(3):
        conv_back[o * C : (o + 1) * C] = jnp.concatenate(
            [tall[(9 * o + k) * C : (9 * o + k + 1) * C] for k in range(9)], axis=1
        )
    tall = jnp.transpose(down_kernel[...].astype(F32)).astype(BF)
    down_rows = jnp.concatenate(
        [
            jnp.concatenate([tall[(4 * tx + t) * C : (4 * tx + t + 1) * C] for t in range(4)], axis=1)
            for tx in range(2)
        ],
        axis=0,
    )
    left = low_lanes((16, 128))
    edge = jnp.zeros((C, 64), BF)
    wide = jnp.zeros((C, 128), BF)
    total[...] = jnp.zeros_like(total)

    def pair(p, carry):
        triple = nn(conv[...], stack[p])
        for j in range(2):
            s = 2 * p + j
            filled = jnp.where(s < count[0, 0], 1.0, 0.0).astype(F32)
            base = j * 640
            preact = (
                triple[0:C, base : base + 512]
                + triple[C : 2 * C, base + 64 : base + 576]
                + triple[2 * C :, base + 128 : base + 640]
            )
            sigmoid = jax.nn.sigmoid(preact)
            active = (preact * sigmoid * filled).astype(BF)
            for h in range(2):
                halves = [active[:, (2 * h + i) * 128 : (2 * h + i + 1) * 128] for i in range(2)]
                rows = jnp.concatenate([halves[0], halves[0], halves[1], halves[1]], axis=0)
                picked = nt(pick_hot, rows)
                for i in range(2):
                    X = 2 * h + i
                    for q in range(4):
                        lanes = slice(i * 128, (i + 1) * 128)
                        block = jnp.where(
                            left,
                            picked[32 * q : 32 * q + 16, lanes],
                            picked[32 * q + 16 : 32 * q + 32, lanes],
                        )
                        lowered[s, X * 16 : (X + 1) * 16, q * 128 : (q + 1) * 128] = block.astype(BF)
            turned = jnp.transpose(out_grad[0, s].astype(F32)).astype(BF)
            spread = nn(turned, tiles_of(placing, SPREAD_ROWS, 64, 0, 8)).astype(BF)
            spread = jnp.concatenate([spread[:, t * 256 : (t + 1) * 256] for t in range(4)], axis=0)
            grown = nn(down_rows, spread)
            upper = jnp.concatenate(
                [
                    grown[tx * C : (tx + 1) * C, X * 64 : (X + 1) * 64]
                    for X in range(4)
                    for tx in range(2)
                ],
                axis=1,
            )
            grads = upper * sigmoid * (1.0 + preact * (1.0 - sigmoid)) * filled
            grads = grads.astype(BF)
            grad_preact[s] = grads
            shifted[0:C, base : base + 640] = jnp.concatenate([grads, wide], axis=1)
            shifted[C : 2 * C, base : base + 640] = jnp.concatenate([edge, grads, edge], axis=1)
            shifted[2 * C :, base : base + 640] = jnp.concatenate([wide, grads], axis=1)
        total[...] += nt(shifted[...], stack[p])
        return carry

    lax.fori_loop(0, SLOTS // 2, pair, 0)
    rows = lowered[...].reshape(SLOTS * 64, 512)
    coarse[...] = nt(rows, down_kernel[...]).astype(BF).reshape(coarse.shape)
    turned = jnp.transpose(out_grad[...].reshape(SLOTS * 64, C2).astype(F32)).astype(BF)
    grad_down = nn(turned, rows)
    for j in range(5):
        width = min(128, 576 - j * 128)
        sums[j * 192 : (j + 1) * 192, 0:width] = total[:, j * 128 : j * 128 + width].astype(BF)
    sums[4 * 192 : 5 * 192, 64:128] = jnp.zeros((192, 64), BF)
    for j in range(4):
        sums[960 + j * C2 : 960 + (j + 1) * C2] = grad_down[:, j * 128 : (j + 1) * 128].astype(BF)
    sums[1472:1536] = jnp.zeros((64, 128), BF)


def fold_kernel(
    sources,
    grads_far,
    conv_far,
    placing_far,
    interior,
    grad_local,
    to_ahead,
    to_behind,
    to_ahead2,
    to_behind2,
    grad_preact,
    conv_back,
    placing,
    planes,
    stack,
    high,
    low,
    rims,
    grad_table,
    grad_table_high,
    done,
):
    copies = fetch(
        (grads_far, conv_far, placing_far.at[0:FOLD_ROWS]), (grad_preact, conv_back, placing), done
    )
    grad_table[...] = jnp.zeros_like(grad_table)
    grad_table_high[...] = jnp.zeros_like(grad_table_high)
    wait(copies)
    cap_hot = placing[CAP_ROWS : CAP_ROWS + 640]
    inner_hot = tiles_of(placing, INNER_ROWS, 128, 0, 2)
    rows = grad_preact[...].reshape(SLOTS * C, 512)
    for i in range(4):
        block = nn(rows[:, i * 128 : (i + 1) * 128], inner_hot)
        planes[:, i * 256 : (i + 1) * 256] = block.astype(BF)
    high[...] = jnp.zeros_like(high)

    def brick(s, carry):
        here = pl.ds(pl.multiple_of(s * C, C), C)
        for x in range(8):
            plane = planes[here, x * 128 : (x + 1) * 128]
            for k, shift in enumerate(SHIFTS):
                moved = plane if shift == 0 else pltpu.roll(plane, shift % 128, 1)
                stack[k * C : (k + 1) * C, x * 128 : (x + 1) * 128] = moved
        triple = nn(conv_back[...], stack[...])
        for x in range(10):
            value = None
            for o in range(3):
                if 0 <= x - o < 8:
                    part = triple[o * C : (o + 1) * C, (x - o) * 128 : (x - o + 1) * 128]
                    value = part if value is None else value + part
            top = value.astype(BF)
            high[here, x * 128 : (x + 1) * 128] = top
            low[here, x * 128 : (x + 1) * 128] = (value - top.astype(F32)).astype(BF)
        return carry

    lax.fori_loop(0, SLOTS, brick, 0)
    rims[:, 0:640] = nt(high[:, 0:128], cap_hot)
    rims[:, 640:1152] = nt(high[:, 128:1152], side_tiles(placing, 0, 8))
    rims[:, 1152:1792] = nt(high[:, 1152:1280], cap_hot)
    for s in range(SLOTS):
        for t in range(14):
            block = rims[s * C : (s + 1) * C, t * 128 : (t + 1) * 128]
            grad_table[sources[0, s, PLACES[2 * t]]] += block
            if PLACES[2 * t + 1] is not None:
                grad_table_high[sources[0, s, PLACES[2 * t + 1]]] += block
    turned = pltpu.roll(grad_table_high[...].reshape(TABLE * C, 128), 64, 1)
    grad_table[...] += turned.reshape(TABLE, C, 128)
    for i in range(4):
        lanes = slice(128 + i * 256, 384 + i * 256)
        interior[:, i * 128 : (i + 1) * 128] = nt(high[:, lanes], inner_hot) + nt(
            low[:, lanes], inner_hot
        )
    grad_local[...] = grad_table[0:LOCAL]
    left = low_lanes((C, 128))
    for j in range(NOFF):
        for q in range(CAP // 2):
            place = LOCAL + j * CAP + 2 * q
            block = jnp.where(left, grad_table[place], pltpu.roll(grad_table[place + 1], 64, 1))
            (to_ahead, to_behind, to_ahead2, to_behind2)[j][q] = block.astype(BF)


def unpack_kernel(sums, grad_kernel, grad_down):
    parts = []
    for o in range(3):
        tiles = [sums[j * 192 + o * C : j * 192 + (o + 1) * C].astype(F32) for j in range(5)]
        parts.append(jnp.concatenate(tiles, axis=1)[:, :576])
    grad_kernel[...] = jnp.concatenate(parts, axis=1)
    tiles = [sums[960 + t * C2 : 960 + (t + 1) * C2].astype(F32) for t in range(4)]
    grad_down[...] = jnp.concatenate(tiles, axis=1)


def finish_kernel(
    count,
    sends,
    interior,
    grad_local,
    ahead,
    behind,
    ahead2,
    behind2,
    face_hot,
    grad_features,
    table,
    layers,
):
    table[...] = grad_local[...]
    for j in range(NOFF):
        for q in range(CAP // 2):
            block = (ahead, behind, ahead2, behind2)[j][q].astype(F32)
            table[sends[0, 0, j, 2 * q]] += block
            table[sends[0, 0, j, 2 * q + 1]] += pltpu.roll(block, 64, 1)
    for s in range(SLOTS):
        for f in range(6):
            layers[s * C : (s + 1) * C, f * 128 : (f + 1) * 128] = table[6 * s + f].astype(BF)
    whole = interior[...] + nt(layers[...], face_hot[...])
    for s in range(SLOTS):
        filled = jnp.where(s < count[0, 0], 1.0, 0.0).astype(F32)
        grad_features[0, s] = (whole[s * C : (s + 1) * C] * filled).astype(BF)


def call(kernel, limit, memories, outs, scratch, flops, *args):
    where = {"s": pltpu.SMEM, "v": pltpu.VMEM, "h": pltpu.HBM}
    return pl.pallas_call(
        kernel,
        in_specs=[pl.BlockSpec(memory_space=where[m]) for m in memories],
        out_specs=[pl.BlockSpec(memory_space=pltpu.VMEM) for _ in outs],
        out_shape=[jax.ShapeDtypeStruct(s, d) for s, d in outs],
        scratch_shapes=[pltpu.VMEM(*s) if isinstance(s, tuple) else s for s in scratch],
        compiler_params=pltpu.CompilerParams(vmem_limit_bytes=int(limit * 2**20)),
        cost_estimate=pl.CostEstimate(flops=flops, bytes_accessed=2**20, transcendentals=0),
        name=kernel.__name__,
    )(*args)


def gather_sum(block, axes, parts):
    copies = jnp.broadcast_to(block[None], (parts,) + block.shape)
    got = lax.all_to_all(copies, axes, 0, 0)
    return got.astype(F32).sum(0)


def near_sum(block, sizes):
    parts = sizes["x"] * sizes["c"] * sizes["grp"]
    rows = block.shape[0] // parts
    got = lax.all_to_all(block.reshape(parts, rows, 128), NEAR, 0, 0)
    return got.astype(F32).sum(0).astype(BF)


def near_gather(block, sizes):
    parts = sizes["x"] * sizes["c"] * sizes["grp"]
    copies = jnp.broadcast_to(block[None], (parts,) + block.shape)
    return lax.all_to_all(copies, NEAR, 0, 0).reshape(parts * block.shape[0], 128)


def from_behind(block, axes, devices, distance):
    route = [(i - distance, i) for i in range(devices) if 0 <= i - distance < devices]
    return lax.ppermute(block, axes, route)


def on_device(sizes, features, brick_count, send_list, halo_src, kernel, down_kernel, out_grad):
    face_hot, placing = one_hot_tables()
    tile = ("z", "x", "c")
    devices = sizes["z"] * sizes["x"] * sizes["c"]
    swap = [((CAP // 2, C, 128), BF)] * NOFF

    table, *outgoing = call(
        faces_kernel,
        56,
        "shhh",
        [((LOCAL, C, 128), BF)] + swap,
        [
            pltpu.SMEM((1, 1, NOFF, CAP), jnp.int32),
            ((1, SLOTS, C, 512), BF),
            ((512, 768), BF),
            pltpu.SemaphoreType.DMA((3,)),
        ],
        2 * 256 * 512 * 768,
        brick_count,
        send_list,
        features,
        face_hot,
    )
    received = [from_behind(b, tile, devices, o) for b, o in zip(outgoing, OFFSETS)]
    coarse, grad_preact, sums, conv_back = call(
        main_kernel,
        53.8,
        "s" + "h" * 11,
        [
            ((1, SLOTS, 64, C2), BF),
            ((SLOTS, C, 512), BF),
            ((1536, 128), BF),
            ((192, 576), BF),
        ],
        [
            pltpu.SMEM((1, SLOTS, 26), jnp.int32),
            ((NOFF, CAP // 2, C, 128), BF),
            ((1, SLOTS, C, 512), BF),
            ((ALL_ROWS, 128), BF),
            ((C, 1728), BF),
            ((C2, 512), BF),
            ((1, SLOTS, 64, C2), BF),
            ((TABLE, C, 128), BF),
            ((TABLE, C, 128), BF),
            ((192, 576), BF),
            ((256, 14 * 128), BF),
            ((256, 1280), BF),
            ((2, 576, 1280), BF),
            ((192, 1280), BF),
            ((SLOTS, 64, 512), BF),
            ((192, 576), F32),
            pltpu.SemaphoreType.DMA((11,)),
        ],
        5 * 10**9,
        brick_count,
        halo_src,
        table,
        *received,
        features,
        placing,
        kernel,
        down_kernel,
        out_grad,
    )
    part = near_sum(sums, sizes)
    interior, grad_local, *remote = call(
        fold_kernel,
        56,
        "shhh",
        [((256, 512), F32), ((LOCAL, C, 128), F32)] + swap,
        [
            ((SLOTS, C, 512), BF),
            ((192, 576), BF),
            ((FOLD_ROWS, 128), BF),
            ((256, 1024), BF),
            ((576, 1024), BF),
            ((256, 1280), BF),
            ((256, 1280), BF),
            ((256, 14 * 128), F32),
            ((TABLE, C, 128), F32),
            ((TABLE, C, 128), F32),
            pltpu.SemaphoreType.DMA((3,)),
        ],
        3 * 10**9,
        halo_src,
        grad_preact,
        conv_back,
        placing,
    )
    part, *remote = lax.optimization_barrier((part, *remote))
    part = gather_sum(part, ("z",), sizes["z"])
    returned = [from_behind(b, tile, devices, -o) for b, o in zip(remote, OFFSETS)]
    part, *returned = lax.optimization_barrier((part, *returned))
    sums = near_gather(part.astype(BF), sizes)
    (grad_features,) = call(
        finish_kernel,
        12,
        "ss" + "v" * 7,
        [((1, SLOTS, C, 512), BF)],
        [((LOCAL, C, 128), F32), ((256, 768), BF)],
        2 * 256 * 512 * 768,
        brick_count,
        send_list,
        interior,
        grad_local,
        *returned,
        face_hot,
    )
    grad_kernel, grad_down = call(
        unpack_kernel, 8, "v", [((C, 1728), F32), ((C2, 512), F32)], [], 10**6, sums
    )
    return coarse, grad_features, grad_kernel, grad_down


def solution(mesh):
    tile, grp = mesh.shape["tile"], mesh.shape["grp"]
    sizes = {"z": tile // 8, "x": 4, "c": 2, "grp": grp}
    fine = Mesh(mesh.devices.reshape(tuple(sizes.values())), tuple(sizes))
    line = ("z", "x", "c")
    in_specs = (
        P("grp", line, None, None),
        P("grp", line),
        P("grp", line, None, None),
        P("grp", line, None),
        P(),
        P(),
        P("grp", line, None, None),
    )
    out_specs = (P("grp", line, None, None), P("grp", line, None, None), P(), P())

    def step(*args):
        return on_device(sizes, *args)

    return jax.shard_map(step, mesh=fine, in_specs=in_specs, out_specs=out_specs, check_vma=False)
```

```python
import jax
import jax.numpy as jnp
import ml_dtypes
import numpy as np
from jax import lax
from jax.experimental import pallas as pl
from jax.experimental.pallas import tpu as pltpu
from jax.sharding import Mesh
from jax.sharding import PartitionSpec as P

BF = jnp.bfloat16
F32 = jnp.float32
DIRECTIONS = [
    (a, b, c) for a in (-1, 0, 1) for b in (-1, 0, 1) for c in (-1, 0, 1) if (a, b, c) != (0, 0, 0)
]
SHIFTS = [10 * b + c for b in (-1, 0, 1) for c in (-1, 0, 1)]
SLOTS, C, C2, NOFF, CAP = 4, 64, 128, 4, 4
LOCAL = 6 * SLOTS + 1
TABLE = LOCAL + NOFF * CAP
PLACES = list(range(9)) + [None] + list(range(9, 26)) + [None]
OFFSETS = (1, -1, 2, -2)
NEAR = ("x", "c", "grp")


def rim_cells(d, full):
    if d == -1:
        return [(7, 0)]
    if d == 1:
        return [(0, 9)]
    return [(i, i + 1) for i in range(full)]


def one_hot_tables():
    faces = np.zeros((512, 6, 128), np.float32)
    for x in range(8):
        for y in range(8):
            for z in range(8):
                v = (x, y, z)
                for a in range(3):
                    p, q = [v[i] for i in range(3) if i != a]
                    for e in range(2):
                        if v[a] == 7 * e:
                            faces[x * 64 + y * 8 + z, 2 * a + e, p * 8 + q] = 1
    inner = np.zeros((2, 64, 2, 128), np.float32)
    for s in range(2):
        for y in range(8):
            for z in range(8):
                inner[s, y * 8 + z, s, (y + 1) * 10 + z + 1] = 1
    cap = np.zeros((10, 64, 128), np.float32)
    side = np.zeros((8, 64, 128), np.float32)
    for m, d in enumerate([d for d in DIRECTIONS if d[0] == 0]):
        if d[1] != 0:
            yy = 0 if d[1] == -1 else 9
            for x in range(8):
                for i, zz in rim_cells(d[2], 8):
                    side[m, x * 8 + i, yy * 10 + zz] = 1
        else:
            zz = 0 if d[2] == -1 else 9
            for x in range(8):
                for y in range(8):
                    side[m, x * 8 + y, (y + 1) * 10 + zz] = 1
    for m, (dy, dz) in enumerate([(b, c) for b in (-1, 0, 1) for c in (-1, 0, 1)]):
        for i, yy in rim_cells(dy, 8):
            for k, zz in rim_cells(dz, 8):
                cap[m, i * 8 + k, yy * 10 + zz] = 1
    window = np.zeros((2, 128, 9, 2, 64), np.float32)
    for k, shift in enumerate(SHIFTS):
        for y in range(8):
            for z in range(8):
                for p in range(2):
                    window[p, (y + 1) * 10 + z + 1 + shift, k, p, y * 8 + z] = 1
    spread = np.zeros((4, 4, 4, 2, 2, 4, 64), np.float32)
    pick = np.zeros((2, 2, 2, 4, 4, 2, 64), np.float32)
    for ty in range(2):
        for tz in range(2):
            for Y in range(4):
                for Z in range(4):
                    lane = (2 * Y + ty) * 8 + 2 * Z + tz
                    for X in range(4):
                        spread[X, Y, Z, ty, tz, X, lane] = 1
                    for tx in range(2):
                        pick[tx, ty, tz, Y, Z, tx, lane] = 1
    def stacked(table):
        rows, lanes = table.shape
        return table.reshape(rows, lanes // 128, 128).transpose(1, 0, 2).reshape(-1, 128)

    placing = np.concatenate(
        [
            cap.reshape(640, 128),
            side.reshape(512, 128),
            stacked(inner.reshape(128, 256)),
            pick.reshape(128, 128),
            stacked(spread.reshape(64, 1024)),
            stacked(window.reshape(256, 1152)),
        ]
    )
    b = ml_dtypes.bfloat16
    packed = faces[:, 2:, :64].reshape(512, 256)
    inner = inner.reshape(128, 256)
    return packed.astype(b), faces.reshape(512, 768).astype(b), inner.astype(b), placing.astype(b)


CAP_ROWS, SIDE_ROWS, INNER_ROWS, PICK_ROWS, SPREAD_ROWS = 0, 640, 1152, 1408, 1536
WINDOW_ROWS, FOLD_ROWS, ALL_ROWS = 2048, 1408, 4352


def tiles_of(table, start, rows, first, count):
    blocks = [table[start + (first + i) * rows : start + (first + i + 1) * rows] for i in range(count)]
    return jnp.concatenate(blocks, axis=1)


def side_tiles(table, first, count):
    side = table[SIDE_ROWS : SIDE_ROWS + 512]
    plane = (lax.broadcasted_iota(jnp.int32, (512, 128), 0) // 8) % 8
    return jnp.concatenate(
        [jnp.where(plane == first + i, side, jnp.zeros_like(side)) for i in range(count)], axis=1
    )


def low_lanes(shape):
    return lax.broadcasted_iota(jnp.int32, shape, 1) < 64


def nn(a, b):
    return jnp.dot(a, b, preferred_element_type=F32)


def nt(a, b):
    return lax.dot_general(a, b, (((1,), (1,)), ((), ())), preferred_element_type=F32)


def masked_rows(features, count):
    return jnp.concatenate(
        [features[0, s] * jnp.where(s < count, 1.0, 0.0).astype(BF) for s in range(SLOTS)], axis=0
    )


def fetch(sources, targets, done):
    copies = [
        pltpu.make_async_copy(a, b, done.at[i]) for i, (a, b) in enumerate(zip(sources, targets))
    ]
    for copy in copies:
        copy.start()
    return copies


def wait(copies):
    for copy in copies:
        copy.wait()


def faces_kernel(
    count, sends_far, features_far, face_far, table, *rest
):
    outgoing, (sends, features, face_hot, done) = rest[:NOFF], rest[NOFF:]
    wait(fetch((features_far, face_far, sends_far), (features, face_hot, sends), done))
    masked = masked_rows(features, count[0, 0])
    low = low_lanes((SLOTS * C, 128))
    none = jnp.zeros((SLOTS * C, 128), BF)
    found = nn(masked, face_hot[...]).astype(BF)
    pairs = (found[:, 0:128], found[:, 128:256])
    layers = [masked[:, 0:128], pltpu.roll(masked[:, 384:512], 64, 1)]
    for block in pairs:
        layers += [block, pltpu.roll(block, 64, 1)]
    for f in range(6):
        layer = jnp.where(low, layers[f], none)
        for s in range(SLOTS):
            table[6 * s + f] = layer[s * C : (s + 1) * C]
    table[6 * SLOTS] = jnp.zeros((C, 128), BF)
    for j in range(NOFF):
        for q in range(CAP // 2):
            high = table[sends[0, 0, j, 2 * q + 1]]
            outgoing[j][q] = table[sends[0, 0, j, 2 * q]] + pltpu.roll(high, 64, 1)


def main_kernel(
    count,
    sources_far,
    table,
    ahead,
    behind,
    ahead2,
    behind2,
    features_far,
    placing_far,
    kernel_far,
    down_far,
    out_far,
    coarse,
    grad_preact,
    sums,
    conv_back,
    sources,
    arrived,
    features,
    placing,
    kernel,
    down_kernel,
    out_grad,
    halo,
    halo_high,
    conv,
    entries,
    padded,
    stack,
    shifted,
    lowered,
    total,
    done,
):
    copies = fetch(
        (ahead, behind, ahead2, behind2, table, sources_far)
        + (features_far, placing_far, kernel_far, down_far, out_far),
        [arrived.at[j] for j in range(NOFF)]
        + [halo.at[0:LOCAL], sources, features, placing, kernel, down_kernel, out_grad],
        done,
    )
    wait(copies[: NOFF + 2])
    low = low_lanes((C, 128))
    none = jnp.zeros((C, 128), BF)
    halo_high[0:LOCAL] = pltpu.roll(
        halo[0:LOCAL].reshape(LOCAL * C, 128), 64, 1
    ).reshape(LOCAL, C, 128)
    for j in range(NOFF):
        for q in range(CAP // 2):
            block, place = arrived[j, q], LOCAL + j * CAP + 2 * q
            turned = pltpu.roll(block, 64, 1)
            halo[place] = jnp.where(low, block, none)
            halo[place + 1] = jnp.where(low, turned, none)
            halo_high[place] = jnp.where(low, none, turned)
            halo_high[place + 1] = jnp.where(low, none, block)
    for s in range(SLOTS):
        for t in range(14):
            even, odd = PLACES[2 * t], PLACES[2 * t + 1]
            block = halo[sources[0, s, even]]
            if odd is not None:
                block = block + halo_high[sources[0, s, odd]]
            entries[s * C : (s + 1) * C, t * 128 : (t + 1) * 128] = block
    wait(copies[NOFF + 2 :])
    cap_hot = placing[CAP_ROWS : CAP_ROWS + 640]
    inner_hot = tiles_of(placing, INNER_ROWS, 128, 0, 2)
    pick_hot = placing[PICK_ROWS : PICK_ROWS + 128]
    masked = masked_rows(features, count[0, 0])
    padded[:, 0:128] = nn(entries[:, 0:640], cap_hot).astype(BF)
    padded[:, 1152:1280] = nn(entries[:, 1152:1792], cap_hot).astype(BF)
    for i in range(4):
        block = nn(entries[:, 640:1152], side_tiles(placing, 2 * i, 2))
        block = block + nn(masked[:, i * 128 : (i + 1) * 128], inner_hot)
        padded[:, 128 + i * 256 : 384 + i * 256] = block.astype(BF)
    window_hot = tiles_of(placing, WINDOW_ROWS, 256, 0, 9)
    for i in range(5):
        planes = nn(padded[:, i * 256 : (i + 1) * 256], window_hot).astype(BF)
        for s in range(SLOTS):
            lanes = slice((s % 2) * 640 + i * 128, (s % 2) * 640 + (i + 1) * 128)
            for k in range(9):
                block = planes[s * C : (s + 1) * C, k * 128 : (k + 1) * 128]
                stack[s // 2, k * C : (k + 1) * C, lanes] = block

    for o in range(3):
        conv[o * C : (o + 1) * C] = kernel[:, o * 576 : (o + 1) * 576]
    tall = jnp.transpose(kernel[...].astype(F32)).astype(BF)
    for o in range(3):
        conv_back[o * C : (o + 1) * C] = jnp.concatenate(
            [tall[(9 * o + k) * C : (9 * o + k + 1) * C] for k in range(9)], axis=1
        )
    tall = jnp.transpose(down_kernel[...].astype(F32)).astype(BF)
    down_rows = jnp.concatenate(
        [
            jnp.concatenate([tall[(4 * tx + t) * C : (4 * tx + t + 1) * C] for t in range(4)], axis=1)
            for tx in range(2)
        ],
        axis=0,
    )
    left = low_lanes((16, 128))
    edge = jnp.zeros((C, 64), BF)
    wide = jnp.zeros((C, 128), BF)
    total[...] = jnp.zeros_like(total)

    def pair(p, carry):
        triple = nn(conv[...], stack[p])
        for j in range(2):
            s = 2 * p + j
            filled = jnp.where(s < count[0, 0], 1.0, 0.0).astype(F32)
            base = j * 640
            preact = (
                triple[0:C, base : base + 512]
                + triple[C : 2 * C, base + 64 : base + 576]
                + triple[2 * C :, base + 128 : base + 640]
            )
            sigmoid = jax.nn.sigmoid(preact)
            active = (preact * sigmoid * filled).astype(BF)
            for h in range(2):
                halves = [active[:, (2 * h + i) * 128 : (2 * h + i + 1) * 128] for i in range(2)]
                rows = jnp.concatenate([halves[0], halves[0], halves[1], halves[1]], axis=0)
                picked = nt(pick_hot, rows)
                for i in range(2):
                    X = 2 * h + i
                    for q in range(4):
                        lanes = slice(i * 128, (i + 1) * 128)
                        block = jnp.where(
                            left,
                            picked[32 * q : 32 * q + 16, lanes],
                            picked[32 * q + 16 : 32 * q + 32, lanes],
                        )
                        lowered[s, X * 16 : (X + 1) * 16, q * 128 : (q + 1) * 128] = block.astype(BF)
            turned = jnp.transpose(out_grad[0, s].astype(F32)).astype(BF)
            spread = nn(turned, tiles_of(placing, SPREAD_ROWS, 64, 0, 8)).astype(BF)
            spread = jnp.concatenate([spread[:, t * 256 : (t + 1) * 256] for t in range(4)], axis=0)
            grown = nn(down_rows, spread)
            upper = jnp.concatenate(
                [
                    grown[tx * C : (tx + 1) * C, X * 64 : (X + 1) * 64]
                    for X in range(4)
                    for tx in range(2)
                ],
                axis=1,
            )
            grads = upper * sigmoid * (1.0 + preact * (1.0 - sigmoid)) * filled
            grads = grads.astype(BF)
            grad_preact[s] = grads
            shifted[0:C, base : base + 640] = jnp.concatenate([grads, wide], axis=1)
            shifted[C : 2 * C, base : base + 640] = jnp.concatenate([edge, grads, edge], axis=1)
            shifted[2 * C :, base : base + 640] = jnp.concatenate([wide, grads], axis=1)
        total[...] += nt(shifted[...], stack[p])
        return carry

    lax.fori_loop(0, SLOTS // 2, pair, 0)
    rows = lowered[...].reshape(SLOTS * 64, 512)
    coarse[...] = nt(rows, down_kernel[...]).astype(BF).reshape(coarse.shape)
    turned = jnp.transpose(out_grad[...].reshape(SLOTS * 64, C2).astype(F32)).astype(BF)
    grad_down = nn(turned, rows)
    for j in range(5):
        width = min(128, 576 - j * 128)
        sums[j * 192 : (j + 1) * 192, 0:width] = total[:, j * 128 : j * 128 + width].astype(BF)
    sums[4 * 192 : 5 * 192, 64:128] = jnp.zeros((192, 64), BF)
    for j in range(4):
        sums[960 + j * C2 : 960 + (j + 1) * C2] = grad_down[:, j * 128 : (j + 1) * 128].astype(BF)
    sums[1472:1536] = jnp.zeros((64, 128), BF)


def fold_kernel(
    sources,
    grads_far,
    conv_far,
    placing_far,
    folded,
    grad_local,
    to_ahead,
    to_behind,
    to_ahead2,
    to_behind2,
    grad_preact,
    conv_back,
    placing,
    planes,
    stack,
    high,
    rims,
    grad_table,
    grad_table_high,
    done,
):
    copies = fetch(
        (grads_far, placing_far.at[0:FOLD_ROWS], conv_far), (grad_preact, placing, conv_back), done
    )
    grad_table[...] = jnp.zeros_like(grad_table)
    grad_table_high[...] = jnp.zeros_like(grad_table_high)
    wait(copies[:2])
    cap_hot = placing[CAP_ROWS : CAP_ROWS + 640]
    inner_hot = tiles_of(placing, INNER_ROWS, 128, 0, 2)
    rows = grad_preact[...].reshape(SLOTS * C, 512)
    for i in range(4):
        block = nn(rows[:, i * 128 : (i + 1) * 128], inner_hot)
        planes[:, i * 256 : (i + 1) * 256] = block.astype(BF)
    wait(copies[2:])

    def brick(s, carry):
        here = pl.ds(pl.multiple_of(s * C, C), C)
        for x in range(8):
            plane = planes[here, x * 128 : (x + 1) * 128]
            for k, shift in enumerate(SHIFTS):
                moved = plane if shift == 0 else pltpu.roll(plane, shift % 128, 1)
                stack[k * C : (k + 1) * C, x * 128 : (x + 1) * 128] = moved
        triple = nn(conv_back[...], stack[...])
        for x in range(10):
            value = None
            for o in range(3):
                if 0 <= x - o < 8:
                    part = triple[o * C : (o + 1) * C, (x - o) * 128 : (x - o + 1) * 128]
                    value = part if value is None else value + part
            high[here, x * 128 : (x + 1) * 128] = value.astype(BF)
            if 1 <= x <= 8:
                folded[here, (x - 1) * 128 : x * 128] = value
        return carry

    lax.fori_loop(0, SLOTS, brick, 0)
    rims[:, 0:640] = nt(high[:, 0:128], cap_hot)
    rims[:, 640:1152] = nt(high[:, 128:1152], side_tiles(placing, 0, 8))
    rims[:, 1152:1792] = nt(high[:, 1152:1280], cap_hot)
    for s in range(SLOTS):
        for t in range(14):
            block = rims[s * C : (s + 1) * C, t * 128 : (t + 1) * 128]
            grad_table[sources[0, s, PLACES[2 * t]]] += block
            if PLACES[2 * t + 1] is not None:
                grad_table_high[sources[0, s, PLACES[2 * t + 1]]] += block
    turned = pltpu.roll(grad_table_high[...].reshape(TABLE * C, 128), 64, 1)
    grad_table[...] += turned.reshape(TABLE, C, 128)
    grad_local[...] = grad_table[0:LOCAL]
    left = low_lanes((C, 128))
    for j in range(NOFF):
        for q in range(CAP // 2):
            place = LOCAL + j * CAP + 2 * q
            block = jnp.where(left, grad_table[place], pltpu.roll(grad_table[place + 1], 64, 1))
            (to_ahead, to_behind, to_ahead2, to_behind2)[j][q] = block.astype(BF)


def unpack_kernel(sums, grad_kernel, grad_down):
    parts = []
    for o in range(3):
        tiles = [sums[j * 192 + o * C : j * 192 + (o + 1) * C].astype(F32) for j in range(5)]
        parts.append(jnp.concatenate(tiles, axis=1)[:, :576])
    grad_kernel[...] = jnp.concatenate(parts, axis=1)
    tiles = [sums[960 + t * C2 : 960 + (t + 1) * C2].astype(F32) for t in range(4)]
    grad_down[...] = jnp.concatenate(tiles, axis=1)


def finish_kernel(
    count,
    sends,
    folded,
    grad_local,
    ahead,
    behind,
    ahead2,
    behind2,
    face_hot,
    inner_hot,
    grad_features,
    table,
    layers,
):
    table[...] = grad_local[...]
    for j in range(NOFF):
        for q in range(CAP // 2):
            block = (ahead, behind, ahead2, behind2)[j][q].astype(F32)
            table[sends[0, 0, j, 2 * q]] += block
            table[sends[0, 0, j, 2 * q + 1]] += pltpu.roll(block, 64, 1)
    for s in range(SLOTS):
        for f in range(6):
            layers[s * C : (s + 1) * C, f * 128 : (f + 1) * 128] = table[6 * s + f].astype(BF)
    tiles = []
    for i in range(4):
        value = folded[:, i * 256 : (i + 1) * 256]
        top = value.astype(BF)
        rest = (value - top.astype(F32)).astype(BF)
        tiles.append(nt(top, inner_hot[...]) + nt(rest, inner_hot[...]))
    whole = jnp.concatenate(tiles, axis=1) + nt(layers[...], face_hot[...])
    for s in range(SLOTS):
        filled = jnp.where(s < count[0, 0], 1.0, 0.0).astype(F32)
        grad_features[0, s] = (whole[s * C : (s + 1) * C] * filled).astype(BF)


def call(kernel, limit, memories, outs, scratch, flops, *args):
    where = {"s": pltpu.SMEM, "v": pltpu.VMEM, "h": pltpu.HBM}
    return pl.pallas_call(
        kernel,
        in_specs=[pl.BlockSpec(memory_space=where[m]) for m in memories],
        out_specs=[pl.BlockSpec(memory_space=pltpu.VMEM) for _ in outs],
        out_shape=[jax.ShapeDtypeStruct(s, d) for s, d in outs],
        scratch_shapes=[pltpu.VMEM(*s) if isinstance(s, tuple) else s for s in scratch],
        compiler_params=pltpu.CompilerParams(vmem_limit_bytes=int(limit * 2**20)),
        cost_estimate=pl.CostEstimate(flops=flops, bytes_accessed=2**20, transcendentals=0),
        name=kernel.__name__,
    )(*args)


def gather_sum(block, axes, parts):
    copies = jnp.broadcast_to(block[None], (parts,) + block.shape)
    got = lax.all_to_all(copies, axes, 0, 0)
    return got.astype(F32).sum(0)


def near_sum(block, sizes):
    parts = sizes["x"] * sizes["c"] * sizes["grp"]
    rows = block.shape[0] // parts
    got = lax.all_to_all(block.reshape(parts, rows, 128), NEAR, 0, 0)
    return got.astype(F32).sum(0).astype(BF)


def near_gather(block, sizes):
    parts = sizes["x"] * sizes["c"] * sizes["grp"]
    copies = jnp.broadcast_to(block[None], (parts,) + block.shape)
    return lax.all_to_all(copies, NEAR, 0, 0).reshape(parts * block.shape[0], 128)


def from_behind(block, axes, devices, distance):
    route = [(i - distance, i) for i in range(devices) if 0 <= i - distance < devices]
    return lax.ppermute(block, axes, route)


def on_device(sizes, features, brick_count, send_list, halo_src, kernel, down_kernel, out_grad):
    face_packed, face_hot, inner_hot, placing = one_hot_tables()
    tile = ("z", "x", "c")
    devices = sizes["z"] * sizes["x"] * sizes["c"]
    swap = [((CAP // 2, C, 128), BF)] * NOFF

    table, *outgoing = call(
        faces_kernel,
        56,
        "shhh",
        [((LOCAL, C, 128), BF)] + swap,
        [
            pltpu.SMEM((1, 1, NOFF, CAP), jnp.int32),
            ((1, SLOTS, C, 512), BF),
            ((512, 256), BF),
            pltpu.SemaphoreType.DMA((3,)),
        ],
        2 * 256 * 512 * 768,
        brick_count,
        send_list,
        features,
        face_packed,
    )
    received = [from_behind(b, tile, devices, o) for b, o in zip(outgoing, OFFSETS)]
    coarse, grad_preact, sums, conv_back = call(
        main_kernel,
        53.8,
        "s" + "h" * 11,
        [
            ((1, SLOTS, 64, C2), BF),
            ((SLOTS, C, 512), BF),
            ((1536, 128), BF),
            ((192, 576), BF),
        ],
        [
            pltpu.SMEM((1, SLOTS, 26), jnp.int32),
            ((NOFF, CAP // 2, C, 128), BF),
            ((1, SLOTS, C, 512), BF),
            ((ALL_ROWS, 128), BF),
            ((C, 1728), BF),
            ((C2, 512), BF),
            ((1, SLOTS, 64, C2), BF),
            ((TABLE, C, 128), BF),
            ((TABLE, C, 128), BF),
            ((192, 576), BF),
            ((256, 14 * 128), BF),
            ((256, 1280), BF),
            ((2, 576, 1280), BF),
            ((192, 1280), BF),
            ((SLOTS, 64, 512), BF),
            ((192, 576), F32),
            pltpu.SemaphoreType.DMA((11,)),
        ],
        5 * 10**9,
        brick_count,
        halo_src,
        table,
        *received,
        features,
        placing,
        kernel,
        down_kernel,
        out_grad,
    )
    part = near_sum(sums, sizes)
    folded, grad_local, *remote = call(
        fold_kernel,
        56,
        "shhh",
        [((256, 1024), F32), ((LOCAL, C, 128), F32)] + swap,
        [
            ((SLOTS, C, 512), BF),
            ((192, 576), BF),
            ((FOLD_ROWS, 128), BF),
            ((256, 1024), BF),
            ((576, 1024), BF),
            ((256, 1280), BF),
            ((256, 14 * 128), F32),
            ((TABLE, C, 128), F32),
            ((TABLE, C, 128), F32),
            pltpu.SemaphoreType.DMA((3,)),
        ],
        3 * 10**9,
        halo_src,
        grad_preact,
        conv_back,
        placing,
    )
    part, *remote = lax.optimization_barrier((part, *remote))
    part = gather_sum(part, ("z",), sizes["z"])
    returned = [from_behind(b, tile, devices, -o) for b, o in zip(remote, OFFSETS)]
    part, *returned = lax.optimization_barrier((part, *returned))
    sums = near_gather(part.astype(BF), sizes)
    (grad_features,) = call(
        finish_kernel,
        12,
        "ss" + "v" * 8,
        [((1, SLOTS, C, 512), BF)],
        [((LOCAL, C, 128), F32), ((256, 768), BF)],
        2 * 256 * 512 * 768,
        brick_count,
        send_list,
        folded,
        grad_local,
        *returned,
        face_hot,
        inner_hot,
    )
    grad_kernel, grad_down = call(
        unpack_kernel, 8, "v", [((C, 1728), F32), ((C2, 512), F32)], [], 10**6, sums
    )
    return coarse, grad_features, grad_kernel, grad_down


def solution(mesh):
    tile, grp = mesh.shape["tile"], mesh.shape["grp"]
    sizes = {"z": tile // 8, "x": 4, "c": 2, "grp": grp}
    fine = Mesh(mesh.devices.reshape(tuple(sizes.values())), tuple(sizes))
    line = ("z", "x", "c")
    in_specs = (
        P("grp", line, None, None),
        P("grp", line),
        P("grp", line, None, None),
        P("grp", line, None),
        P(),
        P(),
        P("grp", line, None, None),
    )
    out_specs = (P("grp", line, None, None), P("grp", line, None, None), P(), P())

    def step(*args):
        return on_device(sizes, *args)

    return jax.shard_map(step, mesh=fine, in_specs=in_specs, out_specs=out_specs, check_vma=False)
```

```python
import jax
import jax.numpy as jnp
import ml_dtypes
import numpy as np
from jax import lax
from jax.experimental import pallas as pl
from jax.experimental.pallas import tpu as pltpu
from jax.sharding import Mesh
from jax.sharding import PartitionSpec as P

BF = jnp.bfloat16
F32 = jnp.float32
DIRECTIONS = [
    (a, b, c) for a in (-1, 0, 1) for b in (-1, 0, 1) for c in (-1, 0, 1) if (a, b, c) != (0, 0, 0)
]
SHIFTS = [10 * b + c for b in (-1, 0, 1) for c in (-1, 0, 1)]
SLOTS, C, C2, NOFF, CAP = 4, 64, 128, 4, 4
LOCAL = 6 * SLOTS + 1
TABLE = LOCAL + NOFF * CAP
PLACES = list(range(9)) + [None] + list(range(9, 26)) + [None]
OFFSETS = (1, -1, 2, -2)
NEAR = ("zl", "x", "c", "grp")


def rim_cells(d, full):
    if d == -1:
        return [(7, 0)]
    if d == 1:
        return [(0, 9)]
    return [(i, i + 1) for i in range(full)]


def one_hot_tables():
    faces = np.zeros((512, 6, 128), np.float32)
    for x in range(8):
        for y in range(8):
            for z in range(8):
                v = (x, y, z)
                for a in range(3):
                    p, q = [v[i] for i in range(3) if i != a]
                    for e in range(2):
                        if v[a] == 7 * e:
                            faces[x * 64 + y * 8 + z, 2 * a + e, p * 8 + q] = 1
    inner = np.zeros((2, 64, 2, 128), np.float32)
    for s in range(2):
        for y in range(8):
            for z in range(8):
                inner[s, y * 8 + z, s, (y + 1) * 10 + z + 1] = 1
    cap = np.zeros((10, 64, 128), np.float32)
    side = np.zeros((8, 64, 128), np.float32)
    for m, d in enumerate([d for d in DIRECTIONS if d[0] == 0]):
        if d[1] != 0:
            yy = 0 if d[1] == -1 else 9
            for x in range(8):
                for i, zz in rim_cells(d[2], 8):
                    side[m, x * 8 + i, yy * 10 + zz] = 1
        else:
            zz = 0 if d[2] == -1 else 9
            for x in range(8):
                for y in range(8):
                    side[m, x * 8 + y, (y + 1) * 10 + zz] = 1
    for m, (dy, dz) in enumerate([(b, c) for b in (-1, 0, 1) for c in (-1, 0, 1)]):
        for i, yy in rim_cells(dy, 8):
            for k, zz in rim_cells(dz, 8):
                cap[m, i * 8 + k, yy * 10 + zz] = 1
    window = np.zeros((2, 128, 9, 2, 64), np.float32)
    for k, shift in enumerate(SHIFTS):
        for y in range(8):
            for z in range(8):
                for p in range(2):
                    window[p, (y + 1) * 10 + z + 1 + shift, k, p, y * 8 + z] = 1
    spread = np.zeros((4, 4, 4, 2, 2, 4, 64), np.float32)
    pick = np.zeros((2, 2, 2, 4, 4, 2, 64), np.float32)
    for ty in range(2):
        for tz in range(2):
            for Y in range(4):
                for Z in range(4):
                    lane = (2 * Y + ty) * 8 + 2 * Z + tz
                    for X in range(4):
                        spread[X, Y, Z, ty, tz, X, lane] = 1
                    for tx in range(2):
                        pick[tx, ty, tz, Y, Z, tx, lane] = 1
    def stacked(table):
        rows, lanes = table.shape
        return table.reshape(rows, lanes // 128, 128).transpose(1, 0, 2).reshape(-1, 128)

    placing = np.concatenate(
        [
            cap.reshape(640, 128),
            side.reshape(512, 128),
            stacked(inner.reshape(128, 256)),
            pick.reshape(128, 128),
            stacked(spread.reshape(64, 1024)),
            stacked(window.reshape(256, 1152)),
        ]
    )
    b = ml_dtypes.bfloat16
    packed = faces[:, 2:, :64].reshape(512, 256)
    inner = inner.reshape(128, 256)
    return packed.astype(b), faces.reshape(512, 768).astype(b), inner.astype(b), placing.astype(b)


CAP_ROWS, SIDE_ROWS, INNER_ROWS, PICK_ROWS, SPREAD_ROWS = 0, 640, 1152, 1408, 1536
WINDOW_ROWS, FOLD_ROWS, ALL_ROWS = 2048, 1408, 4352


def tiles_of(table, start, rows, first, count):
    blocks = [table[start + (first + i) * rows : start + (first + i + 1) * rows] for i in range(count)]
    return jnp.concatenate(blocks, axis=1)


def side_tiles(table, first, count):
    side = table[SIDE_ROWS : SIDE_ROWS + 512]
    plane = (lax.broadcasted_iota(jnp.int32, (512, 128), 0) // 8) % 8
    return jnp.concatenate(
        [jnp.where(plane == first + i, side, jnp.zeros_like(side)) for i in range(count)], axis=1
    )


def low_lanes(shape):
    return lax.broadcasted_iota(jnp.int32, shape, 1) < 64


def nn(a, b):
    return jnp.dot(a, b, preferred_element_type=F32)


def nt(a, b):
    return lax.dot_general(a, b, (((1,), (1,)), ((), ())), preferred_element_type=F32)


def masked_rows(features, count):
    return jnp.concatenate(
        [features[0, s] * jnp.where(s < count, 1.0, 0.0).astype(BF) for s in range(SLOTS)], axis=0
    )


def fetch(sources, targets, done):
    copies = [
        pltpu.make_async_copy(a, b, done.at[i]) for i, (a, b) in enumerate(zip(sources, targets))
    ]
    for copy in copies:
        copy.start()
    return copies


def wait(copies):
    for copy in copies:
        copy.wait()


def faces_kernel(
    count, sends_far, features_far, face_far, table, *rest
):
    outgoing, (sends, features, face_hot, done) = rest[:NOFF], rest[NOFF:]
    wait(fetch((features_far, face_far, sends_far), (features, face_hot, sends), done))
    masked = masked_rows(features, count[0, 0])
    low = low_lanes((SLOTS * C, 128))
    none = jnp.zeros((SLOTS * C, 128), BF)
    found = nn(masked, face_hot[...]).astype(BF)
    pairs = (found[:, 0:128], found[:, 128:256])
    layers = [masked[:, 0:128], pltpu.roll(masked[:, 384:512], 64, 1)]
    for block in pairs:
        layers += [block, pltpu.roll(block, 64, 1)]
    for f in range(6):
        layer = jnp.where(low, layers[f], none)
        for s in range(SLOTS):
            table[6 * s + f] = layer[s * C : (s + 1) * C]
    table[6 * SLOTS] = jnp.zeros((C, 128), BF)
    for j in range(NOFF):
        for q in range(CAP // 2):
            high = table[sends[0, 0, j, 2 * q + 1]]
            outgoing[j][q] = table[sends[0, 0, j, 2 * q]] + pltpu.roll(high, 64, 1)


def main_kernel(
    count,
    sources_far,
    table,
    ahead,
    behind,
    ahead2,
    behind2,
    features_far,
    placing_far,
    kernel_far,
    down_far,
    out_far,
    coarse,
    grad_preact,
    sums,
    conv_back,
    sources,
    arrived,
    features,
    placing,
    kernel,
    down_kernel,
    out_grad,
    halo,
    halo_high,
    conv,
    entries,
    padded,
    stack,
    shifted,
    lowered,
    total,
    done,
):
    copies = fetch(
        (ahead, behind, ahead2, behind2, table, sources_far)
        + (features_far, placing_far, kernel_far, down_far, out_far),
        [arrived.at[j] for j in range(NOFF)]
        + [halo.at[0:LOCAL], sources, features, placing, kernel, down_kernel, out_grad],
        done,
    )
    wait(copies[: NOFF + 2])
    low = low_lanes((C, 128))
    none = jnp.zeros((C, 128), BF)
    halo_high[0:LOCAL] = pltpu.roll(
        halo[0:LOCAL].reshape(LOCAL * C, 128), 64, 1
    ).reshape(LOCAL, C, 128)
    for j in range(NOFF):
        for q in range(CAP // 2):
            block, place = arrived[j, q], LOCAL + j * CAP + 2 * q
            turned = pltpu.roll(block, 64, 1)
            halo[place] = jnp.where(low, block, none)
            halo[place + 1] = jnp.where(low, turned, none)
            halo_high[place] = jnp.where(low, none, turned)
            halo_high[place + 1] = jnp.where(low, none, block)
    for s in range(SLOTS):
        for t in range(14):
            even, odd = PLACES[2 * t], PLACES[2 * t + 1]
            block = halo[sources[0, s, even]]
            if odd is not None:
                block = block + halo_high[sources[0, s, odd]]
            entries[s * C : (s + 1) * C, t * 128 : (t + 1) * 128] = block
    wait(copies[NOFF + 2 :])
    cap_hot = placing[CAP_ROWS : CAP_ROWS + 640]
    inner_hot = tiles_of(placing, INNER_ROWS, 128, 0, 2)
    pick_hot = placing[PICK_ROWS : PICK_ROWS + 128]
    masked = masked_rows(features, count[0, 0])
    padded[:, 0:128] = nn(entries[:, 0:640], cap_hot).astype(BF)
    padded[:, 1152:1280] = nn(entries[:, 1152:1792], cap_hot).astype(BF)
    for i in range(4):
        block = nn(entries[:, 640:1152], side_tiles(placing, 2 * i, 2))
        block = block + nn(masked[:, i * 128 : (i + 1) * 128], inner_hot)
        padded[:, 128 + i * 256 : 384 + i * 256] = block.astype(BF)
    window_hot = tiles_of(placing, WINDOW_ROWS, 256, 0, 9)
    for i in range(5):
        planes = nn(padded[:, i * 256 : (i + 1) * 256], window_hot).astype(BF)
        for s in range(SLOTS):
            lanes = slice((s % 2) * 640 + i * 128, (s % 2) * 640 + (i + 1) * 128)
            for k in range(9):
                block = planes[s * C : (s + 1) * C, k * 128 : (k + 1) * 128]
                stack[s // 2, k * C : (k + 1) * C, lanes] = block

    for o in range(3):
        conv[o * C : (o + 1) * C] = kernel[:, o * 576 : (o + 1) * 576]
    tall = jnp.transpose(kernel[...].astype(F32)).astype(BF)
    for o in range(3):
        conv_back[o * C : (o + 1) * C] = jnp.concatenate(
            [tall[(9 * o + k) * C : (9 * o + k + 1) * C] for k in range(9)], axis=1
        )
    tall = jnp.transpose(down_kernel[...].astype(F32)).astype(BF)
    down_rows = jnp.concatenate(
        [
            jnp.concatenate([tall[(4 * tx + t) * C : (4 * tx + t + 1) * C] for t in range(4)], axis=1)
            for tx in range(2)
        ],
        axis=0,
    )
    left = low_lanes((16, 128))
    edge = jnp.zeros((C, 64), BF)
    wide = jnp.zeros((C, 128), BF)
    total[...] = jnp.zeros_like(total)

    def pair(p, carry):
        triple = nn(conv[...], stack[p])
        for j in range(2):
            s = 2 * p + j
            filled = jnp.where(s < count[0, 0], 1.0, 0.0).astype(F32)
            base = j * 640
            preact = (
                triple[0:C, base : base + 512]
                + triple[C : 2 * C, base + 64 : base + 576]
                + triple[2 * C :, base + 128 : base + 640]
            )
            sigmoid = jax.nn.sigmoid(preact)
            active = (preact * sigmoid * filled).astype(BF)
            for h in range(2):
                halves = [active[:, (2 * h + i) * 128 : (2 * h + i + 1) * 128] for i in range(2)]
                rows = jnp.concatenate([halves[0], halves[0], halves[1], halves[1]], axis=0)
                picked = nt(pick_hot, rows)
                for i in range(2):
                    X = 2 * h + i
                    for q in range(4):
                        lanes = slice(i * 128, (i + 1) * 128)
                        block = jnp.where(
                            left,
                            picked[32 * q : 32 * q + 16, lanes],
                            picked[32 * q + 16 : 32 * q + 32, lanes],
                        )
                        lowered[s, X * 16 : (X + 1) * 16, q * 128 : (q + 1) * 128] = block.astype(BF)
            turned = jnp.transpose(out_grad[0, s].astype(F32)).astype(BF)
            spread = nn(turned, tiles_of(placing, SPREAD_ROWS, 64, 0, 8)).astype(BF)
            spread = jnp.concatenate([spread[:, t * 256 : (t + 1) * 256] for t in range(4)], axis=0)
            grown = nn(down_rows, spread)
            upper = jnp.concatenate(
                [
                    grown[tx * C : (tx + 1) * C, X * 64 : (X + 1) * 64]
                    for X in range(4)
                    for tx in range(2)
                ],
                axis=1,
            )
            grads = upper * sigmoid * (1.0 + preact * (1.0 - sigmoid)) * filled
            grads = grads.astype(BF)
            grad_preact[s] = grads
            shifted[0:C, base : base + 640] = jnp.concatenate([grads, wide], axis=1)
            shifted[C : 2 * C, base : base + 640] = jnp.concatenate([edge, grads, edge], axis=1)
            shifted[2 * C :, base : base + 640] = jnp.concatenate([wide, grads], axis=1)
        total[...] += nt(shifted[...], stack[p])
        return carry

    lax.fori_loop(0, SLOTS // 2, pair, 0)
    rows = lowered[...].reshape(SLOTS * 64, 512)
    coarse[...] = nt(rows, down_kernel[...]).astype(BF).reshape(coarse.shape)
    turned = jnp.transpose(out_grad[...].reshape(SLOTS * 64, C2).astype(F32)).astype(BF)
    grad_down = nn(turned, rows)
    for j in range(5):
        width = min(128, 576 - j * 128)
        sums[j * 192 : (j + 1) * 192, 0:width] = total[:, j * 128 : j * 128 + width].astype(BF)
    sums[4 * 192 : 5 * 192, 64:128] = jnp.zeros((192, 64), BF)
    for j in range(4):
        sums[960 + j * C2 : 960 + (j + 1) * C2] = grad_down[:, j * 128 : (j + 1) * 128].astype(BF)
    sums[1472:1536] = jnp.zeros((64, 128), BF)


def fold_kernel(
    sources,
    grads_far,
    conv_far,
    placing_far,
    folded,
    grad_local,
    to_ahead,
    to_behind,
    to_ahead2,
    to_behind2,
    grad_preact,
    conv_back,
    placing,
    planes,
    stack,
    high,
    rims,
    grad_table,
    grad_table_high,
    done,
):
    copies = fetch(
        (grads_far, placing_far.at[0:FOLD_ROWS], conv_far), (grad_preact, placing, conv_back), done
    )
    grad_table[...] = jnp.zeros_like(grad_table)
    grad_table_high[...] = jnp.zeros_like(grad_table_high)
    wait(copies[:2])
    cap_hot = placing[CAP_ROWS : CAP_ROWS + 640]
    inner_hot = tiles_of(placing, INNER_ROWS, 128, 0, 2)
    rows = grad_preact[...].reshape(SLOTS * C, 512)
    for i in range(4):
        block = nn(rows[:, i * 128 : (i + 1) * 128], inner_hot)
        planes[:, i * 256 : (i + 1) * 256] = block.astype(BF)
    wait(copies[2:])

    def brick(s, carry):
        here = pl.ds(pl.multiple_of(s * C, C), C)
        for x in range(8):
            plane = planes[here, x * 128 : (x + 1) * 128]
            for k, shift in enumerate(SHIFTS):
                moved = plane if shift == 0 else pltpu.roll(plane, shift % 128, 1)
                stack[k * C : (k + 1) * C, x * 128 : (x + 1) * 128] = moved
        triple = nn(conv_back[...], stack[...])
        for x in range(10):
            value = None
            for o in range(3):
                if 0 <= x - o < 8:
                    part = triple[o * C : (o + 1) * C, (x - o) * 128 : (x - o + 1) * 128]
                    value = part if value is None else value + part
            high[here, x * 128 : (x + 1) * 128] = value.astype(BF)
            if 1 <= x <= 8:
                folded[here, (x - 1) * 128 : x * 128] = value
        return carry

    lax.fori_loop(0, SLOTS, brick, 0)
    rims[:, 0:640] = nt(high[:, 0:128], cap_hot)
    rims[:, 640:1152] = nt(high[:, 128:1152], side_tiles(placing, 0, 8))
    rims[:, 1152:1792] = nt(high[:, 1152:1280], cap_hot)
    for s in range(SLOTS):
        for t in range(14):
            block = rims[s * C : (s + 1) * C, t * 128 : (t + 1) * 128]
            grad_table[sources[0, s, PLACES[2 * t]]] += block
            if PLACES[2 * t + 1] is not None:
                grad_table_high[sources[0, s, PLACES[2 * t + 1]]] += block
    turned = pltpu.roll(grad_table_high[...].reshape(TABLE * C, 128), 64, 1)
    grad_table[...] += turned.reshape(TABLE, C, 128)
    grad_local[...] = grad_table[0:LOCAL]
    left = low_lanes((C, 128))
    for j in range(NOFF):
        for q in range(CAP // 2):
            place = LOCAL + j * CAP + 2 * q
            block = jnp.where(left, grad_table[place], pltpu.roll(grad_table[place + 1], 64, 1))
            (to_ahead, to_behind, to_ahead2, to_behind2)[j][q] = block.astype(BF)


def unpack_kernel(sums, grad_kernel, grad_down):
    parts = []
    for o in range(3):
        tiles = [sums[j * 192 + o * C : j * 192 + (o + 1) * C].astype(F32) for j in range(5)]
        parts.append(jnp.concatenate(tiles, axis=1)[:, :576])
    grad_kernel[...] = jnp.concatenate(parts, axis=1)
    tiles = [sums[960 + t * C2 : 960 + (t + 1) * C2].astype(F32) for t in range(4)]
    grad_down[...] = jnp.concatenate(tiles, axis=1)


def finish_kernel(
    count,
    sends,
    folded,
    grad_local,
    ahead,
    behind,
    ahead2,
    behind2,
    face_hot,
    inner_hot,
    grad_features,
    table,
    layers,
):
    table[...] = grad_local[...]
    for j in range(NOFF):
        for q in range(CAP // 2):
            block = (ahead, behind, ahead2, behind2)[j][q].astype(F32)
            table[sends[0, 0, j, 2 * q]] += block
            table[sends[0, 0, j, 2 * q + 1]] += pltpu.roll(block, 64, 1)
    for s in range(SLOTS):
        for f in range(6):
            layers[s * C : (s + 1) * C, f * 128 : (f + 1) * 128] = table[6 * s + f].astype(BF)
    tiles = []
    for i in range(4):
        value = folded[:, i * 256 : (i + 1) * 256]
        top = value.astype(BF)
        rest = (value - top.astype(F32)).astype(BF)
        tiles.append(nt(top, inner_hot[...]) + nt(rest, inner_hot[...]))
    whole = jnp.concatenate(tiles, axis=1) + nt(layers[...], face_hot[...])
    for s in range(SLOTS):
        filled = jnp.where(s < count[0, 0], 1.0, 0.0).astype(F32)
        grad_features[0, s] = (whole[s * C : (s + 1) * C] * filled).astype(BF)


def call(kernel, limit, memories, outs, scratch, flops, *args):
    where = {"s": pltpu.SMEM, "v": pltpu.VMEM, "h": pltpu.HBM}
    return pl.pallas_call(
        kernel,
        in_specs=[pl.BlockSpec(memory_space=where[m]) for m in memories],
        out_specs=[pl.BlockSpec(memory_space=pltpu.VMEM) for _ in outs],
        out_shape=[jax.ShapeDtypeStruct(s, d) for s, d in outs],
        scratch_shapes=[pltpu.VMEM(*s) if isinstance(s, tuple) else s for s in scratch],
        compiler_params=pltpu.CompilerParams(vmem_limit_bytes=int(limit * 2**20)),
        cost_estimate=pl.CostEstimate(flops=flops, bytes_accessed=2**20, transcendentals=0),
        name=kernel.__name__,
    )(*args)


def gather_sum(block, axes, parts):
    copies = jnp.broadcast_to(block[None], (parts,) + block.shape)
    got = lax.all_to_all(copies, axes, 0, 0)
    return got.astype(F32).sum(0)


def near_sum(block, sizes):
    parts = sizes["zl"] * sizes["x"] * sizes["c"] * sizes["grp"]
    rows = block.shape[0] // parts
    got = lax.all_to_all(block.reshape(parts, rows, 128), NEAR, 0, 0)
    return got.astype(F32).sum(0).astype(BF)


def near_gather(block, sizes):
    parts = sizes["zl"] * sizes["x"] * sizes["c"] * sizes["grp"]
    copies = jnp.broadcast_to(block[None], (parts,) + block.shape)
    return lax.all_to_all(copies, NEAR, 0, 0).reshape(parts * block.shape[0], 128)


def from_behind(block, axes, devices, distance):
    route = [(i - distance, i) for i in range(devices) if 0 <= i - distance < devices]
    return lax.ppermute(block, axes, route)


def on_device(sizes, features, brick_count, send_list, halo_src, kernel, down_kernel, out_grad):
    face_packed, face_hot, inner_hot, placing = one_hot_tables()
    tile = ("zh", "zl", "x", "c")
    devices = sizes["zh"] * sizes["zl"] * sizes["x"] * sizes["c"]
    swap = [((CAP // 2, C, 128), BF)] * NOFF

    table, *outgoing = call(
        faces_kernel,
        56,
        "shhh",
        [((LOCAL, C, 128), BF)] + swap,
        [
            pltpu.SMEM((1, 1, NOFF, CAP), jnp.int32),
            ((1, SLOTS, C, 512), BF),
            ((512, 256), BF),
            pltpu.SemaphoreType.DMA((3,)),
        ],
        2 * 256 * 512 * 768,
        brick_count,
        send_list,
        features,
        face_packed,
    )
    received = [from_behind(b, tile, devices, o) for b, o in zip(outgoing, OFFSETS)]
    coarse, grad_preact, sums, conv_back = call(
        main_kernel,
        53.8,
        "s" + "h" * 11,
        [
            ((1, SLOTS, 64, C2), BF),
            ((SLOTS, C, 512), BF),
            ((1536, 128), BF),
            ((192, 576), BF),
        ],
        [
            pltpu.SMEM((1, SLOTS, 26), jnp.int32),
            ((NOFF, CAP // 2, C, 128), BF),
            ((1, SLOTS, C, 512), BF),
            ((ALL_ROWS, 128), BF),
            ((C, 1728), BF),
            ((C2, 512), BF),
            ((1, SLOTS, 64, C2), BF),
            ((TABLE, C, 128), BF),
            ((TABLE, C, 128), BF),
            ((192, 576), BF),
            ((256, 14 * 128), BF),
            ((256, 1280), BF),
            ((2, 576, 1280), BF),
            ((192, 1280), BF),
            ((SLOTS, 64, 512), BF),
            ((192, 576), F32),
            pltpu.SemaphoreType.DMA((11,)),
        ],
        5 * 10**9,
        brick_count,
        halo_src,
        table,
        *received,
        features,
        placing,
        kernel,
        down_kernel,
        out_grad,
    )
    part = near_sum(sums, sizes)
    folded, grad_local, *remote = call(
        fold_kernel,
        56,
        "shhh",
        [((256, 1024), F32), ((LOCAL, C, 128), F32)] + swap,
        [
            ((SLOTS, C, 512), BF),
            ((192, 576), BF),
            ((FOLD_ROWS, 128), BF),
            ((256, 1024), BF),
            ((576, 1024), BF),
            ((256, 1280), BF),
            ((256, 14 * 128), F32),
            ((TABLE, C, 128), F32),
            ((TABLE, C, 128), F32),
            pltpu.SemaphoreType.DMA((3,)),
        ],
        3 * 10**9,
        halo_src,
        grad_preact,
        conv_back,
        placing,
    )
    part, *remote = lax.optimization_barrier((part, *remote))
    part = gather_sum(part, ("zh",), sizes["zh"])
    returned = [from_behind(b, tile, devices, -o) for b, o in zip(remote, OFFSETS)]
    part, *returned = lax.optimization_barrier((part, *returned))
    sums = near_gather(part.astype(BF), sizes)
    (grad_features,) = call(
        finish_kernel,
        12,
        "ss" + "v" * 8,
        [((1, SLOTS, C, 512), BF)],
        [((LOCAL, C, 128), F32), ((256, 768), BF)],
        2 * 256 * 512 * 768,
        brick_count,
        send_list,
        folded,
        grad_local,
        *returned,
        face_hot,
        inner_hot,
    )
    grad_kernel, grad_down = call(
        unpack_kernel, 8, "v", [((C, 1728), F32), ((C2, 512), F32)], [], 10**6, sums
    )
    return coarse, grad_features, grad_kernel, grad_down


def solution(mesh):
    tile, grp = mesh.shape["tile"], mesh.shape["grp"]
    planes = tile // 8
    pair = 2 - planes % 2
    sizes = {"zh": planes // pair, "zl": pair, "x": 4, "c": 2, "grp": grp}
    fine = Mesh(mesh.devices.reshape(tuple(sizes.values())), tuple(sizes))
    line = ("zh", "zl", "x", "c")
    in_specs = (
        P("grp", line, None, None),
        P("grp", line),
        P("grp", line, None, None),
        P("grp", line, None),
        P(),
        P(),
        P("grp", line, None, None),
    )
    out_specs = (P("grp", line, None, None), P("grp", line, None, None), P(), P())

    def step(*args):
        return on_device(sizes, *args)

    return jax.shard_map(step, mesh=fine, in_specs=in_specs, out_specs=out_specs, check_vma=False)
```

```python
import jax
import jax.numpy as jnp
import ml_dtypes
import numpy as np
from jax import lax
from jax.experimental import pallas as pl
from jax.experimental.pallas import tpu as pltpu
from jax.sharding import Mesh
from jax.sharding import PartitionSpec as P

BF = jnp.bfloat16
F32 = jnp.float32
DIRECTIONS = [
    (a, b, c) for a in (-1, 0, 1) for b in (-1, 0, 1) for c in (-1, 0, 1) if (a, b, c) != (0, 0, 0)
]
SHIFTS = [10 * b + c for b in (-1, 0, 1) for c in (-1, 0, 1)]
SLOTS, C, C2, NOFF, CAP = 4, 64, 128, 4, 4
LOCAL = 6 * SLOTS + 1
TABLE = LOCAL + NOFF * CAP
PLACES = list(range(9)) + [None] + list(range(9, 26)) + [None]
OFFSETS = (1, -1, 2, -2)
NEAR = ("x", "c", "grp")


def rim_cells(d, full):
    if d == -1:
        return [(7, 0)]
    if d == 1:
        return [(0, 9)]
    return [(i, i + 1) for i in range(full)]


def one_hot_tables():
    faces = np.zeros((512, 6, 128), np.float32)
    for x in range(8):
        for y in range(8):
            for z in range(8):
                v = (x, y, z)
                for a in range(3):
                    p, q = [v[i] for i in range(3) if i != a]
                    for e in range(2):
                        if v[a] == 7 * e:
                            faces[x * 64 + y * 8 + z, 2 * a + e, p * 8 + q] = 1
    inner = np.zeros((2, 64, 2, 128), np.float32)
    for s in range(2):
        for y in range(8):
            for z in range(8):
                inner[s, y * 8 + z, s, (y + 1) * 10 + z + 1] = 1
    cap = np.zeros((10, 64, 128), np.float32)
    side = np.zeros((8, 64, 128), np.float32)
    for m, d in enumerate([d for d in DIRECTIONS if d[0] == 0]):
        if d[1] != 0:
            yy = 0 if d[1] == -1 else 9
            for x in range(8):
                for i, zz in rim_cells(d[2], 8):
                    side[m, x * 8 + i, yy * 10 + zz] = 1
        else:
            zz = 0 if d[2] == -1 else 9
            for x in range(8):
                for y in range(8):
                    side[m, x * 8 + y, (y + 1) * 10 + zz] = 1
    for m, (dy, dz) in enumerate([(b, c) for b in (-1, 0, 1) for c in (-1, 0, 1)]):
        for i, yy in rim_cells(dy, 8):
            for k, zz in rim_cells(dz, 8):
                cap[m, i * 8 + k, yy * 10 + zz] = 1
    window = np.zeros((2, 128, 9, 2, 64), np.float32)
    for k, shift in enumerate(SHIFTS):
        for y in range(8):
            for z in range(8):
                for p in range(2):
                    window[p, (y + 1) * 10 + z + 1 + shift, k, p, y * 8 + z] = 1
    spread = np.zeros((4, 4, 4, 2, 2, 4, 64), np.float32)
    pick = np.zeros((2, 2, 2, 4, 4, 2, 64), np.float32)
    for ty in range(2):
        for tz in range(2):
            for Y in range(4):
                for Z in range(4):
                    lane = (2 * Y + ty) * 8 + 2 * Z + tz
                    for X in range(4):
                        spread[X, Y, Z, ty, tz, X, lane] = 1
                    for tx in range(2):
                        pick[tx, ty, tz, Y, Z, tx, lane] = 1
    def stacked(table):
        rows, lanes = table.shape
        return table.reshape(rows, lanes // 128, 128).transpose(1, 0, 2).reshape(-1, 128)

    placing = np.concatenate(
        [
            cap.reshape(640, 128),
            side.reshape(512, 128),
            stacked(inner.reshape(128, 256)),
            pick.reshape(128, 128),
            stacked(spread.reshape(64, 1024)),
            stacked(window.reshape(256, 1152)),
        ]
    )
    b = ml_dtypes.bfloat16
    packed = faces[:, 2:, :64].reshape(512, 256)
    inner = inner.reshape(128, 256)
    return packed.astype(b), faces.reshape(512, 768).astype(b), inner.astype(b), placing.astype(b)


CAP_ROWS, SIDE_ROWS, INNER_ROWS, PICK_ROWS, SPREAD_ROWS = 0, 640, 1152, 1408, 1536
WINDOW_ROWS, FOLD_ROWS, ALL_ROWS = 2048, 1408, 4352


def tiles_of(table, start, rows, first, count):
    blocks = [table[start + (first + i) * rows : start + (first + i + 1) * rows] for i in range(count)]
    return jnp.concatenate(blocks, axis=1)


def side_tiles(table, first, count):
    side = table[SIDE_ROWS : SIDE_ROWS + 512]
    plane = (lax.broadcasted_iota(jnp.int32, (512, 128), 0) // 8) % 8
    return jnp.concatenate(
        [jnp.where(plane == first + i, side, jnp.zeros_like(side)) for i in range(count)], axis=1
    )


def low_lanes(shape):
    return lax.broadcasted_iota(jnp.int32, shape, 1) < 64


def nn(a, b):
    return jnp.dot(a, b, preferred_element_type=F32)


def nt(a, b):
    return lax.dot_general(a, b, (((1,), (1,)), ((), ())), preferred_element_type=F32)


def masked_rows(features, count):
    return jnp.concatenate(
        [features[0, s] * jnp.where(s < count, 1.0, 0.0).astype(BF) for s in range(SLOTS)], axis=0
    )


def fetch(sources, targets, done):
    copies = [
        pltpu.make_async_copy(a, b, done.at[i]) for i, (a, b) in enumerate(zip(sources, targets))
    ]
    for copy in copies:
        copy.start()
    return copies


def wait(copies):
    for copy in copies:
        copy.wait()


def faces_kernel(
    count, sends_far, features_far, face_far, table, *rest
):
    outgoing, (sends, features, face_hot, done) = rest[:NOFF], rest[NOFF:]
    wait(fetch((features_far, face_far, sends_far), (features, face_hot, sends), done))
    masked = masked_rows(features, count[0, 0])
    low = low_lanes((SLOTS * C, 128))
    none = jnp.zeros((SLOTS * C, 128), BF)
    found = nn(masked, face_hot[...]).astype(BF)
    pairs = (found[:, 0:128], found[:, 128:256])
    layers = [masked[:, 0:128], pltpu.roll(masked[:, 384:512], 64, 1)]
    for block in pairs:
        layers += [block, pltpu.roll(block, 64, 1)]
    for f in range(6):
        layer = jnp.where(low, layers[f], none)
        for s in range(SLOTS):
            table[6 * s + f] = layer[s * C : (s + 1) * C]
    table[6 * SLOTS] = jnp.zeros((C, 128), BF)
    for j in range(NOFF):
        for q in range(CAP // 2):
            high = table[sends[0, 0, j, 2 * q + 1]]
            outgoing[j][q] = table[sends[0, 0, j, 2 * q]] + pltpu.roll(high, 64, 1)


def upper_kernel(
    out_far,
    down_far,
    kernel_far,
    placing_far,
    grad_active,
    conv_back,
    out_grad,
    down_kernel,
    kernel,
    spread_rows,
    done,
):
    spread_far = placing_far.at[SPREAD_ROWS : SPREAD_ROWS + 512]
    copies = fetch(
        (out_far, down_far, spread_far, kernel_far),
        (out_grad, down_kernel, spread_rows, kernel),
        done,
    )
    wait(copies[:3])
    turned = jnp.concatenate(
        [jnp.transpose(out_grad[0, s].astype(F32)).astype(BF) for s in range(SLOTS)], axis=0
    )
    spread = nn(turned, tiles_of(spread_rows, 0, 64, 0, 8)).astype(BF)
    tall = jnp.transpose(down_kernel[...].astype(F32)).astype(BF)
    down_rows = jnp.concatenate(
        [
            jnp.concatenate([tall[(4 * tx + t) * C : (4 * tx + t + 1) * C] for t in range(4)], axis=1)
            for tx in range(2)
        ],
        axis=0,
    )
    for s in range(SLOTS):
        rows = slice(s * C2, (s + 1) * C2)
        block = jnp.concatenate([spread[rows, t * 256 : (t + 1) * 256] for t in range(4)], axis=0)
        grown = nn(down_rows, block)
        grad_active[s] = jnp.concatenate(
            [
                grown[tx * C : (tx + 1) * C, X * 64 : (X + 1) * 64]
                for X in range(4)
                for tx in range(2)
            ],
            axis=1,
        )
    wait(copies[3:])
    tall = jnp.transpose(kernel[...].astype(F32)).astype(BF)
    for o in range(3):
        conv_back[o * C : (o + 1) * C] = jnp.concatenate(
            [tall[(9 * o + k) * C : (9 * o + k + 1) * C] for k in range(9)], axis=1
        )


def main_kernel(
    count,
    sources_far,
    table,
    ahead,
    behind,
    ahead2,
    behind2,
    features_far,
    placing_far,
    kernel_far,
    down_far,
    out_far,
    active_far,
    coarse,
    grad_preact,
    sums,
    sources,
    arrived,
    features,
    placing,
    kernel,
    down_kernel,
    out_grad,
    grad_active,
    halo,
    halo_high,
    conv,
    entries,
    padded,
    stack,
    shifted,
    lowered,
    total,
    done,
):
    copies = fetch(
        (ahead, behind, ahead2, behind2, table, sources_far)
        + (features_far, placing_far, kernel_far, down_far, out_far, active_far),
        [arrived.at[j] for j in range(NOFF)]
        + [halo.at[0:LOCAL], sources, features, placing, kernel, down_kernel, out_grad]
        + [grad_active],
        done,
    )
    wait(copies[: NOFF + 2])
    low = low_lanes((C, 128))
    none = jnp.zeros((C, 128), BF)
    halo_high[0:LOCAL] = pltpu.roll(
        halo[0:LOCAL].reshape(LOCAL * C, 128), 64, 1
    ).reshape(LOCAL, C, 128)
    for j in range(NOFF):
        for q in range(CAP // 2):
            block, place = arrived[j, q], LOCAL + j * CAP + 2 * q
            turned = pltpu.roll(block, 64, 1)
            halo[place] = jnp.where(low, block, none)
            halo[place + 1] = jnp.where(low, turned, none)
            halo_high[place] = jnp.where(low, none, turned)
            halo_high[place + 1] = jnp.where(low, none, block)
    for s in range(SLOTS):
        for t in range(14):
            even, odd = PLACES[2 * t], PLACES[2 * t + 1]
            block = halo[sources[0, s, even]]
            if odd is not None:
                block = block + halo_high[sources[0, s, odd]]
            entries[s * C : (s + 1) * C, t * 128 : (t + 1) * 128] = block
    wait(copies[NOFF + 2 :])
    cap_hot = placing[CAP_ROWS : CAP_ROWS + 640]
    inner_hot = tiles_of(placing, INNER_ROWS, 128, 0, 2)
    pick_hot = placing[PICK_ROWS : PICK_ROWS + 128]
    masked = masked_rows(features, count[0, 0])
    padded[:, 0:128] = nn(entries[:, 0:640], cap_hot).astype(BF)
    padded[:, 1152:1280] = nn(entries[:, 1152:1792], cap_hot).astype(BF)
    for i in range(4):
        block = nn(entries[:, 640:1152], side_tiles(placing, 2 * i, 2))
        block = block + nn(masked[:, i * 128 : (i + 1) * 128], inner_hot)
        padded[:, 128 + i * 256 : 384 + i * 256] = block.astype(BF)
    window_hot = tiles_of(placing, WINDOW_ROWS, 256, 0, 9)
    for i in range(5):
        planes = nn(padded[:, i * 256 : (i + 1) * 256], window_hot).astype(BF)
        for s in range(SLOTS):
            lanes = slice((s % 2) * 640 + i * 128, (s % 2) * 640 + (i + 1) * 128)
            for k in range(9):
                block = planes[s * C : (s + 1) * C, k * 128 : (k + 1) * 128]
                stack[s // 2, k * C : (k + 1) * C, lanes] = block

    for o in range(3):
        conv[o * C : (o + 1) * C] = kernel[:, o * 576 : (o + 1) * 576]
    left = low_lanes((16, 128))
    edge = jnp.zeros((C, 64), BF)
    wide = jnp.zeros((C, 128), BF)
    total[...] = jnp.zeros_like(total)

    def pair(p, carry):
        triple = nn(conv[...], stack[p])
        for j in range(2):
            s = 2 * p + j
            filled = jnp.where(s < count[0, 0], 1.0, 0.0).astype(F32)
            base = j * 640
            preact = (
                triple[0:C, base : base + 512]
                + triple[C : 2 * C, base + 64 : base + 576]
                + triple[2 * C :, base + 128 : base + 640]
            )
            sigmoid = jax.nn.sigmoid(preact)
            active = (preact * sigmoid * filled).astype(BF)
            for h in range(2):
                halves = [active[:, (2 * h + i) * 128 : (2 * h + i + 1) * 128] for i in range(2)]
                rows = jnp.concatenate([halves[0], halves[0], halves[1], halves[1]], axis=0)
                picked = nt(pick_hot, rows)
                for i in range(2):
                    X = 2 * h + i
                    for q in range(4):
                        lanes = slice(i * 128, (i + 1) * 128)
                        block = jnp.where(
                            left,
                            picked[32 * q : 32 * q + 16, lanes],
                            picked[32 * q + 16 : 32 * q + 32, lanes],
                        )
                        lowered[s, X * 16 : (X + 1) * 16, q * 128 : (q + 1) * 128] = block.astype(BF)
            grads = grad_active[s] * sigmoid * (1.0 + preact * (1.0 - sigmoid)) * filled
            grads = grads.astype(BF)
            grad_preact[s] = grads
            shifted[0:C, base : base + 640] = jnp.concatenate([grads, wide], axis=1)
            shifted[C : 2 * C, base : base + 640] = jnp.concatenate([edge, grads, edge], axis=1)
            shifted[2 * C :, base : base + 640] = jnp.concatenate([wide, grads], axis=1)
        total[...] += nt(shifted[...], stack[p])
        return carry

    lax.fori_loop(0, SLOTS // 2, pair, 0)
    rows = lowered[...].reshape(SLOTS * 64, 512)
    coarse[...] = nt(rows, down_kernel[...]).astype(BF).reshape(coarse.shape)
    turned = jnp.transpose(out_grad[...].reshape(SLOTS * 64, C2).astype(F32)).astype(BF)
    grad_down = nn(turned, rows)
    for j in range(5):
        width = min(128, 576 - j * 128)
        sums[j * 192 : (j + 1) * 192, 0:width] = total[:, j * 128 : j * 128 + width].astype(BF)
    sums[4 * 192 : 5 * 192, 64:128] = jnp.zeros((192, 64), BF)
    for j in range(4):
        sums[960 + j * C2 : 960 + (j + 1) * C2] = grad_down[:, j * 128 : (j + 1) * 128].astype(BF)
    sums[1472:1536] = jnp.zeros((64, 128), BF)


def fold_kernel(
    sources,
    grads_far,
    conv_far,
    placing_far,
    folded,
    grad_local,
    to_ahead,
    to_behind,
    to_ahead2,
    to_behind2,
    grad_preact,
    conv_back,
    placing,
    planes,
    stack,
    high,
    rims,
    grad_table,
    grad_table_high,
    done,
):
    copies = fetch(
        (grads_far, placing_far.at[0:FOLD_ROWS], conv_far), (grad_preact, placing, conv_back), done
    )
    grad_table[...] = jnp.zeros_like(grad_table)
    grad_table_high[...] = jnp.zeros_like(grad_table_high)
    wait(copies[:2])
    cap_hot = placing[CAP_ROWS : CAP_ROWS + 640]
    inner_hot = tiles_of(placing, INNER_ROWS, 128, 0, 2)
    rows = grad_preact[...].reshape(SLOTS * C, 512)
    for i in range(4):
        block = nn(rows[:, i * 128 : (i + 1) * 128], inner_hot)
        planes[:, i * 256 : (i + 1) * 256] = block.astype(BF)
    wait(copies[2:])

    def brick(s, carry):
        here = pl.ds(pl.multiple_of(s * C, C), C)
        for x in range(8):
            plane = planes[here, x * 128 : (x + 1) * 128]
            for k, shift in enumerate(SHIFTS):
                moved = plane if shift == 0 else pltpu.roll(plane, shift % 128, 1)
                stack[k * C : (k + 1) * C, x * 128 : (x + 1) * 128] = moved
        triple = nn(conv_back[...], stack[...])
        for x in range(10):
            value = None
            for o in range(3):
                if 0 <= x - o < 8:
                    part = triple[o * C : (o + 1) * C, (x - o) * 128 : (x - o + 1) * 128]
                    value = part if value is None else value + part
            high[here, x * 128 : (x + 1) * 128] = value.astype(BF)
            if 1 <= x <= 8:
                folded[here, (x - 1) * 128 : x * 128] = value
        return carry

    lax.fori_loop(0, SLOTS, brick, 0)
    rims[:, 0:640] = nt(high[:, 0:128], cap_hot)
    rims[:, 640:1152] = nt(high[:, 128:1152], side_tiles(placing, 0, 8))
    rims[:, 1152:1792] = nt(high[:, 1152:1280], cap_hot)
    for s in range(SLOTS):
        for t in range(14):
            block = rims[s * C : (s + 1) * C, t * 128 : (t + 1) * 128]
            grad_table[sources[0, s, PLACES[2 * t]]] += block
            if PLACES[2 * t + 1] is not None:
                grad_table_high[sources[0, s, PLACES[2 * t + 1]]] += block
    turned = pltpu.roll(grad_table_high[...].reshape(TABLE * C, 128), 64, 1)
    grad_table[...] += turned.reshape(TABLE, C, 128)
    grad_local[...] = grad_table[0:LOCAL]
    left = low_lanes((C, 128))
    for j in range(NOFF):
        for q in range(CAP // 2):
            place = LOCAL + j * CAP + 2 * q
            block = jnp.where(left, grad_table[place], pltpu.roll(grad_table[place + 1], 64, 1))
            (to_ahead, to_behind, to_ahead2, to_behind2)[j][q] = block.astype(BF)


def unpack_kernel(sums, grad_kernel, grad_down):
    parts = []
    for o in range(3):
        tiles = [sums[j * 192 + o * C : j * 192 + (o + 1) * C].astype(F32) for j in range(5)]
        parts.append(jnp.concatenate(tiles, axis=1)[:, :576])
    grad_kernel[...] = jnp.concatenate(parts, axis=1)
    tiles = [sums[960 + t * C2 : 960 + (t + 1) * C2].astype(F32) for t in range(4)]
    grad_down[...] = jnp.concatenate(tiles, axis=1)


def finish_kernel(
    count,
    sends,
    folded,
    grad_local,
    ahead,
    behind,
    ahead2,
    behind2,
    face_hot,
    inner_hot,
    grad_features,
    table,
    layers,
):
    table[...] = grad_local[...]
    for j in range(NOFF):
        for q in range(CAP // 2):
            block = (ahead, behind, ahead2, behind2)[j][q].astype(F32)
            table[sends[0, 0, j, 2 * q]] += block
            table[sends[0, 0, j, 2 * q + 1]] += pltpu.roll(block, 64, 1)
    for s in range(SLOTS):
        for f in range(6):
            layers[s * C : (s + 1) * C, f * 128 : (f + 1) * 128] = table[6 * s + f].astype(BF)
    tiles = []
    for i in range(4):
        value = folded[:, i * 256 : (i + 1) * 256]
        top = value.astype(BF)
        rest = (value - top.astype(F32)).astype(BF)
        tiles.append(nt(top, inner_hot[...]) + nt(rest, inner_hot[...]))
    whole = jnp.concatenate(tiles, axis=1) + nt(layers[...], face_hot[...])
    for s in range(SLOTS):
        filled = jnp.where(s < count[0, 0], 1.0, 0.0).astype(F32)
        grad_features[0, s] = (whole[s * C : (s + 1) * C] * filled).astype(BF)


def call(kernel, limit, memories, outs, scratch, flops, *args):
    where = {"s": pltpu.SMEM, "v": pltpu.VMEM, "h": pltpu.HBM}
    return pl.pallas_call(
        kernel,
        in_specs=[pl.BlockSpec(memory_space=where[m]) for m in memories],
        out_specs=[pl.BlockSpec(memory_space=pltpu.VMEM) for _ in outs],
        out_shape=[jax.ShapeDtypeStruct(s, d) for s, d in outs],
        scratch_shapes=[pltpu.VMEM(*s) if isinstance(s, tuple) else s for s in scratch],
        compiler_params=pltpu.CompilerParams(vmem_limit_bytes=int(limit * 2**20)),
        cost_estimate=pl.CostEstimate(flops=flops, bytes_accessed=2**20, transcendentals=0),
        name=kernel.__name__,
    )(*args)


def gather_sum(block, axes, parts):
    copies = jnp.broadcast_to(block[None], (parts,) + block.shape)
    got = lax.all_to_all(copies, axes, 0, 0)
    return got.astype(F32).sum(0)


def near_sum(block, sizes):
    parts = sizes["x"] * sizes["c"] * sizes["grp"]
    rows = block.shape[0] // parts
    got = lax.all_to_all(block.reshape(parts, rows, 128), NEAR, 0, 0)
    return got.astype(F32).sum(0).astype(BF)


def near_gather(block, sizes):
    parts = sizes["x"] * sizes["c"] * sizes["grp"]
    copies = jnp.broadcast_to(block[None], (parts,) + block.shape)
    return lax.all_to_all(copies, NEAR, 0, 0).reshape(parts * block.shape[0], 128)


def from_behind(block, axes, devices, distance):
    route = [(i - distance, i) for i in range(devices) if 0 <= i - distance < devices]
    return lax.ppermute(block, axes, route)


def on_device(sizes, features, brick_count, send_list, halo_src, kernel, down_kernel, out_grad):
    face_packed, face_hot, inner_hot, placing = one_hot_tables()
    tile = ("z", "x", "c")
    devices = sizes["z"] * sizes["x"] * sizes["c"]
    swap = [((CAP // 2, C, 128), BF)] * NOFF

    table, *outgoing = call(
        faces_kernel,
        56,
        "shhh",
        [((LOCAL, C, 128), BF)] + swap,
        [
            pltpu.SMEM((1, 1, NOFF, CAP), jnp.int32),
            ((1, SLOTS, C, 512), BF),
            ((512, 256), BF),
            pltpu.SemaphoreType.DMA((3,)),
        ],
        2 * 256 * 512 * 768,
        brick_count,
        send_list,
        features,
        face_packed,
    )
    received = [from_behind(b, tile, devices, o) for b, o in zip(outgoing, OFFSETS)]
    grad_active, conv_back = call(
        upper_kernel,
        56,
        "hhhh",
        [((SLOTS, C, 512), F32), ((192, 576), BF)],
        [
            ((1, SLOTS, 64, C2), BF),
            ((C2, 512), BF),
            ((C, 1728), BF),
            ((512, 128), BF),
            pltpu.SemaphoreType.DMA((4,)),
        ],
        10**9,
        out_grad,
        down_kernel,
        kernel,
        placing,
    )
    coarse, grad_preact, sums = call(
        main_kernel,
        53.8,
        "s" + "h" * 12,
        [
            ((1, SLOTS, 64, C2), BF),
            ((SLOTS, C, 512), BF),
            ((1536, 128), BF),
        ],
        [
            pltpu.SMEM((1, SLOTS, 26), jnp.int32),
            ((NOFF, CAP // 2, C, 128), BF),
            ((1, SLOTS, C, 512), BF),
            ((ALL_ROWS, 128), BF),
            ((C, 1728), BF),
            ((C2, 512), BF),
            ((1, SLOTS, 64, C2), BF),
            ((SLOTS, C, 512), F32),
            ((TABLE, C, 128), BF),
            ((TABLE, C, 128), BF),
            ((192, 576), BF),
            ((256, 14 * 128), BF),
            ((256, 1280), BF),
            ((2, 576, 1280), BF),
            ((192, 1280), BF),
            ((SLOTS, 64, 512), BF),
            ((192, 576), F32),
            pltpu.SemaphoreType.DMA((12,)),
        ],
        5 * 10**9,
        brick_count,
        halo_src,
        table,
        *received,
        features,
        placing,
        kernel,
        down_kernel,
        out_grad,
        grad_active,
    )
    part = near_sum(sums, sizes)
    folded, grad_local, *remote = call(
        fold_kernel,
        56,
        "shhh",
        [((256, 1024), F32), ((LOCAL, C, 128), F32)] + swap,
        [
            ((SLOTS, C, 512), BF),
            ((192, 576), BF),
            ((FOLD_ROWS, 128), BF),
            ((256, 1024), BF),
            ((576, 1024), BF),
            ((256, 1280), BF),
            ((256, 14 * 128), F32),
            ((TABLE, C, 128), F32),
            ((TABLE, C, 128), F32),
            pltpu.SemaphoreType.DMA((3,)),
        ],
        3 * 10**9,
        halo_src,
        grad_preact,
        conv_back,
        placing,
    )
    part, *remote = lax.optimization_barrier((part, *remote))
    part = gather_sum(part, ("z",), sizes["z"])
    returned = [from_behind(b, tile, devices, -o) for b, o in zip(remote, OFFSETS)]
    part, *returned = lax.optimization_barrier((part, *returned))
    sums = near_gather(part.astype(BF), sizes)
    (grad_features,) = call(
        finish_kernel,
        12,
        "ss" + "v" * 8,
        [((1, SLOTS, C, 512), BF)],
        [((LOCAL, C, 128), F32), ((256, 768), BF)],
        2 * 256 * 512 * 768,
        brick_count,
        send_list,
        folded,
        grad_local,
        *returned,
        face_hot,
        inner_hot,
    )
    grad_kernel, grad_down = call(
        unpack_kernel, 8, "v", [((C, 1728), F32), ((C2, 512), F32)], [], 10**6, sums
    )
    return coarse, grad_features, grad_kernel, grad_down


def solution(mesh):
    tile, grp = mesh.shape["tile"], mesh.shape["grp"]
    sizes = {"z": tile // 8, "x": 4, "c": 2, "grp": grp}
    fine = Mesh(mesh.devices.reshape(tuple(sizes.values())), tuple(sizes))
    line = ("z", "x", "c")
    in_specs = (
        P("grp", line, None, None),
        P("grp", line),
        P("grp", line, None, None),
        P("grp", line, None),
        P(),
        P(),
        P("grp", line, None, None),
    )
    out_specs = (P("grp", line, None, None), P("grp", line, None, None), P(), P())

    def step(*args):
        return on_device(sizes, *args)

    return jax.shard_map(step, mesh=fine, in_specs=in_specs, out_specs=out_specs, check_vma=False)
```

```python
import jax
import jax.numpy as jnp
import ml_dtypes
import numpy as np
from jax import lax
from jax.experimental import pallas as pl
from jax.experimental.pallas import tpu as pltpu
from jax.sharding import Mesh
from jax.sharding import PartitionSpec as P

BF = jnp.bfloat16
F32 = jnp.float32
DIRECTIONS = [
    (a, b, c) for a in (-1, 0, 1) for b in (-1, 0, 1) for c in (-1, 0, 1) if (a, b, c) != (0, 0, 0)
]
SHIFTS = [10 * b + c for b in (-1, 0, 1) for c in (-1, 0, 1)]
SLOTS, C, C2, NOFF, CAP = 4, 64, 128, 4, 4
LOCAL = 6 * SLOTS + 1
TABLE = LOCAL + NOFF * CAP
PLACES = list(range(9)) + [None] + list(range(9, 26)) + [None]
NEAR = ("x", "c", "grp")


def rim_cells(d, full):
    if d == -1:
        return [(7, 0)]
    if d == 1:
        return [(0, 9)]
    return [(i, i + 1) for i in range(full)]


def one_hot_tables():
    faces = np.zeros((512, 6, 128), np.float32)
    for x in range(8):
        for y in range(8):
            for z in range(8):
                v = (x, y, z)
                for a in range(3):
                    p, q = [v[i] for i in range(3) if i != a]
                    for e in range(2):
                        if v[a] == 7 * e:
                            faces[x * 64 + y * 8 + z, 2 * a + e, p * 8 + q] = 1
    inner = np.zeros((2, 64, 2, 128), np.float32)
    for s in range(2):
        for y in range(8):
            for z in range(8):
                inner[s, y * 8 + z, s, (y + 1) * 10 + z + 1] = 1
    cap = np.zeros((10, 64, 128), np.float32)
    side = np.zeros((8, 64, 128), np.float32)
    for m, d in enumerate([d for d in DIRECTIONS if d[0] == 0]):
        if d[1] != 0:
            yy = 0 if d[1] == -1 else 9
            for x in range(8):
                for i, zz in rim_cells(d[2], 8):
                    side[m, x * 8 + i, yy * 10 + zz] = 1
        else:
            zz = 0 if d[2] == -1 else 9
            for x in range(8):
                for y in range(8):
                    side[m, x * 8 + y, (y + 1) * 10 + zz] = 1
    for m, (dy, dz) in enumerate([(b, c) for b in (-1, 0, 1) for c in (-1, 0, 1)]):
        for i, yy in rim_cells(dy, 8):
            for k, zz in rim_cells(dz, 8):
                cap[m, i * 8 + k, yy * 10 + zz] = 1
    window = np.zeros((2, 128, 9, 2, 64), np.float32)
    for k, shift in enumerate(SHIFTS):
        for y in range(8):
            for z in range(8):
                for p in range(2):
                    window[p, (y + 1) * 10 + z + 1 + shift, k, p, y * 8 + z] = 1
    spread = np.zeros((4, 4, 4, 2, 2, 4, 64), np.float32)
    pick = np.zeros((2, 2, 2, 4, 4, 2, 64), np.float32)
    for ty in range(2):
        for tz in range(2):
            for Y in range(4):
                for Z in range(4):
                    lane = (2 * Y + ty) * 8 + 2 * Z + tz
                    for X in range(4):
                        spread[X, Y, Z, ty, tz, X, lane] = 1
                    for tx in range(2):
                        pick[tx, ty, tz, Y, Z, tx, lane] = 1
    def stacked(table):
        rows, lanes = table.shape
        return table.reshape(rows, lanes // 128, 128).transpose(1, 0, 2).reshape(-1, 128)

    placing = np.concatenate(
        [
            cap.reshape(640, 128),
            side.reshape(512, 128),
            stacked(inner.reshape(128, 256)),
            pick.reshape(128, 128),
            stacked(spread.reshape(64, 1024)),
            stacked(window.reshape(256, 1152)),
        ]
    )
    b = ml_dtypes.bfloat16
    packed = faces[:, 2:, :64].reshape(512, 256)
    inner = inner.reshape(128, 256)
    return packed.astype(b), faces.reshape(512, 768).astype(b), inner.astype(b), placing.astype(b)


CAP_ROWS, SIDE_ROWS, INNER_ROWS, PICK_ROWS, SPREAD_ROWS = 0, 640, 1152, 1408, 1536
WINDOW_ROWS, FOLD_ROWS, ALL_ROWS = 2048, 1408, 4352


def tiles_of(table, start, rows, first, count):
    blocks = [table[start + (first + i) * rows : start + (first + i + 1) * rows] for i in range(count)]
    return jnp.concatenate(blocks, axis=1)


def side_tiles(table, first, count):
    side = table[SIDE_ROWS : SIDE_ROWS + 512]
    plane = (lax.broadcasted_iota(jnp.int32, (512, 128), 0) // 8) % 8
    return jnp.concatenate(
        [jnp.where(plane == first + i, side, jnp.zeros_like(side)) for i in range(count)], axis=1
    )


def low_lanes(shape):
    return lax.broadcasted_iota(jnp.int32, shape, 1) < 64


def nn(a, b):
    return jnp.dot(a, b, preferred_element_type=F32)


def nt(a, b):
    return lax.dot_general(a, b, (((1,), (1,)), ((), ())), preferred_element_type=F32)


def masked_rows(features, count):
    return jnp.concatenate(
        [features[0, s] * jnp.where(s < count, 1.0, 0.0).astype(BF) for s in range(SLOTS)], axis=0
    )


def fetch(sources, targets, done):
    copies = [
        pltpu.make_async_copy(a, b, done.at[i]) for i, (a, b) in enumerate(zip(sources, targets))
    ]
    for copy in copies:
        copy.start()
    return copies


def wait(copies):
    for copy in copies:
        copy.wait()


def partners(mine):
    first = lax.axis_index("c") == (0 if mine else 1)
    second = lax.axis_index("x") % 2 == (0 if mine else 1)
    return (
        jnp.where(second, 3, 2),
        jnp.where(second, 2, 3),
        jnp.where(first, 1, 0),
        jnp.where(first, 0, 1),
    )


def faces_kernel(
    count, sends_far, features_far, face_far, table, *rest
):
    outgoing, (sends, features, face_hot, done) = rest[:NOFF], rest[NOFF:]
    wait(fetch((features_far, face_far, sends_far), (features, face_hot, sends), done))
    masked = masked_rows(features, count[0, 0])
    low = low_lanes((SLOTS * C, 128))
    none = jnp.zeros((SLOTS * C, 128), BF)
    found = nn(masked, face_hot[...]).astype(BF)
    pairs = (found[:, 0:128], found[:, 128:256])
    layers = [masked[:, 0:128], pltpu.roll(masked[:, 384:512], 64, 1)]
    for block in pairs:
        layers += [block, pltpu.roll(block, 64, 1)]
    for f in range(6):
        layer = jnp.where(low, layers[f], none)
        for s in range(SLOTS):
            table[6 * s + f] = layer[s * C : (s + 1) * C]
    table[6 * SLOTS] = jnp.zeros((C, 128), BF)
    for p, j in enumerate(partners(True)):
        for q in range(CAP // 2):
            high = table[sends[0, 0, j, 2 * q + 1]]
            outgoing[p][q] = table[sends[0, 0, j, 2 * q]] + pltpu.roll(high, 64, 1)


def upper_kernel(
    out_far,
    down_far,
    kernel_far,
    placing_far,
    grad_active,
    conv_back,
    out_grad,
    down_kernel,
    kernel,
    spread_rows,
    done,
):
    spread_far = placing_far.at[SPREAD_ROWS : SPREAD_ROWS + 512]
    copies = fetch(
        (out_far, down_far, spread_far, kernel_far),
        (out_grad, down_kernel, spread_rows, kernel),
        done,
    )
    wait(copies[:3])
    turned = jnp.concatenate(
        [jnp.transpose(out_grad[0, s].astype(F32)).astype(BF) for s in range(SLOTS)], axis=0
    )
    spread = nn(turned, tiles_of(spread_rows, 0, 64, 0, 8)).astype(BF)
    tall = jnp.transpose(down_kernel[...].astype(F32)).astype(BF)
    down_rows = jnp.concatenate(
        [
            jnp.concatenate([tall[(4 * tx + t) * C : (4 * tx + t + 1) * C] for t in range(4)], axis=1)
            for tx in range(2)
        ],
        axis=0,
    )
    for s in range(SLOTS):
        rows = slice(s * C2, (s + 1) * C2)
        block = jnp.concatenate([spread[rows, t * 256 : (t + 1) * 256] for t in range(4)], axis=0)
        grown = nn(down_rows, block)
        grad_active[s] = jnp.concatenate(
            [
                grown[tx * C : (tx + 1) * C, X * 64 : (X + 1) * 64]
                for X in range(4)
                for tx in range(2)
            ],
            axis=1,
        )
    wait(copies[3:])
    tall = jnp.transpose(kernel[...].astype(F32)).astype(BF)
    for o in range(3):
        conv_back[o * C : (o + 1) * C] = jnp.concatenate(
            [tall[(9 * o + k) * C : (9 * o + k + 1) * C] for k in range(9)], axis=1
        )


def main_kernel(
    count,
    sources_far,
    table,
    from_a,
    from_b,
    from_c,
    from_d,
    features_far,
    placing_far,
    kernel_far,
    down_far,
    out_far,
    active_far,
    coarse,
    grad_preact,
    sums,
    sources,
    arrived,
    features,
    placing,
    kernel,
    down_kernel,
    out_grad,
    grad_active,
    halo,
    halo_high,
    conv,
    entries,
    padded,
    stack,
    shifted,
    lowered,
    total,
    done,
):
    copies = fetch(
        (from_a, from_b, from_c, from_d, table, sources_far)
        + (features_far, placing_far, kernel_far, down_far, out_far, active_far),
        [arrived.at[j] for j in range(NOFF)]
        + [halo.at[0:LOCAL], sources, features, placing, kernel, down_kernel, out_grad]
        + [grad_active],
        done,
    )
    wait(copies[: NOFF + 2])
    low = low_lanes((C, 128))
    none = jnp.zeros((C, 128), BF)
    halo_high[0:LOCAL] = pltpu.roll(
        halo[0:LOCAL].reshape(LOCAL * C, 128), 64, 1
    ).reshape(LOCAL, C, 128)
    for p, j in enumerate(partners(False)):
        for q in range(CAP // 2):
            block, place = arrived[p, q], LOCAL + j * CAP + 2 * q
            turned = pltpu.roll(block, 64, 1)
            halo[place] = jnp.where(low, block, none)
            halo[place + 1] = jnp.where(low, turned, none)
            halo_high[place] = jnp.where(low, none, turned)
            halo_high[place + 1] = jnp.where(low, none, block)
    for s in range(SLOTS):
        for t in range(14):
            even, odd = PLACES[2 * t], PLACES[2 * t + 1]
            block = halo[sources[0, s, even]]
            if odd is not None:
                block = block + halo_high[sources[0, s, odd]]
            entries[s * C : (s + 1) * C, t * 128 : (t + 1) * 128] = block
    wait(copies[NOFF + 2 :])
    cap_hot = placing[CAP_ROWS : CAP_ROWS + 640]
    inner_hot = tiles_of(placing, INNER_ROWS, 128, 0, 2)
    pick_hot = placing[PICK_ROWS : PICK_ROWS + 128]
    masked = masked_rows(features, count[0, 0])
    padded[:, 0:128] = nn(entries[:, 0:640], cap_hot).astype(BF)
    padded[:, 1152:1280] = nn(entries[:, 1152:1792], cap_hot).astype(BF)
    for i in range(4):
        block = nn(entries[:, 640:1152], side_tiles(placing, 2 * i, 2))
        block = block + nn(masked[:, i * 128 : (i + 1) * 128], inner_hot)
        padded[:, 128 + i * 256 : 384 + i * 256] = block.astype(BF)
    window_hot = tiles_of(placing, WINDOW_ROWS, 256, 0, 9)
    for i in range(5):
        planes = nn(padded[:, i * 256 : (i + 1) * 256], window_hot).astype(BF)
        for s in range(SLOTS):
            lanes = slice((s % 2) * 640 + i * 128, (s % 2) * 640 + (i + 1) * 128)
            for k in range(9):
                block = planes[s * C : (s + 1) * C, k * 128 : (k + 1) * 128]
                stack[s // 2, k * C : (k + 1) * C, lanes] = block

    for o in range(3):
        conv[o * C : (o + 1) * C] = kernel[:, o * 576 : (o + 1) * 576]
    left = low_lanes((16, 128))
    edge = jnp.zeros((C, 64), BF)
    wide = jnp.zeros((C, 128), BF)
    total[...] = jnp.zeros_like(total)

    def pair(p, carry):
        triple = nn(conv[...], stack[p])
        for j in range(2):
            s = 2 * p + j
            filled = jnp.where(s < count[0, 0], 1.0, 0.0).astype(F32)
            base = j * 640
            preact = (
                triple[0:C, base : base + 512]
                + triple[C : 2 * C, base + 64 : base + 576]
                + triple[2 * C :, base + 128 : base + 640]
            )
            sigmoid = jax.nn.sigmoid(preact)
            active = (preact * sigmoid * filled).astype(BF)
            for h in range(2):
                halves = [active[:, (2 * h + i) * 128 : (2 * h + i + 1) * 128] for i in range(2)]
                rows = jnp.concatenate([halves[0], halves[0], halves[1], halves[1]], axis=0)
                picked = nt(pick_hot, rows)
                for i in range(2):
                    X = 2 * h + i
                    for q in range(4):
                        lanes = slice(i * 128, (i + 1) * 128)
                        block = jnp.where(
                            left,
                            picked[32 * q : 32 * q + 16, lanes],
                            picked[32 * q + 16 : 32 * q + 32, lanes],
                        )
                        lowered[s, X * 16 : (X + 1) * 16, q * 128 : (q + 1) * 128] = block.astype(BF)
            grads = grad_active[s] * sigmoid * (1.0 + preact * (1.0 - sigmoid)) * filled
            grads = grads.astype(BF)
            grad_preact[s] = grads
            shifted[0:C, base : base + 640] = jnp.concatenate([grads, wide], axis=1)
            shifted[C : 2 * C, base : base + 640] = jnp.concatenate([edge, grads, edge], axis=1)
            shifted[2 * C :, base : base + 640] = jnp.concatenate([wide, grads], axis=1)
        total[...] += nt(shifted[...], stack[p])
        return carry

    lax.fori_loop(0, SLOTS // 2, pair, 0)
    rows = lowered[...].reshape(SLOTS * 64, 512)
    coarse[...] = nt(rows, down_kernel[...]).astype(BF).reshape(coarse.shape)
    turned = jnp.transpose(out_grad[...].reshape(SLOTS * 64, C2).astype(F32)).astype(BF)
    grad_down = nn(turned, rows)
    for j in range(5):
        width = min(128, 576 - j * 128)
        sums[j * 192 : (j + 1) * 192, 0:width] = total[:, j * 128 : j * 128 + width].astype(BF)
    sums[4 * 192 : 5 * 192, 64:128] = jnp.zeros((192, 64), BF)
    for j in range(4):
        sums[960 + j * C2 : 960 + (j + 1) * C2] = grad_down[:, j * 128 : (j + 1) * 128].astype(BF)
    sums[1472:1536] = jnp.zeros((64, 128), BF)


def fold_kernel(
    sources,
    grads_far,
    conv_far,
    placing_far,
    folded,
    grad_local,
    to_four_a,
    to_four_b,
    to_four_c,
    to_four_d,
    grad_preact,
    conv_back,
    placing,
    planes,
    stack,
    high,
    rims,
    grad_table,
    grad_table_high,
    done,
):
    copies = fetch(
        (grads_far, placing_far.at[0:FOLD_ROWS], conv_far), (grad_preact, placing, conv_back), done
    )
    grad_table[...] = jnp.zeros_like(grad_table)
    grad_table_high[...] = jnp.zeros_like(grad_table_high)
    wait(copies[:2])
    cap_hot = placing[CAP_ROWS : CAP_ROWS + 640]
    inner_hot = tiles_of(placing, INNER_ROWS, 128, 0, 2)
    rows = grad_preact[...].reshape(SLOTS * C, 512)
    for i in range(4):
        block = nn(rows[:, i * 128 : (i + 1) * 128], inner_hot)
        planes[:, i * 256 : (i + 1) * 256] = block.astype(BF)
    wait(copies[2:])

    def brick(s, carry):
        here = pl.ds(pl.multiple_of(s * C, C), C)
        for x in range(8):
            plane = planes[here, x * 128 : (x + 1) * 128]
            for k, shift in enumerate(SHIFTS):
                moved = plane if shift == 0 else pltpu.roll(plane, shift % 128, 1)
                stack[k * C : (k + 1) * C, x * 128 : (x + 1) * 128] = moved
        triple = nn(conv_back[...], stack[...])
        for x in range(10):
            value = None
            for o in range(3):
                if 0 <= x - o < 8:
                    part = triple[o * C : (o + 1) * C, (x - o) * 128 : (x - o + 1) * 128]
                    value = part if value is None else value + part
            high[here, x * 128 : (x + 1) * 128] = value.astype(BF)
            if 1 <= x <= 8:
                folded[here, (x - 1) * 128 : x * 128] = value
        return carry

    lax.fori_loop(0, SLOTS, brick, 0)
    rims[:, 0:640] = nt(high[:, 0:128], cap_hot)
    rims[:, 640:1152] = nt(high[:, 128:1152], side_tiles(placing, 0, 8))
    rims[:, 1152:1792] = nt(high[:, 1152:1280], cap_hot)
    for s in range(SLOTS):
        for t in range(14):
            block = rims[s * C : (s + 1) * C, t * 128 : (t + 1) * 128]
            grad_table[sources[0, s, PLACES[2 * t]]] += block
            if PLACES[2 * t + 1] is not None:
                grad_table_high[sources[0, s, PLACES[2 * t + 1]]] += block
    turned = pltpu.roll(grad_table_high[...].reshape(TABLE * C, 128), 64, 1)
    grad_table[...] += turned.reshape(TABLE, C, 128)
    grad_local[...] = grad_table[0:LOCAL]
    left = low_lanes((C, 128))
    for p, j in enumerate(partners(False)):
        for q in range(CAP // 2):
            place = LOCAL + j * CAP + 2 * q
            block = jnp.where(left, grad_table[place], pltpu.roll(grad_table[place + 1], 64, 1))
            (to_four_a, to_four_b, to_four_c, to_four_d)[p][q] = block.astype(BF)


def unpack_kernel(sums, grad_kernel, grad_down):
    parts = []
    for o in range(3):
        tiles = [sums[j * 192 + o * C : j * 192 + (o + 1) * C].astype(F32) for j in range(5)]
        parts.append(jnp.concatenate(tiles, axis=1)[:, :576])
    grad_kernel[...] = jnp.concatenate(parts, axis=1)
    tiles = [sums[960 + t * C2 : 960 + (t + 1) * C2].astype(F32) for t in range(4)]
    grad_down[...] = jnp.concatenate(tiles, axis=1)


def finish_kernel(
    count,
    sends,
    folded,
    grad_local,
    from_a,
    from_b,
    from_c,
    from_d,
    face_hot,
    inner_hot,
    grad_features,
    table,
    layers,
):
    table[...] = grad_local[...]
    for p, j in enumerate(partners(True)):
        for q in range(CAP // 2):
            block = (from_a, from_b, from_c, from_d)[p][q].astype(F32)
            table[sends[0, 0, j, 2 * q]] += block
            table[sends[0, 0, j, 2 * q + 1]] += pltpu.roll(block, 64, 1)
    for s in range(SLOTS):
        for f in range(6):
            layers[s * C : (s + 1) * C, f * 128 : (f + 1) * 128] = table[6 * s + f].astype(BF)
    tiles = []
    for i in range(4):
        value = folded[:, i * 256 : (i + 1) * 256]
        top = value.astype(BF)
        rest = (value - top.astype(F32)).astype(BF)
        tiles.append(nt(top, inner_hot[...]) + nt(rest, inner_hot[...]))
    whole = jnp.concatenate(tiles, axis=1) + nt(layers[...], face_hot[...])
    for s in range(SLOTS):
        filled = jnp.where(s < count[0, 0], 1.0, 0.0).astype(F32)
        grad_features[0, s] = (whole[s * C : (s + 1) * C] * filled).astype(BF)


def call(kernel, limit, memories, outs, scratch, flops, *args):
    where = {"s": pltpu.SMEM, "v": pltpu.VMEM, "h": pltpu.HBM}
    return pl.pallas_call(
        kernel,
        in_specs=[pl.BlockSpec(memory_space=where[m]) for m in memories],
        out_specs=[pl.BlockSpec(memory_space=pltpu.VMEM) for _ in outs],
        out_shape=[jax.ShapeDtypeStruct(s, d) for s, d in outs],
        scratch_shapes=[pltpu.VMEM(*s) if isinstance(s, tuple) else s for s in scratch],
        compiler_params=pltpu.CompilerParams(vmem_limit_bytes=int(limit * 2**20)),
        cost_estimate=pl.CostEstimate(flops=flops, bytes_accessed=2**20, transcendentals=0),
        name=kernel.__name__,
    )(*args)


def gather_sum(block, axes, parts):
    copies = jnp.broadcast_to(block[None], (parts,) + block.shape)
    got = lax.all_to_all(copies, axes, 0, 0)
    return got.astype(F32).sum(0)


def near_sum(block, sizes):
    parts = sizes["x"] * sizes["c"] * sizes["grp"]
    rows = block.shape[0] // parts
    got = lax.all_to_all(block.reshape(parts, rows, 128), NEAR, 0, 0)
    return got.astype(F32).sum(0).astype(BF)


def near_gather(block, sizes):
    parts = sizes["x"] * sizes["c"] * sizes["grp"]
    copies = jnp.broadcast_to(block[None], (parts,) + block.shape)
    return lax.all_to_all(copies, NEAR, 0, 0).reshape(parts * block.shape[0], 128)


def swap(blocks, axes, devices):
    pairs = [
        [(t, t + 2) for t in range(devices - 2) if t % 4 >= 2],
        [(t, t + 2) for t in range(devices - 2) if t % 4 < 2],
        [(t, t + 1) for t in range(devices - 1) if t % 2 == 1],
        [(t, t + 1) for t in range(devices - 1) if t % 2 == 0],
    ]
    routes = [two + [(b, a) for a, b in two] for two in pairs]
    return [lax.ppermute(block, axes, route) for block, route in zip(blocks, routes)]


def on_device(sizes, features, brick_count, send_list, halo_src, kernel, down_kernel, out_grad):
    face_packed, face_hot, inner_hot, placing = one_hot_tables()
    tile = ("z", "x", "c")
    devices = sizes["z"] * sizes["x"] * sizes["c"]
    blocks = [((CAP // 2, C, 128), BF)] * NOFF

    table, *outgoing = call(
        faces_kernel,
        56,
        "shhh",
        [((LOCAL, C, 128), BF)] + blocks,
        [
            pltpu.SMEM((1, 1, NOFF, CAP), jnp.int32),
            ((1, SLOTS, C, 512), BF),
            ((512, 256), BF),
            pltpu.SemaphoreType.DMA((3,)),
        ],
        2 * 256 * 512 * 768,
        brick_count,
        send_list,
        features,
        face_packed,
    )
    received = swap(outgoing, tile, devices)
    grad_active, conv_back = call(
        upper_kernel,
        56,
        "hhhh",
        [((SLOTS, C, 512), F32), ((192, 576), BF)],
        [
            ((1, SLOTS, 64, C2), BF),
            ((C2, 512), BF),
            ((C, 1728), BF),
            ((512, 128), BF),
            pltpu.SemaphoreType.DMA((4,)),
        ],
        10**9,
        out_grad,
        down_kernel,
        kernel,
        placing,
    )
    coarse, grad_preact, sums = call(
        main_kernel,
        53.8,
        "s" + "h" * 12,
        [
            ((1, SLOTS, 64, C2), BF),
            ((SLOTS, C, 512), BF),
            ((1536, 128), BF),
        ],
        [
            pltpu.SMEM((1, SLOTS, 26), jnp.int32),
            ((NOFF, CAP // 2, C, 128), BF),
            ((1, SLOTS, C, 512), BF),
            ((ALL_ROWS, 128), BF),
            ((C, 1728), BF),
            ((C2, 512), BF),
            ((1, SLOTS, 64, C2), BF),
            ((SLOTS, C, 512), F32),
            ((TABLE, C, 128), BF),
            ((TABLE, C, 128), BF),
            ((192, 576), BF),
            ((256, 14 * 128), BF),
            ((256, 1280), BF),
            ((2, 576, 1280), BF),
            ((192, 1280), BF),
            ((SLOTS, 64, 512), BF),
            ((192, 576), F32),
            pltpu.SemaphoreType.DMA((12,)),
        ],
        5 * 10**9,
        brick_count,
        halo_src,
        table,
        *received,
        features,
        placing,
        kernel,
        down_kernel,
        out_grad,
        grad_active,
    )
    part = near_sum(sums, sizes)
    folded, grad_local, *remote = call(
        fold_kernel,
        56,
        "shhh",
        [((256, 1024), F32), ((LOCAL, C, 128), F32)] + blocks,
        [
            ((SLOTS, C, 512), BF),
            ((192, 576), BF),
            ((FOLD_ROWS, 128), BF),
            ((256, 1024), BF),
            ((576, 1024), BF),
            ((256, 1280), BF),
            ((256, 14 * 128), F32),
            ((TABLE, C, 128), F32),
            ((TABLE, C, 128), F32),
            pltpu.SemaphoreType.DMA((3,)),
        ],
        3 * 10**9,
        halo_src,
        grad_preact,
        conv_back,
        placing,
    )
    part, *remote = lax.optimization_barrier((part, *remote))
    part = gather_sum(part, ("z",), sizes["z"])
    returned = swap(remote, tile, devices)
    part, *returned = lax.optimization_barrier((part, *returned))
    sums = near_gather(part.astype(BF), sizes)
    (grad_features,) = call(
        finish_kernel,
        12,
        "ss" + "v" * 8,
        [((1, SLOTS, C, 512), BF)],
        [((LOCAL, C, 128), F32), ((256, 768), BF)],
        2 * 256 * 512 * 768,
        brick_count,
        send_list,
        folded,
        grad_local,
        *returned,
        face_hot,
        inner_hot,
    )
    grad_kernel, grad_down = call(
        unpack_kernel, 8, "v", [((C, 1728), F32), ((C2, 512), F32)], [], 10**6, sums
    )
    return coarse, grad_features, grad_kernel, grad_down


def solution(mesh):
    tile, grp = mesh.shape["tile"], mesh.shape["grp"]
    sizes = {"z": tile // 8, "x": 4, "c": 2, "grp": grp}
    fine = Mesh(mesh.devices.reshape(tuple(sizes.values())), tuple(sizes))
    line = ("z", "x", "c")
    in_specs = (
        P("grp", line, None, None),
        P("grp", line),
        P("grp", line, None, None),
        P("grp", line, None),
        P(),
        P(),
        P("grp", line, None, None),
    )
    out_specs = (P("grp", line, None, None), P("grp", line, None, None), P(), P())

    def step(*args):
        return on_device(sizes, *args)

    return jax.shard_map(step, mesh=fine, in_specs=in_specs, out_specs=out_specs, check_vma=False)
```

```python
import jax
import jax.numpy as jnp
import ml_dtypes
import numpy as np
from jax import lax
from jax.experimental import pallas as pl
from jax.experimental.pallas import tpu as pltpu
from jax.sharding import Mesh
from jax.sharding import PartitionSpec as P

BF = jnp.bfloat16
F32 = jnp.float32
DIRECTIONS = [
    (a, b, c) for a in (-1, 0, 1) for b in (-1, 0, 1) for c in (-1, 0, 1) if (a, b, c) != (0, 0, 0)
]
SHIFTS = [10 * b + c for b in (-1, 0, 1) for c in (-1, 0, 1)]
SLOTS, C, C2, NOFF, CAP = 4, 64, 128, 4, 4
LOCAL = 6 * SLOTS + 1
TABLE = LOCAL + NOFF * CAP
PLACES = list(range(9)) + [None] + list(range(9, 26)) + [None]
NEAR = ("x", "c", "grp")


def rim_cells(d, full):
    if d == -1:
        return [(7, 0)]
    if d == 1:
        return [(0, 9)]
    return [(i, i + 1) for i in range(full)]


def one_hot_tables():
    faces = np.zeros((512, 6, 128), np.float32)
    for x in range(8):
        for y in range(8):
            for z in range(8):
                v = (x, y, z)
                for a in range(3):
                    p, q = [v[i] for i in range(3) if i != a]
                    for e in range(2):
                        if v[a] == 7 * e:
                            faces[x * 64 + y * 8 + z, 2 * a + e, p * 8 + q] = 1
    inner = np.zeros((2, 64, 2, 128), np.float32)
    for s in range(2):
        for y in range(8):
            for z in range(8):
                inner[s, y * 8 + z, s, (y + 1) * 10 + z + 1] = 1
    cap = np.zeros((10, 64, 128), np.float32)
    side = np.zeros((8, 64, 128), np.float32)
    for m, d in enumerate([d for d in DIRECTIONS if d[0] == 0]):
        if d[1] != 0:
            yy = 0 if d[1] == -1 else 9
            for x in range(8):
                for i, zz in rim_cells(d[2], 8):
                    side[m, x * 8 + i, yy * 10 + zz] = 1
        else:
            zz = 0 if d[2] == -1 else 9
            for x in range(8):
                for y in range(8):
                    side[m, x * 8 + y, (y + 1) * 10 + zz] = 1
    for m, (dy, dz) in enumerate([(b, c) for b in (-1, 0, 1) for c in (-1, 0, 1)]):
        for i, yy in rim_cells(dy, 8):
            for k, zz in rim_cells(dz, 8):
                cap[m, i * 8 + k, yy * 10 + zz] = 1
    window = np.zeros((2, 128, 9, 2, 64), np.float32)
    for k, shift in enumerate(SHIFTS):
        for y in range(8):
            for z in range(8):
                for p in range(2):
                    window[p, (y + 1) * 10 + z + 1 + shift, k, p, y * 8 + z] = 1
    spread = np.zeros((4, 4, 4, 2, 2, 4, 64), np.float32)
    pick = np.zeros((2, 2, 2, 4, 4, 2, 64), np.float32)
    for ty in range(2):
        for tz in range(2):
            for Y in range(4):
                for Z in range(4):
                    lane = (2 * Y + ty) * 8 + 2 * Z + tz
                    for X in range(4):
                        spread[X, Y, Z, ty, tz, X, lane] = 1
                    for tx in range(2):
                        pick[tx, ty, tz, Y, Z, tx, lane] = 1
    def stacked(table):
        rows, lanes = table.shape
        return table.reshape(rows, lanes // 128, 128).transpose(1, 0, 2).reshape(-1, 128)

    placing = np.concatenate(
        [
            cap.reshape(640, 128),
            side.reshape(512, 128),
            stacked(inner.reshape(128, 256)),
            pick.reshape(128, 128),
            stacked(spread.reshape(64, 1024)),
            stacked(window.reshape(256, 1152)),
        ]
    )
    b = ml_dtypes.bfloat16
    packed = faces[:, 2:, :64].reshape(512, 256)
    inner = inner.reshape(128, 256)
    return packed.astype(b), faces.reshape(512, 768).astype(b), inner.astype(b), placing.astype(b)


CAP_ROWS, SIDE_ROWS, INNER_ROWS, PICK_ROWS, SPREAD_ROWS = 0, 640, 1152, 1408, 1536
WINDOW_ROWS, FOLD_ROWS, ALL_ROWS = 2048, 1408, 4352


def tiles_of(table, start, rows, first, count):
    blocks = [table[start + (first + i) * rows : start + (first + i + 1) * rows] for i in range(count)]
    return jnp.concatenate(blocks, axis=1)


def side_tiles(table, first, count):
    side = table[SIDE_ROWS : SIDE_ROWS + 512]
    plane = (lax.broadcasted_iota(jnp.int32, (512, 128), 0) // 8) % 8
    return jnp.concatenate(
        [jnp.where(plane == first + i, side, jnp.zeros_like(side)) for i in range(count)], axis=1
    )


def low_lanes(shape):
    return lax.broadcasted_iota(jnp.int32, shape, 1) < 64


def nn(a, b):
    return jnp.dot(a, b, preferred_element_type=F32)


def nt(a, b):
    return lax.dot_general(a, b, (((1,), (1,)), ((), ())), preferred_element_type=F32)


def masked_rows(features, count):
    return jnp.concatenate(
        [features[0, s] * jnp.where(s < count, 1.0, 0.0).astype(BF) for s in range(SLOTS)], axis=0
    )


def fetch(sources, targets, done):
    copies = [
        pltpu.make_async_copy(a, b, done.at[i]) for i, (a, b) in enumerate(zip(sources, targets))
    ]
    for copy in copies:
        copy.start()
    return copies


def wait(copies):
    for copy in copies:
        copy.wait()


def partners(mine):
    first = lax.axis_index("c") == (0 if mine else 1)
    second = lax.axis_index("x") % 2 == (0 if mine else 1)
    return (
        jnp.where(second, 3, 2),
        jnp.where(second, 2, 3),
        jnp.where(first, 1, 0),
        jnp.where(first, 0, 1),
    )


def faces_kernel(
    count, sends_far, features_far, face_far, table, *rest
):
    outgoing, (sends, features, face_hot, done) = rest[:NOFF], rest[NOFF:]
    wait(fetch((features_far, face_far, sends_far), (features, face_hot, sends), done))
    masked = masked_rows(features, count[0, 0])
    low = low_lanes((SLOTS * C, 128))
    none = jnp.zeros((SLOTS * C, 128), BF)
    found = nn(masked, face_hot[...]).astype(BF)
    pairs = (found[:, 0:128], found[:, 128:256])
    layers = [masked[:, 0:128], pltpu.roll(masked[:, 384:512], 64, 1)]
    for block in pairs:
        layers += [block, pltpu.roll(block, 64, 1)]
    for f in range(6):
        layer = jnp.where(low, layers[f], none)
        for s in range(SLOTS):
            table[6 * s + f] = layer[s * C : (s + 1) * C]
    table[6 * SLOTS] = jnp.zeros((C, 128), BF)
    for p, j in enumerate(partners(True)):
        for q in range(CAP // 2):
            high = table[sends[0, 0, j, 2 * q + 1]]
            outgoing[p][q] = table[sends[0, 0, j, 2 * q]] + pltpu.roll(high, 64, 1)


def upper_kernel(
    out_far,
    down_far,
    kernel_far,
    placing_far,
    grad_active,
    conv_back,
    out_grad,
    down_kernel,
    kernel,
    spread_rows,
    done,
):
    spread_far = placing_far.at[SPREAD_ROWS : SPREAD_ROWS + 512]
    copies = fetch(
        (out_far, down_far, spread_far, kernel_far),
        (out_grad, down_kernel, spread_rows, kernel),
        done,
    )
    wait(copies[:3])
    turned = jnp.concatenate(
        [jnp.transpose(out_grad[0, s].astype(F32)).astype(BF) for s in range(SLOTS)], axis=0
    )
    spread = nn(turned, tiles_of(spread_rows, 0, 64, 0, 8)).astype(BF)
    tall = jnp.transpose(down_kernel[...].astype(F32)).astype(BF)
    down_rows = jnp.concatenate(
        [
            jnp.concatenate([tall[(4 * tx + t) * C : (4 * tx + t + 1) * C] for t in range(4)], axis=1)
            for tx in range(2)
        ],
        axis=0,
    )
    for s in range(SLOTS):
        rows = slice(s * C2, (s + 1) * C2)
        block = jnp.concatenate([spread[rows, t * 256 : (t + 1) * 256] for t in range(4)], axis=0)
        grown = nn(down_rows, block)
        grad_active[s] = jnp.concatenate(
            [
                grown[tx * C : (tx + 1) * C, X * 64 : (X + 1) * 64]
                for X in range(4)
                for tx in range(2)
            ],
            axis=1,
        )
    wait(copies[3:])
    tall = jnp.transpose(kernel[...].astype(F32)).astype(BF)
    for o in range(3):
        conv_back[o * C : (o + 1) * C] = jnp.concatenate(
            [tall[(9 * o + k) * C : (9 * o + k + 1) * C] for k in range(9)], axis=1
        )


def main_kernel(
    count,
    sources_far,
    table,
    from_a,
    from_b,
    from_c,
    from_d,
    features_far,
    placing_far,
    kernel_far,
    down_far,
    out_far,
    active_far,
    coarse,
    grad_preact,
    sums,
    sources,
    arrived,
    features,
    placing,
    kernel,
    down_kernel,
    out_grad,
    grad_active,
    halo,
    halo_high,
    conv,
    entries,
    padded,
    stack,
    shifted,
    lowered,
    total,
    done,
):
    copies = fetch(
        (from_a, from_b, from_c, from_d, table, sources_far)
        + (features_far, placing_far, kernel_far, down_far, out_far, active_far),
        [arrived.at[j] for j in range(NOFF)]
        + [halo.at[0:LOCAL], sources, features, placing, kernel, down_kernel, out_grad]
        + [grad_active],
        done,
    )
    wait(copies[: NOFF + 2])
    low = low_lanes((C, 128))
    none = jnp.zeros((C, 128), BF)
    halo_high[0:LOCAL] = pltpu.roll(
        halo[0:LOCAL].reshape(LOCAL * C, 128), 64, 1
    ).reshape(LOCAL, C, 128)
    for p, j in enumerate(partners(False)):
        for q in range(CAP // 2):
            block, place = arrived[p, q], LOCAL + j * CAP + 2 * q
            turned = pltpu.roll(block, 64, 1)
            halo[place] = jnp.where(low, block, none)
            halo[place + 1] = jnp.where(low, turned, none)
            halo_high[place] = jnp.where(low, none, turned)
            halo_high[place + 1] = jnp.where(low, none, block)
    for s in range(SLOTS):
        for t in range(14):
            even, odd = PLACES[2 * t], PLACES[2 * t + 1]
            block = halo[sources[0, s, even]]
            if odd is not None:
                block = block + halo_high[sources[0, s, odd]]
            entries[s * C : (s + 1) * C, t * 128 : (t + 1) * 128] = block
    wait(copies[NOFF + 2 :])
    cap_hot = placing[CAP_ROWS : CAP_ROWS + 640]
    inner_hot = tiles_of(placing, INNER_ROWS, 128, 0, 2)
    pick_hot = placing[PICK_ROWS : PICK_ROWS + 128]
    masked = masked_rows(features, count[0, 0])
    padded[:, 0:128] = nn(entries[:, 0:640], cap_hot).astype(BF)
    padded[:, 1152:1280] = nn(entries[:, 1152:1792], cap_hot).astype(BF)
    for i in range(4):
        block = nn(entries[:, 640:1152], side_tiles(placing, 2 * i, 2))
        block = block + nn(masked[:, i * 128 : (i + 1) * 128], inner_hot)
        padded[:, 128 + i * 256 : 384 + i * 256] = block.astype(BF)
    window_hot = tiles_of(placing, WINDOW_ROWS, 256, 0, 9)
    for i in range(5):
        planes = nn(padded[:, i * 256 : (i + 1) * 256], window_hot).astype(BF)
        for s in range(SLOTS):
            lanes = slice((s % 2) * 640 + i * 128, (s % 2) * 640 + (i + 1) * 128)
            for k in range(9):
                block = planes[s * C : (s + 1) * C, k * 128 : (k + 1) * 128]
                stack[s // 2, k * C : (k + 1) * C, lanes] = block

    for o in range(3):
        conv[o * C : (o + 1) * C] = kernel[:, o * 576 : (o + 1) * 576]
    left = low_lanes((16, 128))
    edge = jnp.zeros((C, 64), BF)
    wide = jnp.zeros((C, 128), BF)
    total[...] = jnp.zeros_like(total)

    def pair(p, carry):
        triple = nn(conv[...], stack[p])
        for j in range(2):
            s = 2 * p + j
            filled = jnp.where(s < count[0, 0], 1.0, 0.0).astype(F32)
            base = j * 640
            preact = (
                triple[0:C, base : base + 512]
                + triple[C : 2 * C, base + 64 : base + 576]
                + triple[2 * C :, base + 128 : base + 640]
            )
            sigmoid = jax.nn.sigmoid(preact)
            active = (preact * sigmoid * filled).astype(BF)
            for h in range(2):
                halves = [active[:, (2 * h + i) * 128 : (2 * h + i + 1) * 128] for i in range(2)]
                rows = jnp.concatenate([halves[0], halves[0], halves[1], halves[1]], axis=0)
                picked = nt(pick_hot, rows)
                for i in range(2):
                    X = 2 * h + i
                    for q in range(4):
                        lanes = slice(i * 128, (i + 1) * 128)
                        block = jnp.where(
                            left,
                            picked[32 * q : 32 * q + 16, lanes],
                            picked[32 * q + 16 : 32 * q + 32, lanes],
                        )
                        lowered[s, X * 16 : (X + 1) * 16, q * 128 : (q + 1) * 128] = block.astype(BF)
            grads = grad_active[s] * sigmoid * (1.0 + preact * (1.0 - sigmoid)) * filled
            grads = grads.astype(BF)
            grad_preact[s] = grads
            shifted[0:C, base : base + 640] = jnp.concatenate([grads, wide], axis=1)
            shifted[C : 2 * C, base : base + 640] = jnp.concatenate([edge, grads, edge], axis=1)
            shifted[2 * C :, base : base + 640] = jnp.concatenate([wide, grads], axis=1)
        total[...] += nt(shifted[...], stack[p])
        return carry

    lax.fori_loop(0, SLOTS // 2, pair, 0, unroll=True)
    rows = lowered[...].reshape(SLOTS * 64, 512)
    coarse[...] = nt(rows, down_kernel[...]).astype(BF).reshape(coarse.shape)
    turned = jnp.transpose(out_grad[...].reshape(SLOTS * 64, C2).astype(F32)).astype(BF)
    grad_down = nn(turned, rows)
    for j in range(5):
        width = min(128, 576 - j * 128)
        sums[j * 192 : (j + 1) * 192, 0:width] = total[:, j * 128 : j * 128 + width].astype(BF)
    sums[4 * 192 : 5 * 192, 64:128] = jnp.zeros((192, 64), BF)
    for j in range(4):
        sums[960 + j * C2 : 960 + (j + 1) * C2] = grad_down[:, j * 128 : (j + 1) * 128].astype(BF)
    sums[1472:1536] = jnp.zeros((64, 128), BF)


def fold_kernel(
    sources,
    grads_far,
    conv_far,
    placing_far,
    folded_far,
    grad_local,
    to_four_a,
    to_four_b,
    to_four_c,
    to_four_d,
    grad_preact,
    conv_back,
    placing,
    planes,
    stack,
    high,
    rims,
    grad_table,
    grad_table_high,
    folded,
    done,
    sent,
):
    copies = fetch(
        (grads_far, placing_far.at[0:FOLD_ROWS], conv_far), (grad_preact, placing, conv_back), done
    )
    grad_table[...] = jnp.zeros_like(grad_table)
    grad_table_high[...] = jnp.zeros_like(grad_table_high)
    wait(copies[:2])
    cap_hot = placing[CAP_ROWS : CAP_ROWS + 640]
    inner_hot = tiles_of(placing, INNER_ROWS, 128, 0, 2)
    rows = grad_preact[...].reshape(SLOTS * C, 512)
    for i in range(4):
        block = nn(rows[:, i * 128 : (i + 1) * 128], inner_hot)
        planes[:, i * 256 : (i + 1) * 256] = block.astype(BF)
    wait(copies[2:])

    def brick(s, carry):
        here = pl.ds(pl.multiple_of(s * C, C), C)
        for x in range(8):
            plane = planes[here, x * 128 : (x + 1) * 128]
            for k, shift in enumerate(SHIFTS):
                moved = plane if shift == 0 else pltpu.roll(plane, shift % 128, 1)
                stack[k * C : (k + 1) * C, x * 128 : (x + 1) * 128] = moved
        triple = nn(conv_back[...], stack[...])
        for x in range(10):
            value = None
            for o in range(3):
                if 0 <= x - o < 8:
                    part = triple[o * C : (o + 1) * C, (x - o) * 128 : (x - o + 1) * 128]
                    value = part if value is None else value + part
            high[here, x * 128 : (x + 1) * 128] = value.astype(BF)
            if 1 <= x <= 8:
                folded[here, (x - 1) * 128 : x * 128] = value
        pltpu.make_async_copy(folded.at[here], folded_far.at[here], sent.at[s]).start()
        return carry

    lax.fori_loop(0, SLOTS, brick, 0, unroll=2)
    rims[:, 0:640] = nt(high[:, 0:128], cap_hot)
    rims[:, 640:1152] = nt(high[:, 128:1152], side_tiles(placing, 0, 8))
    rims[:, 1152:1792] = nt(high[:, 1152:1280], cap_hot)
    for s in range(SLOTS):
        for t in range(14):
            block = rims[s * C : (s + 1) * C, t * 128 : (t + 1) * 128]
            grad_table[sources[0, s, PLACES[2 * t]]] += block
            if PLACES[2 * t + 1] is not None:
                grad_table_high[sources[0, s, PLACES[2 * t + 1]]] += block
    turned = pltpu.roll(grad_table_high[...].reshape(TABLE * C, 128), 64, 1)
    grad_table[...] += turned.reshape(TABLE, C, 128)
    grad_local[...] = grad_table[0:LOCAL]
    for s in range(SLOTS):
        rows = pl.ds(s * C, C)
        pltpu.make_async_copy(folded.at[rows], folded_far.at[rows], sent.at[s]).wait()
    left = low_lanes((C, 128))
    for p, j in enumerate(partners(False)):
        for q in range(CAP // 2):
            place = LOCAL + j * CAP + 2 * q
            block = jnp.where(left, grad_table[place], pltpu.roll(grad_table[place + 1], 64, 1))
            (to_four_a, to_four_b, to_four_c, to_four_d)[p][q] = block.astype(BF)


def unpack_kernel(sums, grad_kernel, grad_down):
    parts = []
    for o in range(3):
        tiles = [sums[j * 192 + o * C : j * 192 + (o + 1) * C].astype(F32) for j in range(5)]
        parts.append(jnp.concatenate(tiles, axis=1)[:, :576])
    grad_kernel[...] = jnp.concatenate(parts, axis=1)
    tiles = [sums[960 + t * C2 : 960 + (t + 1) * C2].astype(F32) for t in range(4)]
    grad_down[...] = jnp.concatenate(tiles, axis=1)


def finish_kernel(
    count,
    sends,
    folded,
    grad_local,
    from_a,
    from_b,
    from_c,
    from_d,
    face_hot,
    inner_hot,
    grad_features,
    table,
    layers,
):
    table[...] = grad_local[...]
    for p, j in enumerate(partners(True)):
        for q in range(CAP // 2):
            block = (from_a, from_b, from_c, from_d)[p][q].astype(F32)
            table[sends[0, 0, j, 2 * q]] += block
            table[sends[0, 0, j, 2 * q + 1]] += pltpu.roll(block, 64, 1)
    for s in range(SLOTS):
        for f in range(6):
            layers[s * C : (s + 1) * C, f * 128 : (f + 1) * 128] = table[6 * s + f].astype(BF)
    tiles = []
    for i in range(4):
        value = folded[:, i * 256 : (i + 1) * 256]
        top = value.astype(BF)
        rest = (value - top.astype(F32)).astype(BF)
        tiles.append(nt(top, inner_hot[...]) + nt(rest, inner_hot[...]))
    whole = jnp.concatenate(tiles, axis=1) + nt(layers[...], face_hot[...])
    for s in range(SLOTS):
        filled = jnp.where(s < count[0, 0], 1.0, 0.0).astype(F32)
        grad_features[0, s] = (whole[s * C : (s + 1) * C] * filled).astype(BF)


def call(kernel, limit, memories, outs, scratch, flops, *args, out_memories=None):
    where = {"s": pltpu.SMEM, "v": pltpu.VMEM, "h": pltpu.HBM}
    return pl.pallas_call(
        kernel,
        in_specs=[pl.BlockSpec(memory_space=where[m]) for m in memories],
        out_specs=[pl.BlockSpec(memory_space=where[m]) for m in out_memories or "v" * len(outs)],
        out_shape=[jax.ShapeDtypeStruct(s, d) for s, d in outs],
        scratch_shapes=[pltpu.VMEM(*s) if isinstance(s, tuple) else s for s in scratch],
        compiler_params=pltpu.CompilerParams(vmem_limit_bytes=int(limit * 2**20)),
        cost_estimate=pl.CostEstimate(flops=flops, bytes_accessed=2**20, transcendentals=0),
        name=kernel.__name__,
    )(*args)


def gather_sum(block, axes, parts):
    copies = jnp.broadcast_to(block[None], (parts,) + block.shape)
    got = lax.all_to_all(copies, axes, 0, 0)
    return got.astype(F32).sum(0)


def near_sum(block, sizes):
    parts = sizes["x"] * sizes["c"] * sizes["grp"]
    rows = block.shape[0] // parts
    got = lax.all_to_all(block.reshape(parts, rows, 128), NEAR, 0, 0)
    return got.astype(F32).sum(0).astype(BF)


def near_gather(block, sizes):
    parts = sizes["x"] * sizes["c"] * sizes["grp"]
    copies = jnp.broadcast_to(block[None], (parts,) + block.shape)
    return lax.all_to_all(copies, NEAR, 0, 0).reshape(parts * block.shape[0], 128)


def swap(blocks, axes, devices):
    pairs = [
        [(t, t + 2) for t in range(devices - 2) if t % 4 >= 2],
        [(t, t + 2) for t in range(devices - 2) if t % 4 < 2],
        [(t, t + 1) for t in range(devices - 1) if t % 2 == 1],
        [(t, t + 1) for t in range(devices - 1) if t % 2 == 0],
    ]
    routes = [two + [(b, a) for a, b in two] for two in pairs]
    return [lax.ppermute(block, axes, route) for block, route in zip(blocks, routes)]


def on_device(sizes, features, brick_count, send_list, halo_src, kernel, down_kernel, out_grad):
    face_packed, face_hot, inner_hot, placing = one_hot_tables()
    tile = ("z", "x", "c")
    devices = sizes["z"] * sizes["x"] * sizes["c"]
    blocks = [((CAP // 2, C, 128), BF)] * NOFF

    table, *outgoing = call(
        faces_kernel,
        56,
        "shhh",
        [((LOCAL, C, 128), BF)] + blocks,
        [
            pltpu.SMEM((1, 1, NOFF, CAP), jnp.int32),
            ((1, SLOTS, C, 512), BF),
            ((512, 256), BF),
            pltpu.SemaphoreType.DMA((3,)),
        ],
        2 * 256 * 512 * 768,
        brick_count,
        send_list,
        features,
        face_packed,
    )
    received = swap(outgoing, tile, devices)
    grad_active, conv_back = call(
        upper_kernel,
        56,
        "hhhh",
        [((SLOTS, C, 512), F32), ((192, 576), BF)],
        [
            ((1, SLOTS, 64, C2), BF),
            ((C2, 512), BF),
            ((C, 1728), BF),
            ((512, 128), BF),
            pltpu.SemaphoreType.DMA((4,)),
        ],
        10**9,
        out_grad,
        down_kernel,
        kernel,
        placing,
    )
    coarse, grad_preact, sums = call(
        main_kernel,
        53.8,
        "s" + "h" * 12,
        [
            ((1, SLOTS, 64, C2), BF),
            ((SLOTS, C, 512), BF),
            ((1536, 128), BF),
        ],
        [
            pltpu.SMEM((1, SLOTS, 26), jnp.int32),
            ((NOFF, CAP // 2, C, 128), BF),
            ((1, SLOTS, C, 512), BF),
            ((ALL_ROWS, 128), BF),
            ((C, 1728), BF),
            ((C2, 512), BF),
            ((1, SLOTS, 64, C2), BF),
            ((SLOTS, C, 512), F32),
            ((TABLE, C, 128), BF),
            ((TABLE, C, 128), BF),
            ((192, 576), BF),
            ((256, 14 * 128), BF),
            ((256, 1280), BF),
            ((2, 576, 1280), BF),
            ((192, 1280), BF),
            ((SLOTS, 64, 512), BF),
            ((192, 576), F32),
            pltpu.SemaphoreType.DMA((12,)),
        ],
        5 * 10**9,
        brick_count,
        halo_src,
        table,
        *received,
        features,
        placing,
        kernel,
        down_kernel,
        out_grad,
        grad_active,
    )
    part = near_sum(sums, sizes)
    folded, grad_local, *remote = call(
        fold_kernel,
        56,
        "shhh",
        [((256, 1024), F32), ((LOCAL, C, 128), F32)] + blocks,
        [
            ((SLOTS, C, 512), BF),
            ((192, 576), BF),
            ((FOLD_ROWS, 128), BF),
            ((256, 1024), BF),
            ((576, 1024), BF),
            ((256, 1280), BF),
            ((256, 14 * 128), F32),
            ((TABLE, C, 128), F32),
            ((TABLE, C, 128), F32),
            ((256, 1024), F32),
            pltpu.SemaphoreType.DMA((3,)),
            pltpu.SemaphoreType.DMA((SLOTS,)),
        ],
        3 * 10**9,
        halo_src,
        grad_preact,
        conv_back,
        placing,
        out_memories="hv" + "v" * NOFF,
    )
    part, *remote = lax.optimization_barrier((part, *remote))
    part = gather_sum(part, ("z",), sizes["z"])
    returned = swap(remote, tile, devices)
    part, *returned = lax.optimization_barrier((part, *returned))
    sums = near_gather(part.astype(BF), sizes)
    (grad_features,) = call(
        finish_kernel,
        12,
        "ss" + "v" * 8,
        [((1, SLOTS, C, 512), BF)],
        [((LOCAL, C, 128), F32), ((256, 768), BF)],
        2 * 256 * 512 * 768,
        brick_count,
        send_list,
        folded,
        grad_local,
        *returned,
        face_hot,
        inner_hot,
    )
    grad_kernel, grad_down = call(
        unpack_kernel, 8, "v", [((C, 1728), F32), ((C2, 512), F32)], [], 10**6, sums
    )
    return coarse, grad_features, grad_kernel, grad_down


def solution(mesh):
    tile, grp = mesh.shape["tile"], mesh.shape["grp"]
    sizes = {"z": tile // 8, "x": 4, "c": 2, "grp": grp}
    fine = Mesh(mesh.devices.reshape(tuple(sizes.values())), tuple(sizes))
    line = ("z", "x", "c")
    in_specs = (
        P("grp", line, None, None),
        P("grp", line),
        P("grp", line, None, None),
        P("grp", line, None),
        P(),
        P(),
        P("grp", line, None, None),
    )
    out_specs = (P("grp", line, None, None), P("grp", line, None, None), P(), P())

    def step(*args):
        return on_device(sizes, *args)

    return jax.shard_map(step, mesh=fine, in_specs=in_specs, out_specs=out_specs, check_vma=False)
```

```python
import jax
import jax.numpy as jnp
import ml_dtypes
import numpy as np
from jax import lax
from jax.experimental import pallas as pl
from jax.experimental.pallas import tpu as pltpu
from jax.sharding import Mesh
from jax.sharding import PartitionSpec as P

BF = jnp.bfloat16
F32 = jnp.float32
DIRECTIONS = [
    (a, b, c) for a in (-1, 0, 1) for b in (-1, 0, 1) for c in (-1, 0, 1) if (a, b, c) != (0, 0, 0)
]
SHIFTS = [10 * b + c for b in (-1, 0, 1) for c in (-1, 0, 1)]
SLOTS, C, C2, NOFF, CAP = 4, 64, 128, 4, 4
LOCAL = 6 * SLOTS + 1
TABLE = LOCAL + NOFF * CAP
PLACES = list(range(9)) + [None] + list(range(9, 26)) + [None]
NEAR = ("x", "c", "grp")


def rim_cells(d, full):
    if d == -1:
        return [(7, 0)]
    if d == 1:
        return [(0, 9)]
    return [(i, i + 1) for i in range(full)]


def one_hot_tables():
    faces = np.zeros((512, 6, 128), np.float32)
    for x in range(8):
        for y in range(8):
            for z in range(8):
                v = (x, y, z)
                for a in range(3):
                    p, q = [v[i] for i in range(3) if i != a]
                    for e in range(2):
                        if v[a] == 7 * e:
                            faces[x * 64 + y * 8 + z, 2 * a + e, p * 8 + q] = 1
    inner = np.zeros((2, 64, 2, 128), np.float32)
    for s in range(2):
        for y in range(8):
            for z in range(8):
                inner[s, y * 8 + z, s, (y + 1) * 10 + z + 1] = 1
    cap = np.zeros((10, 64, 128), np.float32)
    side = np.zeros((8, 64, 128), np.float32)
    for m, d in enumerate([d for d in DIRECTIONS if d[0] == 0]):
        if d[1] != 0:
            yy = 0 if d[1] == -1 else 9
            for x in range(8):
                for i, zz in rim_cells(d[2], 8):
                    side[m, x * 8 + i, yy * 10 + zz] = 1
        else:
            zz = 0 if d[2] == -1 else 9
            for x in range(8):
                for y in range(8):
                    side[m, x * 8 + y, (y + 1) * 10 + zz] = 1
    for m, (dy, dz) in enumerate([(b, c) for b in (-1, 0, 1) for c in (-1, 0, 1)]):
        for i, yy in rim_cells(dy, 8):
            for k, zz in rim_cells(dz, 8):
                cap[m, i * 8 + k, yy * 10 + zz] = 1
    window = np.zeros((2, 128, 9, 2, 64), np.float32)
    for k, shift in enumerate(SHIFTS):
        for y in range(8):
            for z in range(8):
                for p in range(2):
                    window[p, (y + 1) * 10 + z + 1 + shift, k, p, y * 8 + z] = 1
    spread = np.zeros((4, 4, 4, 2, 2, 4, 64), np.float32)
    pick = np.zeros((2, 2, 2, 4, 4, 2, 64), np.float32)
    for ty in range(2):
        for tz in range(2):
            for Y in range(4):
                for Z in range(4):
                    lane = (2 * Y + ty) * 8 + 2 * Z + tz
                    for X in range(4):
                        spread[X, Y, Z, ty, tz, X, lane] = 1
                    for tx in range(2):
                        pick[tx, ty, tz, Y, Z, tx, lane] = 1
    def stacked(table):
        rows, lanes = table.shape
        return table.reshape(rows, lanes // 128, 128).transpose(1, 0, 2).reshape(-1, 128)

    placing = np.concatenate(
        [
            cap.reshape(640, 128),
            side.reshape(512, 128),
            stacked(inner.reshape(128, 256)),
            pick.reshape(128, 128),
            stacked(spread.reshape(64, 1024)),
            stacked(window.reshape(256, 1152)),
        ]
    )
    b = ml_dtypes.bfloat16
    packed = faces[:, 2:, :64].reshape(512, 256)
    inner = inner.reshape(128, 256)
    return packed.astype(b), faces.reshape(512, 768).astype(b), inner.astype(b), placing.astype(b)


CAP_ROWS, SIDE_ROWS, INNER_ROWS, PICK_ROWS, SPREAD_ROWS = 0, 640, 1152, 1408, 1536
WINDOW_ROWS, FOLD_ROWS, ALL_ROWS = 2048, 1408, 4352


def tiles_of(table, start, rows, first, count):
    blocks = [table[start + (first + i) * rows : start + (first + i + 1) * rows] for i in range(count)]
    return jnp.concatenate(blocks, axis=1)


def side_tiles(table, first, count):
    side = table[SIDE_ROWS : SIDE_ROWS + 512]
    plane = (lax.broadcasted_iota(jnp.int32, (512, 128), 0) // 8) % 8
    return jnp.concatenate(
        [jnp.where(plane == first + i, side, jnp.zeros_like(side)) for i in range(count)], axis=1
    )


def low_lanes(shape):
    return lax.broadcasted_iota(jnp.int32, shape, 1) < 64


def nn(a, b):
    return jnp.dot(a, b, preferred_element_type=F32)


def nt(a, b):
    return lax.dot_general(a, b, (((1,), (1,)), ((), ())), preferred_element_type=F32)


def masked_rows(features, count):
    return jnp.concatenate(
        [features[0, s] * jnp.where(s < count, 1.0, 0.0).astype(BF) for s in range(SLOTS)], axis=0
    )


def fetch(sources, targets, done):
    copies = [
        pltpu.make_async_copy(a, b, done.at[i]) for i, (a, b) in enumerate(zip(sources, targets))
    ]
    for copy in copies:
        copy.start()
    return copies


def wait(copies):
    for copy in copies:
        copy.wait()


def partners(mine):
    first = lax.axis_index("c") == (0 if mine else 1)
    second = lax.axis_index("x") % 2 == (0 if mine else 1)
    return (
        jnp.where(second, 3, 2),
        jnp.where(second, 2, 3),
        jnp.where(first, 1, 0),
        jnp.where(first, 0, 1),
    )


def faces_kernel(
    count, sends_far, features_far, face_far, table, *rest
):
    outgoing, (sends, features, face_hot, done) = rest[:NOFF], rest[NOFF:]
    wait(fetch((features_far, face_far, sends_far), (features, face_hot, sends), done))
    masked = masked_rows(features, count[0, 0])
    low = low_lanes((SLOTS * C, 128))
    none = jnp.zeros((SLOTS * C, 128), BF)
    found = nn(masked, face_hot[...]).astype(BF)
    pairs = (found[:, 0:128], found[:, 128:256])
    layers = [masked[:, 0:128], pltpu.roll(masked[:, 384:512], 64, 1)]
    for block in pairs:
        layers += [block, pltpu.roll(block, 64, 1)]
    for f in range(6):
        layer = jnp.where(low, layers[f], none)
        for s in range(SLOTS):
            table[6 * s + f] = layer[s * C : (s + 1) * C]
    table[6 * SLOTS] = jnp.zeros((C, 128), BF)
    for p, j in enumerate(partners(True)):
        for q in range(CAP // 2):
            high = table[sends[0, 0, j, 2 * q + 1]]
            outgoing[p][q] = table[sends[0, 0, j, 2 * q]] + pltpu.roll(high, 64, 1)


def upper_kernel(
    out_far,
    down_far,
    placing_far,
    grad_active,
    out_grad,
    down_kernel,
    spread_rows,
    done,
):
    spread_far = placing_far.at[SPREAD_ROWS : SPREAD_ROWS + 512]
    copies = fetch(
        (out_far, down_far, spread_far),
        (out_grad, down_kernel, spread_rows),
        done,
    )
    wait(copies)
    turned = jnp.concatenate(
        [jnp.transpose(out_grad[0, s].astype(F32)).astype(BF) for s in range(SLOTS)], axis=0
    )
    spread = nn(turned, tiles_of(spread_rows, 0, 64, 0, 8)).astype(BF)
    tall = jnp.transpose(down_kernel[...].astype(F32)).astype(BF)
    down_rows = jnp.concatenate(
        [
            jnp.concatenate([tall[(4 * tx + t) * C : (4 * tx + t + 1) * C] for t in range(4)], axis=1)
            for tx in range(2)
        ],
        axis=0,
    )
    for s in range(SLOTS):
        rows = slice(s * C2, (s + 1) * C2)
        block = jnp.concatenate([spread[rows, t * 256 : (t + 1) * 256] for t in range(4)], axis=0)
        grown = nn(down_rows, block)
        grad_active[s] = jnp.concatenate(
            [
                grown[tx * C : (tx + 1) * C, X * 64 : (X + 1) * 64]
                for X in range(4)
                for tx in range(2)
            ],
            axis=1,
        )


def main_kernel(
    count,
    sources_far,
    table,
    from_a,
    from_b,
    from_c,
    from_d,
    features_far,
    placing_far,
    kernel_far,
    down_far,
    out_far,
    active_far,
    coarse,
    grad_preact,
    sums,
    sources,
    arrived,
    features,
    placing,
    kernel,
    down_kernel,
    out_grad,
    grad_active,
    halo,
    halo_high,
    conv,
    entries,
    padded,
    stack,
    shifted,
    lowered,
    total,
    done,
):
    copies = fetch(
        (from_a, from_b, from_c, from_d, table, sources_far)
        + (features_far, placing_far, kernel_far, down_far, out_far, active_far),
        [arrived.at[j] for j in range(NOFF)]
        + [halo.at[0:LOCAL], sources, features, placing, kernel, down_kernel, out_grad]
        + [grad_active],
        done,
    )
    wait(copies[: NOFF + 2])
    low = low_lanes((C, 128))
    none = jnp.zeros((C, 128), BF)
    halo_high[0:LOCAL] = pltpu.roll(
        halo[0:LOCAL].reshape(LOCAL * C, 128), 64, 1
    ).reshape(LOCAL, C, 128)
    for p, j in enumerate(partners(False)):
        for q in range(CAP // 2):
            block, place = arrived[p, q], LOCAL + j * CAP + 2 * q
            turned = pltpu.roll(block, 64, 1)
            halo[place] = jnp.where(low, block, none)
            halo[place + 1] = jnp.where(low, turned, none)
            halo_high[place] = jnp.where(low, none, turned)
            halo_high[place + 1] = jnp.where(low, none, block)
    for s in range(SLOTS):
        for t in range(14):
            even, odd = PLACES[2 * t], PLACES[2 * t + 1]
            block = halo[sources[0, s, even]]
            if odd is not None:
                block = block + halo_high[sources[0, s, odd]]
            entries[s * C : (s + 1) * C, t * 128 : (t + 1) * 128] = block
    wait(copies[NOFF + 2 :])
    cap_hot = placing[CAP_ROWS : CAP_ROWS + 640]
    inner_hot = tiles_of(placing, INNER_ROWS, 128, 0, 2)
    pick_hot = placing[PICK_ROWS : PICK_ROWS + 128]
    masked = masked_rows(features, count[0, 0])
    padded[:, 0:128] = nn(entries[:, 0:640], cap_hot).astype(BF)
    padded[:, 1152:1280] = nn(entries[:, 1152:1792], cap_hot).astype(BF)
    for i in range(4):
        block = nn(entries[:, 640:1152], side_tiles(placing, 2 * i, 2))
        block = block + nn(masked[:, i * 128 : (i + 1) * 128], inner_hot)
        padded[:, 128 + i * 256 : 384 + i * 256] = block.astype(BF)
    window_hot = tiles_of(placing, WINDOW_ROWS, 256, 0, 9)
    for i in range(5):
        planes = nn(padded[:, i * 256 : (i + 1) * 256], window_hot).astype(BF)
        for s in range(SLOTS):
            lanes = slice((s % 2) * 640 + i * 128, (s % 2) * 640 + (i + 1) * 128)
            for k in range(9):
                block = planes[s * C : (s + 1) * C, k * 128 : (k + 1) * 128]
                stack[s // 2, k * C : (k + 1) * C, lanes] = block

    for o in range(3):
        conv[o * C : (o + 1) * C] = kernel[:, o * 576 : (o + 1) * 576]
    left = low_lanes((16, 128))
    edge = jnp.zeros((C, 64), BF)
    wide = jnp.zeros((C, 128), BF)
    total[...] = jnp.zeros_like(total)

    def pair(p, carry):
        triple = nn(conv[...], stack[p])
        for j in range(2):
            s = 2 * p + j
            filled = jnp.where(s < count[0, 0], 1.0, 0.0).astype(F32)
            base = j * 640
            preact = (
                triple[0:C, base : base + 512]
                + triple[C : 2 * C, base + 64 : base + 576]
                + triple[2 * C :, base + 128 : base + 640]
            )
            sigmoid = jax.nn.sigmoid(preact)
            active = (preact * sigmoid * filled).astype(BF)
            for h in range(2):
                halves = [active[:, (2 * h + i) * 128 : (2 * h + i + 1) * 128] for i in range(2)]
                rows = jnp.concatenate([halves[0], halves[0], halves[1], halves[1]], axis=0)
                picked = nt(pick_hot, rows)
                for i in range(2):
                    X = 2 * h + i
                    for q in range(4):
                        lanes = slice(i * 128, (i + 1) * 128)
                        block = jnp.where(
                            left,
                            picked[32 * q : 32 * q + 16, lanes],
                            picked[32 * q + 16 : 32 * q + 32, lanes],
                        )
                        lowered[s, X * 16 : (X + 1) * 16, q * 128 : (q + 1) * 128] = block.astype(BF)
            grads = grad_active[s] * sigmoid * (1.0 + preact * (1.0 - sigmoid)) * filled
            grads = grads.astype(BF)
            grad_preact[s] = grads
            shifted[0:C, base : base + 640] = jnp.concatenate([grads, wide], axis=1)
            shifted[C : 2 * C, base : base + 640] = jnp.concatenate([edge, grads, edge], axis=1)
            shifted[2 * C :, base : base + 640] = jnp.concatenate([wide, grads], axis=1)
        total[...] += nt(shifted[...], stack[p])
        return carry

    lax.fori_loop(0, SLOTS // 2, pair, 0, unroll=True)
    rows = lowered[...].reshape(SLOTS * 64, 512)
    coarse[...] = nt(rows, down_kernel[...]).astype(BF).reshape(coarse.shape)
    turned = jnp.transpose(out_grad[...].reshape(SLOTS * 64, C2).astype(F32)).astype(BF)
    grad_down = nn(turned, rows)
    for j in range(5):
        width = min(128, 576 - j * 128)
        sums[j * 192 : (j + 1) * 192, 0:width] = total[:, j * 128 : j * 128 + width].astype(BF)
    sums[4 * 192 : 5 * 192, 64:128] = jnp.zeros((192, 64), BF)
    for j in range(4):
        sums[960 + j * C2 : 960 + (j + 1) * C2] = grad_down[:, j * 128 : (j + 1) * 128].astype(BF)
    sums[1472:1536] = jnp.zeros((64, 128), BF)


def fold_kernel(
    sources,
    grads_far,
    kernel_far,
    placing_far,
    folded_far,
    grad_local,
    to_four_a,
    to_four_b,
    to_four_c,
    to_four_d,
    grad_preact,
    kernel,
    placing,
    conv_back,
    planes,
    stack,
    high,
    rims,
    grad_table,
    grad_table_high,
    folded,
    done,
    sent,
):
    copies = fetch(
        (kernel_far, grads_far, placing_far.at[0:FOLD_ROWS]), (kernel, grad_preact, placing), done
    )
    grad_table[...] = jnp.zeros_like(grad_table)
    grad_table_high[...] = jnp.zeros_like(grad_table_high)
    wait(copies[:1])
    tall = jnp.transpose(kernel[...].astype(F32)).astype(BF)
    for o in range(3):
        conv_back[o * C : (o + 1) * C] = jnp.concatenate(
            [tall[(9 * o + k) * C : (9 * o + k + 1) * C] for k in range(9)], axis=1
        )
    wait(copies[1:])
    cap_hot = placing[CAP_ROWS : CAP_ROWS + 640]
    inner_hot = tiles_of(placing, INNER_ROWS, 128, 0, 2)
    rows = grad_preact[...].reshape(SLOTS * C, 512)
    for i in range(4):
        block = nn(rows[:, i * 128 : (i + 1) * 128], inner_hot)
        planes[:, i * 256 : (i + 1) * 256] = block.astype(BF)

    def brick(s, carry):
        here = pl.ds(pl.multiple_of(s * C, C), C)
        for x in range(8):
            plane = planes[here, x * 128 : (x + 1) * 128]
            for k, shift in enumerate(SHIFTS):
                moved = plane if shift == 0 else pltpu.roll(plane, shift % 128, 1)
                stack[k * C : (k + 1) * C, x * 128 : (x + 1) * 128] = moved
        triple = nn(conv_back[...], stack[...])
        for x in range(10):
            value = None
            for o in range(3):
                if 0 <= x - o < 8:
                    part = triple[o * C : (o + 1) * C, (x - o) * 128 : (x - o + 1) * 128]
                    value = part if value is None else value + part
            high[here, x * 128 : (x + 1) * 128] = value.astype(BF)
            if 1 <= x <= 8:
                folded[here, (x - 1) * 128 : x * 128] = value
        pltpu.make_async_copy(folded.at[here], folded_far.at[here], sent.at[s]).start()
        return carry

    lax.fori_loop(0, SLOTS, brick, 0, unroll=2)
    rims[:, 0:640] = nt(high[:, 0:128], cap_hot)
    rims[:, 640:1152] = nt(high[:, 128:1152], side_tiles(placing, 0, 8))
    rims[:, 1152:1792] = nt(high[:, 1152:1280], cap_hot)
    for s in range(SLOTS):
        for t in range(14):
            block = rims[s * C : (s + 1) * C, t * 128 : (t + 1) * 128]
            grad_table[sources[0, s, PLACES[2 * t]]] += block
            if PLACES[2 * t + 1] is not None:
                grad_table_high[sources[0, s, PLACES[2 * t + 1]]] += block
    turned = pltpu.roll(grad_table_high[...].reshape(TABLE * C, 128), 64, 1)
    grad_table[...] += turned.reshape(TABLE, C, 128)
    grad_local[...] = grad_table[0:LOCAL]
    for s in range(SLOTS):
        rows = pl.ds(s * C, C)
        pltpu.make_async_copy(folded.at[rows], folded_far.at[rows], sent.at[s]).wait()
    left = low_lanes((C, 128))
    for p, j in enumerate(partners(False)):
        for q in range(CAP // 2):
            place = LOCAL + j * CAP + 2 * q
            block = jnp.where(left, grad_table[place], pltpu.roll(grad_table[place + 1], 64, 1))
            (to_four_a, to_four_b, to_four_c, to_four_d)[p][q] = block.astype(BF)


def unpack_kernel(sums, grad_kernel, grad_down):
    parts = []
    for o in range(3):
        tiles = [sums[j * 192 + o * C : j * 192 + (o + 1) * C].astype(F32) for j in range(5)]
        parts.append(jnp.concatenate(tiles, axis=1)[:, :576])
    grad_kernel[...] = jnp.concatenate(parts, axis=1)
    tiles = [sums[960 + t * C2 : 960 + (t + 1) * C2].astype(F32) for t in range(4)]
    grad_down[...] = jnp.concatenate(tiles, axis=1)


def finish_kernel(
    count,
    sends,
    folded,
    grad_local,
    from_a,
    from_b,
    from_c,
    from_d,
    face_hot,
    inner_hot,
    grad_features,
    table,
    layers,
):
    table[...] = grad_local[...]
    for p, j in enumerate(partners(True)):
        for q in range(CAP // 2):
            block = (from_a, from_b, from_c, from_d)[p][q].astype(F32)
            table[sends[0, 0, j, 2 * q]] += block
            table[sends[0, 0, j, 2 * q + 1]] += pltpu.roll(block, 64, 1)
    for s in range(SLOTS):
        for f in range(6):
            layers[s * C : (s + 1) * C, f * 128 : (f + 1) * 128] = table[6 * s + f].astype(BF)
    tiles = []
    for i in range(4):
        value = folded[:, i * 256 : (i + 1) * 256]
        top = value.astype(BF)
        rest = (value - top.astype(F32)).astype(BF)
        tiles.append(nt(top, inner_hot[...]) + nt(rest, inner_hot[...]))
    whole = jnp.concatenate(tiles, axis=1) + nt(layers[...], face_hot[...])
    for s in range(SLOTS):
        filled = jnp.where(s < count[0, 0], 1.0, 0.0).astype(F32)
        grad_features[0, s] = (whole[s * C : (s + 1) * C] * filled).astype(BF)


def call(kernel, limit, memories, outs, scratch, flops, *args, out_memories=None):
    where = {"s": pltpu.SMEM, "v": pltpu.VMEM, "h": pltpu.HBM}
    return pl.pallas_call(
        kernel,
        in_specs=[pl.BlockSpec(memory_space=where[m]) for m in memories],
        out_specs=[pl.BlockSpec(memory_space=where[m]) for m in out_memories or "v" * len(outs)],
        out_shape=[jax.ShapeDtypeStruct(s, d) for s, d in outs],
        scratch_shapes=[pltpu.VMEM(*s) if isinstance(s, tuple) else s for s in scratch],
        compiler_params=pltpu.CompilerParams(vmem_limit_bytes=int(limit * 2**20)),
        cost_estimate=pl.CostEstimate(flops=flops, bytes_accessed=2**20, transcendentals=0),
        name=kernel.__name__,
    )(*args)


def gather_sum(block, axes, parts):
    copies = jnp.broadcast_to(block[None], (parts,) + block.shape)
    got = lax.all_to_all(copies, axes, 0, 0)
    return got.astype(F32).sum(0)


def near_sum(block, sizes):
    parts = sizes["x"] * sizes["c"] * sizes["grp"]
    rows = block.shape[0] // parts
    got = lax.all_to_all(block.reshape(parts, rows, 128), NEAR, 0, 0)
    return got.astype(F32).sum(0).astype(BF)


def near_gather(block, sizes):
    parts = sizes["x"] * sizes["c"] * sizes["grp"]
    copies = jnp.broadcast_to(block[None], (parts,) + block.shape)
    return lax.all_to_all(copies, NEAR, 0, 0).reshape(parts * block.shape[0], 128)


def swap(blocks, axes, devices):
    pairs = [
        [(t, t + 2) for t in range(devices - 2) if t % 4 >= 2],
        [(t, t + 2) for t in range(devices - 2) if t % 4 < 2],
        [(t, t + 1) for t in range(devices - 1) if t % 2 == 1],
        [(t, t + 1) for t in range(devices - 1) if t % 2 == 0],
    ]
    routes = [two + [(b, a) for a, b in two] for two in pairs]
    return [lax.ppermute(block, axes, route) for block, route in zip(blocks, routes)]


def on_device(sizes, features, brick_count, send_list, halo_src, kernel, down_kernel, out_grad):
    face_packed, face_hot, inner_hot, placing = one_hot_tables()
    tile = ("z", "x", "c")
    devices = sizes["z"] * sizes["x"] * sizes["c"]
    blocks = [((CAP // 2, C, 128), BF)] * NOFF

    table, *outgoing = call(
        faces_kernel,
        56,
        "shhh",
        [((LOCAL, C, 128), BF)] + blocks,
        [
            pltpu.SMEM((1, 1, NOFF, CAP), jnp.int32),
            ((1, SLOTS, C, 512), BF),
            ((512, 256), BF),
            pltpu.SemaphoreType.DMA((3,)),
        ],
        2 * 256 * 512 * 768,
        brick_count,
        send_list,
        features,
        face_packed,
    )
    received = swap(outgoing, tile, devices)
    (grad_active,) = call(
        upper_kernel,
        56,
        "hhh",
        [((SLOTS, C, 512), F32)],
        [
            ((1, SLOTS, 64, C2), BF),
            ((C2, 512), BF),
            ((512, 128), BF),
            pltpu.SemaphoreType.DMA((3,)),
        ],
        10**9,
        out_grad,
        down_kernel,
        placing,
    )
    coarse, grad_preact, sums = call(
        main_kernel,
        53.8,
        "s" + "h" * 12,
        [
            ((1, SLOTS, 64, C2), BF),
            ((SLOTS, C, 512), BF),
            ((1536, 128), BF),
        ],
        [
            pltpu.SMEM((1, SLOTS, 26), jnp.int32),
            ((NOFF, CAP // 2, C, 128), BF),
            ((1, SLOTS, C, 512), BF),
            ((ALL_ROWS, 128), BF),
            ((C, 1728), BF),
            ((C2, 512), BF),
            ((1, SLOTS, 64, C2), BF),
            ((SLOTS, C, 512), F32),
            ((TABLE, C, 128), BF),
            ((TABLE, C, 128), BF),
            ((192, 576), BF),
            ((256, 14 * 128), BF),
            ((256, 1280), BF),
            ((2, 576, 1280), BF),
            ((192, 1280), BF),
            ((SLOTS, 64, 512), BF),
            ((192, 576), F32),
            pltpu.SemaphoreType.DMA((12,)),
        ],
        5 * 10**9,
        brick_count,
        halo_src,
        table,
        *received,
        features,
        placing,
        kernel,
        down_kernel,
        out_grad,
        grad_active,
    )
    part = near_sum(sums, sizes)
    folded, grad_local, *remote = call(
        fold_kernel,
        56,
        "shhh",
        [((256, 1024), F32), ((LOCAL, C, 128), F32)] + blocks,
        [
            ((SLOTS, C, 512), BF),
            ((C, 1728), BF),
            ((FOLD_ROWS, 128), BF),
            ((192, 576), BF),
            ((256, 1024), BF),
            ((576, 1024), BF),
            ((256, 1280), BF),
            ((256, 14 * 128), F32),
            ((TABLE, C, 128), F32),
            ((TABLE, C, 128), F32),
            ((256, 1024), F32),
            pltpu.SemaphoreType.DMA((3,)),
            pltpu.SemaphoreType.DMA((SLOTS,)),
        ],
        3 * 10**9,
        halo_src,
        grad_preact,
        kernel,
        placing,
        out_memories="hv" + "v" * NOFF,
    )
    part, *remote = lax.optimization_barrier((part, *remote))
    part = gather_sum(part, ("z",), sizes["z"])
    returned = swap(remote, tile, devices)
    part, *returned = lax.optimization_barrier((part, *returned))
    sums = near_gather(part.astype(BF), sizes)
    (grad_features,) = call(
        finish_kernel,
        12,
        "ss" + "v" * 8,
        [((1, SLOTS, C, 512), BF)],
        [((LOCAL, C, 128), F32), ((256, 768), BF)],
        2 * 256 * 512 * 768,
        brick_count,
        send_list,
        folded,
        grad_local,
        *returned,
        face_hot,
        inner_hot,
    )
    grad_kernel, grad_down = call(
        unpack_kernel, 8, "v", [((C, 1728), F32), ((C2, 512), F32)], [], 10**6, sums
    )
    return coarse, grad_features, grad_kernel, grad_down


def solution(mesh):
    tile, grp = mesh.shape["tile"], mesh.shape["grp"]
    sizes = {"z": tile // 8, "x": 4, "c": 2, "grp": grp}
    fine = Mesh(mesh.devices.reshape(tuple(sizes.values())), tuple(sizes))
    line = ("z", "x", "c")
    in_specs = (
        P("grp", line, None, None),
        P("grp", line),
        P("grp", line, None, None),
        P("grp", line, None),
        P(),
        P(),
        P("grp", line, None, None),
    )
    out_specs = (P("grp", line, None, None), P("grp", line, None, None), P(), P())

    def step(*args):
        return on_device(sizes, *args)

    return jax.shard_map(step, mesh=fine, in_specs=in_specs, out_specs=out_specs, check_vma=False)
```

```python
import jax
import jax.numpy as jnp
import ml_dtypes
import numpy as np
from jax import lax
from jax.experimental import pallas as pl
from jax.experimental.pallas import tpu as pltpu
from jax.sharding import Mesh
from jax.sharding import PartitionSpec as P

BF = jnp.bfloat16
F32 = jnp.float32
DIRECTIONS = [
    (a, b, c) for a in (-1, 0, 1) for b in (-1, 0, 1) for c in (-1, 0, 1) if (a, b, c) != (0, 0, 0)
]
SHIFTS = [10 * b + c for b in (-1, 0, 1) for c in (-1, 0, 1)]
SLOTS, C, C2, NOFF, CAP = 4, 64, 128, 4, 4
LOCAL = 6 * SLOTS + 1
TABLE = LOCAL + NOFF * CAP
PLACES = list(range(9)) + [None] + list(range(9, 26)) + [None]
NEAR = ("x", "c", "grp")


def rim_cells(d, full):
    if d == -1:
        return [(7, 0)]
    if d == 1:
        return [(0, 9)]
    return [(i, i + 1) for i in range(full)]


def one_hot_tables():
    faces = np.zeros((512, 6, 128), np.float32)
    for x in range(8):
        for y in range(8):
            for z in range(8):
                v = (x, y, z)
                for a in range(3):
                    p, q = [v[i] for i in range(3) if i != a]
                    for e in range(2):
                        if v[a] == 7 * e:
                            faces[x * 64 + y * 8 + z, 2 * a + e, p * 8 + q] = 1
    inner = np.zeros((2, 64, 2, 128), np.float32)
    for s in range(2):
        for y in range(8):
            for z in range(8):
                inner[s, y * 8 + z, s, (y + 1) * 10 + z + 1] = 1
    cap = np.zeros((10, 64, 128), np.float32)
    side = np.zeros((8, 64, 128), np.float32)
    for m, d in enumerate([d for d in DIRECTIONS if d[0] == 0]):
        if d[1] != 0:
            yy = 0 if d[1] == -1 else 9
            for x in range(8):
                for i, zz in rim_cells(d[2], 8):
                    side[m, x * 8 + i, yy * 10 + zz] = 1
        else:
            zz = 0 if d[2] == -1 else 9
            for x in range(8):
                for y in range(8):
                    side[m, x * 8 + y, (y + 1) * 10 + zz] = 1
    for m, (dy, dz) in enumerate([(b, c) for b in (-1, 0, 1) for c in (-1, 0, 1)]):
        for i, yy in rim_cells(dy, 8):
            for k, zz in rim_cells(dz, 8):
                cap[m, i * 8 + k, yy * 10 + zz] = 1
    window = np.zeros((2, 128, 9, 2, 64), np.float32)
    for k, shift in enumerate(SHIFTS):
        for y in range(8):
            for z in range(8):
                for p in range(2):
                    window[p, (y + 1) * 10 + z + 1 + shift, k, p, y * 8 + z] = 1
    spread = np.zeros((4, 4, 4, 2, 2, 4, 64), np.float32)
    pick = np.zeros((2, 2, 2, 4, 4, 2, 64), np.float32)
    for ty in range(2):
        for tz in range(2):
            for Y in range(4):
                for Z in range(4):
                    lane = (2 * Y + ty) * 8 + 2 * Z + tz
                    for X in range(4):
                        spread[X, Y, Z, ty, tz, X, lane] = 1
                    for tx in range(2):
                        pick[tx, ty, tz, Y, Z, tx, lane] = 1
    def stacked(table):
        rows, lanes = table.shape
        return table.reshape(rows, lanes // 128, 128).transpose(1, 0, 2).reshape(-1, 128)

    placing = np.concatenate(
        [
            cap.reshape(640, 128),
            side.reshape(512, 128),
            stacked(inner.reshape(128, 256)),
            pick.reshape(128, 128),
            stacked(spread.reshape(64, 1024)),
            stacked(window.reshape(256, 1152)),
        ]
    )
    b = ml_dtypes.bfloat16
    packed = faces[:, 2:, :64].reshape(512, 256)
    inner = inner.reshape(128, 256)
    return packed.astype(b), faces.reshape(512, 768).astype(b), inner.astype(b), placing.astype(b)


CAP_ROWS, SIDE_ROWS, INNER_ROWS, PICK_ROWS, SPREAD_ROWS = 0, 640, 1152, 1408, 1536
WINDOW_ROWS, FOLD_ROWS, ALL_ROWS = 2048, 1408, 4352


def tiles_of(table, start, rows, first, count):
    blocks = [table[start + (first + i) * rows : start + (first + i + 1) * rows] for i in range(count)]
    return jnp.concatenate(blocks, axis=1)


def side_tiles(table, first, count):
    side = table[SIDE_ROWS : SIDE_ROWS + 512]
    plane = (lax.broadcasted_iota(jnp.int32, (512, 128), 0) // 8) % 8
    return jnp.concatenate(
        [jnp.where(plane == first + i, side, jnp.zeros_like(side)) for i in range(count)], axis=1
    )


def low_lanes(shape):
    return lax.broadcasted_iota(jnp.int32, shape, 1) < 64


def nn(a, b):
    return jnp.dot(a, b, preferred_element_type=F32)


def nt(a, b):
    return lax.dot_general(a, b, (((1,), (1,)), ((), ())), preferred_element_type=F32)


def masked_rows(features, count):
    return jnp.concatenate(
        [features[0, s] * jnp.where(s < count, 1.0, 0.0).astype(BF) for s in range(SLOTS)], axis=0
    )


def fetch(sources, targets, done):
    copies = [
        pltpu.make_async_copy(a, b, done.at[i]) for i, (a, b) in enumerate(zip(sources, targets))
    ]
    for copy in copies:
        copy.start()
    return copies


def wait(copies):
    for copy in copies:
        copy.wait()


def partners(mine):
    first = lax.axis_index("c") == (0 if mine else 1)
    second = lax.axis_index("x") % 2 == (0 if mine else 1)
    return (
        jnp.where(second, 3, 2),
        jnp.where(second, 2, 3),
        jnp.where(first, 1, 0),
        jnp.where(first, 0, 1),
    )


def faces_kernel(
    count, sends_far, features_far, face_far, table, *rest
):
    outgoing, (sends, features, face_hot, done) = rest[:NOFF], rest[NOFF:]
    wait(fetch((features_far, face_far, sends_far), (features, face_hot, sends), done))
    masked = masked_rows(features, count[0, 0])
    low = low_lanes((SLOTS * C, 128))
    none = jnp.zeros((SLOTS * C, 128), BF)
    found = nn(masked, face_hot[...]).astype(BF)
    pairs = (found[:, 0:128], found[:, 128:256])
    layers = [masked[:, 0:128], pltpu.roll(masked[:, 384:512], 64, 1)]
    for block in pairs:
        layers += [block, pltpu.roll(block, 64, 1)]
    for f in range(6):
        layer = jnp.where(low, layers[f], none)
        for s in range(SLOTS):
            table[6 * s + f] = layer[s * C : (s + 1) * C]
    table[6 * SLOTS] = jnp.zeros((C, 128), BF)
    for p, j in enumerate(partners(True)):
        for q in range(CAP // 2):
            high = table[sends[0, 0, j, 2 * q + 1]]
            outgoing[p][q] = table[sends[0, 0, j, 2 * q]] + pltpu.roll(high, 64, 1)


def upper_kernel(
    out_far,
    down_far,
    placing_far,
    grad_active,
    out_grad,
    down_kernel,
    spread_rows,
    done,
):
    spread_far = placing_far.at[SPREAD_ROWS : SPREAD_ROWS + 512]
    copies = fetch(
        (out_far, down_far, spread_far),
        (out_grad, down_kernel, spread_rows),
        done,
    )
    wait(copies)
    turned = jnp.concatenate(
        [jnp.transpose(out_grad[0, s].astype(F32)).astype(BF) for s in range(SLOTS)], axis=0
    )
    spread = nn(turned, tiles_of(spread_rows, 0, 64, 0, 8)).astype(BF)
    tall = jnp.transpose(down_kernel[...].astype(F32)).astype(BF)
    down_rows = jnp.concatenate(
        [
            jnp.concatenate([tall[(4 * tx + t) * C : (4 * tx + t + 1) * C] for t in range(4)], axis=1)
            for tx in range(2)
        ],
        axis=0,
    )
    for s in range(SLOTS):
        rows = slice(s * C2, (s + 1) * C2)
        block = jnp.concatenate([spread[rows, t * 256 : (t + 1) * 256] for t in range(4)], axis=0)
        grown = nn(down_rows, block)
        grad_active[s] = jnp.concatenate(
            [
                grown[tx * C : (tx + 1) * C, X * 64 : (X + 1) * 64]
                for X in range(4)
                for tx in range(2)
            ],
            axis=1,
        )


def main_kernel(
    count,
    sources_far,
    table,
    from_a,
    from_b,
    from_c,
    from_d,
    features_far,
    placing_far,
    kernel_far,
    down_far,
    out_far,
    active_far,
    coarse,
    grad_preact,
    sums,
    sources,
    arrived,
    features,
    placing,
    kernel,
    down_kernel,
    out_grad,
    grad_active,
    halo,
    halo_high,
    conv,
    entries,
    padded,
    stack,
    shifted,
    lowered,
    total,
    done,
):
    copies = fetch(
        (from_a, from_b, from_c, from_d, table, sources_far)
        + (features_far, placing_far, kernel_far, down_far, out_far, active_far),
        [arrived.at[j] for j in range(NOFF)]
        + [halo.at[0:LOCAL], sources, features, placing, kernel, down_kernel, out_grad]
        + [grad_active],
        done,
    )
    wait(copies[: NOFF + 2])
    low = low_lanes((C, 128))
    none = jnp.zeros((C, 128), BF)
    halo_high[0:LOCAL] = pltpu.roll(
        halo[0:LOCAL].reshape(LOCAL * C, 128), 64, 1
    ).reshape(LOCAL, C, 128)
    for p, j in enumerate(partners(False)):
        for q in range(CAP // 2):
            block, place = arrived[p, q], LOCAL + j * CAP + 2 * q
            turned = pltpu.roll(block, 64, 1)
            halo[place] = jnp.where(low, block, none)
            halo[place + 1] = jnp.where(low, turned, none)
            halo_high[place] = jnp.where(low, none, turned)
            halo_high[place + 1] = jnp.where(low, none, block)
    for s in range(SLOTS):
        for t in range(14):
            even, odd = PLACES[2 * t], PLACES[2 * t + 1]
            block = halo[sources[0, s, even]]
            if odd is not None:
                block = block + halo_high[sources[0, s, odd]]
            entries[s * C : (s + 1) * C, t * 128 : (t + 1) * 128] = block
    wait(copies[NOFF + 2 :])
    cap_hot = placing[CAP_ROWS : CAP_ROWS + 640]
    inner_hot = tiles_of(placing, INNER_ROWS, 128, 0, 2)
    pick_hot = placing[PICK_ROWS : PICK_ROWS + 128]
    masked = masked_rows(features, count[0, 0])
    padded[:, 0:128] = nn(entries[:, 0:640], cap_hot).astype(BF)
    padded[:, 1152:1280] = nn(entries[:, 1152:1792], cap_hot).astype(BF)
    for i in range(4):
        block = nn(entries[:, 640:1152], side_tiles(placing, 2 * i, 2))
        block = block + nn(masked[:, i * 128 : (i + 1) * 128], inner_hot)
        padded[:, 128 + i * 256 : 384 + i * 256] = block.astype(BF)
    window_hot = tiles_of(placing, WINDOW_ROWS, 256, 0, 9)
    for i in range(5):
        planes = nn(padded[:, i * 256 : (i + 1) * 256], window_hot).astype(BF)
        for s in range(SLOTS):
            lanes = slice((s % 2) * 640 + i * 128, (s % 2) * 640 + (i + 1) * 128)
            for k in range(9):
                block = planes[s * C : (s + 1) * C, k * 128 : (k + 1) * 128]
                stack[s // 2, k * C : (k + 1) * C, lanes] = block

    for o in range(3):
        conv[o * C : (o + 1) * C] = kernel[:, o * 576 : (o + 1) * 576]
    left = low_lanes((16, 128))
    edge = jnp.zeros((C, 64), BF)
    wide = jnp.zeros((C, 128), BF)
    total[...] = jnp.zeros_like(total)

    def pair(p, carry):
        triple = nn(conv[...], stack[p])
        for j in range(2):
            s = 2 * p + j
            filled = jnp.where(s < count[0, 0], 1.0, 0.0).astype(F32)
            base = j * 640
            preact = (
                triple[0:C, base : base + 512]
                + triple[C : 2 * C, base + 64 : base + 576]
                + triple[2 * C :, base + 128 : base + 640]
            )
            sigmoid = jax.nn.sigmoid(preact)
            active = (preact * sigmoid * filled).astype(BF)
            for h in range(2):
                halves = [active[:, (2 * h + i) * 128 : (2 * h + i + 1) * 128] for i in range(2)]
                rows = jnp.concatenate([halves[0], halves[0], halves[1], halves[1]], axis=0)
                picked = nt(pick_hot, rows)
                for i in range(2):
                    X = 2 * h + i
                    for q in range(4):
                        lanes = slice(i * 128, (i + 1) * 128)
                        block = jnp.where(
                            left,
                            picked[32 * q : 32 * q + 16, lanes],
                            picked[32 * q + 16 : 32 * q + 32, lanes],
                        )
                        lowered[s, X * 16 : (X + 1) * 16, q * 128 : (q + 1) * 128] = block.astype(BF)
            grads = grad_active[s] * sigmoid * (1.0 + preact * (1.0 - sigmoid)) * filled
            grads = grads.astype(BF)
            grad_preact[s] = grads
            shifted[0:C, base : base + 640] = jnp.concatenate([grads, wide], axis=1)
            shifted[C : 2 * C, base : base + 640] = jnp.concatenate([edge, grads, edge], axis=1)
            shifted[2 * C :, base : base + 640] = jnp.concatenate([wide, grads], axis=1)
        total[...] += nt(shifted[...], stack[p])
        return carry

    lax.fori_loop(0, SLOTS // 2, pair, 0, unroll=True)
    rows = lowered[...].reshape(SLOTS * 64, 512)
    coarse[...] = nt(rows, down_kernel[...]).astype(BF).reshape(coarse.shape)
    turned = jnp.transpose(out_grad[...].reshape(SLOTS * 64, C2).astype(F32)).astype(BF)
    grad_down = nn(turned, rows)
    for j in range(5):
        width = min(128, 576 - j * 128)
        sums[j * 192 : (j + 1) * 192, 0:width] = total[:, j * 128 : j * 128 + width].astype(BF)
    sums[4 * 192 : 5 * 192, 64:128] = jnp.zeros((192, 64), BF)
    for j in range(4):
        sums[960 + j * C2 : 960 + (j + 1) * C2] = grad_down[:, j * 128 : (j + 1) * 128].astype(BF)
    sums[1472:1536] = jnp.zeros((64, 128), BF)


def fold_kernel(
    sources,
    grads_far,
    kernel_far,
    placing_far,
    folded_far,
    grad_local,
    to_four_a,
    to_four_b,
    to_four_c,
    to_four_d,
    grad_preact,
    kernel,
    placing,
    conv_back,
    planes,
    stack,
    high,
    rims,
    grad_table,
    grad_table_high,
    folded,
    done,
    sent,
):
    copies = fetch(
        (kernel_far, grads_far, placing_far.at[0:FOLD_ROWS]), (kernel, grad_preact, placing), done
    )
    grad_table[...] = jnp.zeros_like(grad_table)
    grad_table_high[...] = jnp.zeros_like(grad_table_high)
    wait(copies[:1])
    tall = jnp.transpose(kernel[...].astype(F32)).astype(BF)
    for o in range(3):
        conv_back[o * C : (o + 1) * C] = jnp.concatenate(
            [tall[(9 * o + k) * C : (9 * o + k + 1) * C] for k in range(9)], axis=1
        )
    wait(copies[1:])
    cap_hot = placing[CAP_ROWS : CAP_ROWS + 640]
    inner_hot = tiles_of(placing, INNER_ROWS, 128, 0, 2)
    rows = grad_preact[...].reshape(SLOTS * C, 512)
    for i in range(4):
        block = nn(rows[:, i * 128 : (i + 1) * 128], inner_hot)
        planes[:, i * 256 : (i + 1) * 256] = block.astype(BF)

    def brick(s, carry):
        here = pl.ds(pl.multiple_of(s * C, C), C)
        for x in range(8):
            plane = planes[here, x * 128 : (x + 1) * 128]
            for k, shift in enumerate(SHIFTS):
                moved = plane if shift == 0 else pltpu.roll(plane, shift % 128, 1)
                stack[k * C : (k + 1) * C, x * 128 : (x + 1) * 128] = moved
        triple = nn(conv_back[...], stack[...])
        for x in range(10):
            value = None
            for o in range(3):
                if 0 <= x - o < 8:
                    part = triple[o * C : (o + 1) * C, (x - o) * 128 : (x - o + 1) * 128]
                    value = part if value is None else value + part
            high[here, x * 128 : (x + 1) * 128] = value.astype(BF)
            if 1 <= x <= 8:
                folded[here, (x - 1) * 128 : x * 128] = value
        pltpu.make_async_copy(folded.at[here], folded_far.at[here], sent.at[s]).start()
        return carry

    lax.fori_loop(0, SLOTS, brick, 0, unroll=True)
    rims[:, 0:640] = nt(high[:, 0:128], cap_hot)
    rims[:, 640:1152] = nt(high[:, 128:1152], side_tiles(placing, 0, 8))
    rims[:, 1152:1792] = nt(high[:, 1152:1280], cap_hot)
    for s in range(SLOTS):
        for t in range(14):
            block = rims[s * C : (s + 1) * C, t * 128 : (t + 1) * 128]
            grad_table[sources[0, s, PLACES[2 * t]]] += block
            if PLACES[2 * t + 1] is not None:
                grad_table_high[sources[0, s, PLACES[2 * t + 1]]] += block
    turned = pltpu.roll(grad_table_high[...].reshape(TABLE * C, 128), 64, 1)
    grad_table[...] += turned.reshape(TABLE, C, 128)
    grad_local[...] = grad_table[0:LOCAL]
    for s in range(SLOTS):
        rows = pl.ds(s * C, C)
        pltpu.make_async_copy(folded.at[rows], folded_far.at[rows], sent.at[s]).wait()
    left = low_lanes((C, 128))
    for p, j in enumerate(partners(False)):
        for q in range(CAP // 2):
            place = LOCAL + j * CAP + 2 * q
            block = jnp.where(left, grad_table[place], pltpu.roll(grad_table[place + 1], 64, 1))
            (to_four_a, to_four_b, to_four_c, to_four_d)[p][q] = block.astype(BF)


def unpack_kernel(sums, grad_kernel, grad_down):
    parts = []
    for o in range(3):
        tiles = [sums[j * 192 + o * C : j * 192 + (o + 1) * C].astype(F32) for j in range(5)]
        parts.append(jnp.concatenate(tiles, axis=1)[:, :576])
    grad_kernel[...] = jnp.concatenate(parts, axis=1)
    tiles = [sums[960 + t * C2 : 960 + (t + 1) * C2].astype(F32) for t in range(4)]
    grad_down[...] = jnp.concatenate(tiles, axis=1)


def finish_kernel(
    count,
    sends,
    folded,
    grad_local,
    from_a,
    from_b,
    from_c,
    from_d,
    face_hot,
    inner_hot,
    grad_features,
    table,
    layers,
):
    table[...] = grad_local[...]
    for p, j in enumerate(partners(True)):
        for q in range(CAP // 2):
            block = (from_a, from_b, from_c, from_d)[p][q].astype(F32)
            table[sends[0, 0, j, 2 * q]] += block
            table[sends[0, 0, j, 2 * q + 1]] += pltpu.roll(block, 64, 1)
    for s in range(SLOTS):
        for f in range(6):
            layers[s * C : (s + 1) * C, f * 128 : (f + 1) * 128] = table[6 * s + f].astype(BF)
    tiles = []
    for i in range(4):
        value = folded[:, i * 256 : (i + 1) * 256]
        top = value.astype(BF)
        rest = (value - top.astype(F32)).astype(BF)
        tiles.append(nt(top, inner_hot[...]) + nt(rest, inner_hot[...]))
    whole = jnp.concatenate(tiles, axis=1) + nt(layers[...], face_hot[...])
    for s in range(SLOTS):
        filled = jnp.where(s < count[0, 0], 1.0, 0.0).astype(F32)
        grad_features[0, s] = (whole[s * C : (s + 1) * C] * filled).astype(BF)


def call(kernel, limit, memories, outs, scratch, flops, *args, out_memories=None):
    where = {"s": pltpu.SMEM, "v": pltpu.VMEM, "h": pltpu.HBM}
    return pl.pallas_call(
        kernel,
        in_specs=[pl.BlockSpec(memory_space=where[m]) for m in memories],
        out_specs=[pl.BlockSpec(memory_space=where[m]) for m in out_memories or "v" * len(outs)],
        out_shape=[jax.ShapeDtypeStruct(s, d) for s, d in outs],
        scratch_shapes=[pltpu.VMEM(*s) if isinstance(s, tuple) else s for s in scratch],
        compiler_params=pltpu.CompilerParams(vmem_limit_bytes=int(limit * 2**20)),
        cost_estimate=pl.CostEstimate(flops=flops, bytes_accessed=2**20, transcendentals=0),
        name=kernel.__name__,
    )(*args)


def gather_sum(block, axes, parts):
    copies = jnp.broadcast_to(block[None], (parts,) + block.shape)
    got = lax.all_to_all(copies, axes, 0, 0)
    return got.astype(F32).sum(0)


def near_sum(block, sizes):
    parts = sizes["x"] * sizes["c"] * sizes["grp"]
    rows = block.shape[0] // parts
    got = lax.all_to_all(block.reshape(parts, rows, 128), NEAR, 0, 0)
    return got.astype(F32).sum(0).astype(BF)


def near_gather(block, sizes):
    parts = sizes["x"] * sizes["c"] * sizes["grp"]
    copies = jnp.broadcast_to(block[None], (parts,) + block.shape)
    return lax.all_to_all(copies, NEAR, 0, 0).reshape(parts * block.shape[0], 128)


def swap(blocks, axes, devices):
    pairs = [
        [(t, t + 2) for t in range(devices - 2) if t % 4 >= 2],
        [(t, t + 2) for t in range(devices - 2) if t % 4 < 2],
        [(t, t + 1) for t in range(devices - 1) if t % 2 == 1],
        [(t, t + 1) for t in range(devices - 1) if t % 2 == 0],
    ]
    routes = [two + [(b, a) for a, b in two] for two in pairs]
    return [lax.ppermute(block, axes, route) for block, route in zip(blocks, routes)]


def on_device(sizes, features, brick_count, send_list, halo_src, kernel, down_kernel, out_grad):
    face_packed, face_hot, inner_hot, placing = one_hot_tables()
    tile = ("z", "x", "c")
    devices = sizes["z"] * sizes["x"] * sizes["c"]
    blocks = [((CAP // 2, C, 128), BF)] * NOFF

    table, *outgoing = call(
        faces_kernel,
        56,
        "shhh",
        [((LOCAL, C, 128), BF)] + blocks,
        [
            pltpu.SMEM((1, 1, NOFF, CAP), jnp.int32),
            ((1, SLOTS, C, 512), BF),
            ((512, 256), BF),
            pltpu.SemaphoreType.DMA((3,)),
        ],
        2 * 256 * 512 * 768,
        brick_count,
        send_list,
        features,
        face_packed,
    )
    received = swap(outgoing, tile, devices)
    (grad_active,) = call(
        upper_kernel,
        56,
        "hhh",
        [((SLOTS, C, 512), F32)],
        [
            ((1, SLOTS, 64, C2), BF),
            ((C2, 512), BF),
            ((512, 128), BF),
            pltpu.SemaphoreType.DMA((3,)),
        ],
        10**9,
        out_grad,
        down_kernel,
        placing,
    )
    coarse, grad_preact, sums = call(
        main_kernel,
        53.8,
        "s" + "h" * 12,
        [
            ((1, SLOTS, 64, C2), BF),
            ((SLOTS, C, 512), BF),
            ((1536, 128), BF),
        ],
        [
            pltpu.SMEM((1, SLOTS, 26), jnp.int32),
            ((NOFF, CAP // 2, C, 128), BF),
            ((1, SLOTS, C, 512), BF),
            ((ALL_ROWS, 128), BF),
            ((C, 1728), BF),
            ((C2, 512), BF),
            ((1, SLOTS, 64, C2), BF),
            ((SLOTS, C, 512), F32),
            ((TABLE, C, 128), BF),
            ((TABLE, C, 128), BF),
            ((192, 576), BF),
            ((256, 14 * 128), BF),
            ((256, 1280), BF),
            ((2, 576, 1280), BF),
            ((192, 1280), BF),
            ((SLOTS, 64, 512), BF),
            ((192, 576), F32),
            pltpu.SemaphoreType.DMA((12,)),
        ],
        5 * 10**9,
        brick_count,
        halo_src,
        table,
        *received,
        features,
        placing,
        kernel,
        down_kernel,
        out_grad,
        grad_active,
    )
    part = near_sum(sums, sizes)
    folded, grad_local, *remote = call(
        fold_kernel,
        56,
        "shhh",
        [((256, 1024), F32), ((LOCAL, C, 128), F32)] + blocks,
        [
            ((SLOTS, C, 512), BF),
            ((C, 1728), BF),
            ((FOLD_ROWS, 128), BF),
            ((192, 576), BF),
            ((256, 1024), BF),
            ((576, 1024), BF),
            ((256, 1280), BF),
            ((256, 14 * 128), F32),
            ((TABLE, C, 128), F32),
            ((TABLE, C, 128), F32),
            ((256, 1024), F32),
            pltpu.SemaphoreType.DMA((3,)),
            pltpu.SemaphoreType.DMA((SLOTS,)),
        ],
        3 * 10**9,
        halo_src,
        grad_preact,
        kernel,
        placing,
        out_memories="hv" + "v" * NOFF,
    )
    part, *remote = lax.optimization_barrier((part, *remote))
    part = gather_sum(part, ("z",), sizes["z"])
    returned = swap(remote, tile, devices)
    part, *returned = lax.optimization_barrier((part, *returned))
    sums = near_gather(part.astype(BF), sizes)
    (grad_features,) = call(
        finish_kernel,
        12,
        "ss" + "v" * 8,
        [((1, SLOTS, C, 512), BF)],
        [((LOCAL, C, 128), F32), ((256, 768), BF)],
        2 * 256 * 512 * 768,
        brick_count,
        send_list,
        folded,
        grad_local,
        *returned,
        face_hot,
        inner_hot,
    )
    grad_kernel, grad_down = call(
        unpack_kernel, 8, "v", [((C, 1728), F32), ((C2, 512), F32)], [], 10**6, sums
    )
    return coarse, grad_features, grad_kernel, grad_down


def solution(mesh):
    tile, grp = mesh.shape["tile"], mesh.shape["grp"]
    sizes = {"z": tile // 8, "x": 4, "c": 2, "grp": grp}
    fine = Mesh(mesh.devices.reshape(tuple(sizes.values())), tuple(sizes))
    line = ("z", "x", "c")
    in_specs = (
        P("grp", line, None, None),
        P("grp", line),
        P("grp", line, None, None),
        P("grp", line, None),
        P(),
        P(),
        P("grp", line, None, None),
    )
    out_specs = (P("grp", line, None, None), P("grp", line, None, None), P(), P())

    def step(*args):
        return on_device(sizes, *args)

    return jax.shard_map(step, mesh=fine, in_specs=in_specs, out_specs=out_specs, check_vma=False)
```
